32 devices in a mesh: blk: 16 (over z, y, x), chan: 2 (over core).
Axes of the slice: x: 2, y: 2, z: 4, core: 2. Of those that a mesh axis runs over, the one named last changes fastest.
Arguments:
- inputs: bfloat16 [128, 64, 512], P('chan', 'blk'), may hold values from -6 to 6
- w_first: bfloat16 [3, 3, 128, 128], P(None, None, 'chan'), may hold values from -0.1875 to 0.1875
- w_second: bfloat16 [3, 3, 128, 128], P(None, None, 'chan'), may hold values from -0.1875 to 0.1875
- w_third: bfloat16 [3, 3, 256, 128], P(None, None, 'chan'), may hold values from -0.1875 to 0.1875
- cotangent: bfloat16 [256, 32, 256], P('chan', 'blk'), may hold values from -6 to 6
- mirror: int32 [16], P('blk'), may hold values from 0 to 1
Outputs:
- grad_inputs: bfloat16 [128, 64, 512], P('chan', 'blk')
- grad_first: float32 [3, 3, 128, 128], P(None, None, 'chan')
- grad_second: float32 [3, 3, 128, 128], P(None, None, 'chan')
- grad_third: float32 [3, 3, 256, 128], P(None, None, 'chan')
The draws below stay inside these ranges and needn't reach their ends.
Inputs may be any that keep to these rules, and one draw needn't show every extreme that they name: `mirror`: 1 marks a tile whose columns are stored in reverse order, 0 a tile stored in the cycle's order.
All inputs are finite; a program needn't handle non-finite values.
Results may differ from the reference program's by a relative error of at most 0.024.
Values may be sent and summed in bfloat16 or wider, within the bound.
No kernel may reach another device: no remote copies, remote signals or barrier semaphores. Data moves between devices by JAX's collectives and lax.ppermute only.
A program may use at most 64 MiB of HBM per device.

```python
import math
import jax
import jax.numpy as jnp

C = 128
C2 = 256
COLS = 512
TILES = 16
CYCLE = 64


def set_ends(array, stream_key, low, largest):
    shape = array.shape
    place = [jax.random.randint(jax.random.fold_in(stream_key, axis), (), 0, shape[axis]) for axis in range(len(shape))]
    array = array.at[tuple(place)].set(low)
    longest = shape.index(max(shape))
    place[longest] = (place[longest] + 1) % shape[longest]
    return array.at[tuple(place)].set(largest)


def levels(rng, dims, split, smallest, top_value):
    loudness = 1.0
    for axis_at, blocks in split:
        heights = jax.random.uniform(jax.random.fold_in(jax.random.fold_in(rng, 6), axis_at), (blocks,), jnp.float32, smallest / len(split), top_value / len(split))
        loudness = loudness * jnp.repeat(jnp.exp(heights), dims[axis_at] // blocks).reshape((-1,) + (1,) * (len(dims) - 1 - axis_at))
    return loudness


def scatter_about(rng, extent, scale, bound, cuts=(), kind=jnp.bfloat16):
    gain = levels(rng, extent, cuts, -0.22, 0.18) if cuts else 1.0
    values = jax.random.normal(rng, extent, jnp.float32) * scale * gain
    return jnp.minimum(jnp.maximum(values, -bound), bound).astype(kind)


def setup_inputs(seed: int = 0) -> dict:
    streams_of = jax.random.split(jax.random.key(seed), 7)
    inputs = scatter_about(streams_of[0], (C, CYCLE, COLS), 1.0, 6.0, ((0, 2), (1, 16)))
    w_first = scatter_about(streams_of[1], (3, 3, C, C), (9 * C) ** -0.5, 0.1875, ((2, 2),))
    w_second = scatter_about(streams_of[2], (3, 3, C, C), (9 * C) ** -0.5, 0.1875, ((2, 2),))
    w_third = scatter_about(streams_of[3], (3, 3, C2, C), (9 * C) ** -0.5, 0.1875, ((2, 2),))
    cotangent = scatter_about(streams_of[4], (C2, CYCLE // 2, COLS // 2), 1.0, 6.0, ((0, 2), (1, 16)))
    mirror = set_ends(jax.random.randint(streams_of[5], (TILES,), 0, 2), jax.random.fold_in(streams_of[5], 1), 0, 1).astype(jnp.int32)
    return dict(inputs=inputs, w_first=w_first, w_second=w_second, w_third=w_third, cotangent=cotangent, mirror=mirror)


def orient(field, mirror):
    channels, cycle_rows, columns = field.shape
    tiles = mirror.shape[0]
    blocks = field.reshape(channels, tiles, cycle_rows // tiles, columns)
    turned = jnp.where(mirror[None, :, None, None] == 1, blocks[..., ::-1], blocks)
    return turned.reshape(channels, cycle_rows, columns)

def wrap_rows(field):
    return jnp.concatenate([field[:, -1:], field, field[:, :1]], axis=1)

def conv_taps(padded, weight):
    row_count = padded.shape[1] - 2
    col_count = padded.shape[2]
    framed = jnp.pad(padded, ((0, 0), (0, 0), (1, 1)))
    running = jnp.zeros((weight.shape[2], row_count, col_count), jnp.float32)
    for row_tap in range(3):
        for col_tap in range(3):
            running = running + jnp.einsum('oi,irw->orw', weight[row_tap, col_tap].astype(jnp.float32), framed[:, row_tap:row_tap + row_count, col_tap:col_tap + col_count])
    return running

def weight_taps(grad_out, padded):
    row_count = grad_out.shape[1]
    col_count = grad_out.shape[2]
    framed = jnp.pad(padded, ((0, 0), (0, 0), (1, 1)))
    stacked = []
    for row_tap in range(3):
        line = []
        for col_tap in range(3):
            line.append(jnp.einsum('orw,irw->oi', grad_out, framed[:, row_tap:row_tap + row_count, col_tap:col_tap + col_count]))
        stacked.append(jnp.stack(line))
    return jnp.stack(stacked)

def spread_taps(grad_out, weight):
    row_count = grad_out.shape[1]
    col_count = grad_out.shape[2]
    running = jnp.zeros((weight.shape[3], row_count + 2, col_count + 2), jnp.float32)
    for row_tap in range(3):
        for col_tap in range(3):
            term = jnp.einsum('oi,orw->irw', weight[row_tap, col_tap].astype(jnp.float32), grad_out)
            running = running.at[:, row_tap:row_tap + row_count, col_tap:col_tap + col_count].add(term)
    return running[:, :, 1:-1]

def stride_framed(field):
    stacked = jnp.concatenate([field[:, -1:], field], axis=1)
    return jnp.pad(stacked, ((0, 0), (0, 0), (1, 0)))

def reference(inputs, w_first, w_second, w_third, cotangent, mirror):
    cycle_rows = inputs.shape[1]
    col_count = inputs.shape[2]
    oriented = orient(inputs, mirror)
    upstream = orient(cotangent, mirror).astype(jnp.float32)
    first_pad = wrap_rows(oriented).astype(jnp.float32)
    first_pre = conv_taps(first_pad, w_first)
    first_act = jax.nn.gelu(first_pre).astype(jnp.bfloat16)
    second_pad = wrap_rows(first_act).astype(jnp.float32)
    second_pre = conv_taps(second_pad, w_second)
    second_act = jax.nn.gelu(second_pre).astype(jnp.bfloat16)
    out_rows = upstream.shape[1]
    out_cols = upstream.shape[2]
    framed = stride_framed(second_act.astype(jnp.float32))
    stacked = []
    for row_tap in range(3):
        line = []
        for col_tap in range(3):
            line.append(jnp.einsum('orw,irw->oi', upstream, framed[:, row_tap:row_tap + 2 * out_rows:2, col_tap:col_tap + 2 * out_cols:2]))
        stacked.append(jnp.stack(line))
    third_grad = jnp.stack(stacked)
    running = jnp.zeros((w_third.shape[3], cycle_rows + 1, col_count + 1), jnp.float32)
    for row_tap in range(3):
        for col_tap in range(3):
            term = jnp.einsum('oi,orw->irw', w_third[row_tap, col_tap].astype(jnp.float32), upstream)
            running = running.at[:, row_tap:row_tap + 2 * out_rows:2, col_tap:col_tap + 2 * out_cols:2].add(term)
    running = running[:, :, 1:]
    second_back = running[:, 1:].at[:, -1:].add(running[:, :1])
    second_delta = jax.vjp(jax.nn.gelu, second_pre)[1](second_back)[0].astype(jnp.bfloat16)
    second_delta_f = second_delta.astype(jnp.float32)
    second_grad = weight_taps(second_delta_f, second_pad)
    spread = spread_taps(second_delta_f, w_second)
    first_back = spread[:, 1:-1].at[:, -1:].add(spread[:, :1])
    first_back = first_back.at[:, :1].add(spread[:, -1:])
    first_delta = jax.vjp(jax.nn.gelu, first_pre)[1](first_back)[0].astype(jnp.bfloat16)
    first_delta_f = first_delta.astype(jnp.float32)
    first_grad = weight_taps(first_delta_f, first_pad)
    spread = spread_taps(first_delta_f, w_first)
    input_back = spread[:, 1:-1].at[:, -1:].add(spread[:, :1])
    input_back = input_back.at[:, :1].add(spread[:, -1:])
    grad_inputs = orient(input_back.astype(jnp.bfloat16), mirror)
    cell_count = cycle_rows * col_count
    return (grad_inputs, first_grad / math.sqrt(cell_count), second_grad / math.sqrt(cell_count), third_grad / math.sqrt(cell_count // 4))
```

```python
import functools
import math

import jax
import jax.numpy as jnp
from jax import lax
from jax.experimental import pallas as pl
from jax.experimental.pallas import tpu as pltpu
from jax.sharding import PartitionSpec as P

BF = jnp.bfloat16
F32 = jnp.float32
ROOT = math.sqrt(2.0 / math.pi)
CUBIC = 0.044715


def dot(a, b):
    return jnp.dot(a, b, preferred_element_type=F32)


def dot_t(a, b):
    return lax.dot_general(a, b, (((1,), (1,)), ((), ())), preferred_element_type=F32)


def moved_right(v):
    lane = lax.broadcasted_iota(jnp.int32, v.shape, 1)
    return jnp.where(lane == 0, 0.0, pltpu.roll(v, 1, 1))


def moved_left(v):
    lane = lax.broadcasted_iota(jnp.int32, v.shape, 1)
    width = v.shape[1]
    return jnp.where(lane == width - 1, 0.0, pltpu.roll(v, width - 1, 1))


def put_stack(ref, base, row):
    c = row.shape[0] // 2
    even, odd = row[:c], row[c:]
    ref[pl.ds(base, c), :] = moved_right(odd).astype(BF)
    ref[pl.ds(base + c, 2 * c), :] = row.astype(BF)
    ref[pl.ds(base + 3 * c, c), :] = moved_left(even).astype(BF)


def gelu_parts(v):
    square = v * v
    t = jnp.tanh(v * (ROOT + (ROOT * CUBIC) * square))
    half = 0.5 * v
    return half + half * t, 0.5 + 0.5 * t + half * (1.0 - t * t) * (ROOT + (3.0 * ROOT * CUBIC) * square)


def block_kernel(
    core, own, before, after, w1, w2, w3,
    dw, main, rims,
    tx, th1, th2, tu, td2, td1, s2, s1, dz1, dz2, wb1, wb2, wt2, wt1, wt3e, wt3o,
):
    me = core[0]
    c = 128
    h = c // 2
    m = tx.shape[1]
    stack = 4 * c
    rows = own.shape[1] // 3 * 2

    wb1[...] = jnp.zeros_like(wb1)
    wb2[...] = jnp.zeros_like(wb2)
    wt2[...] = jnp.zeros_like(wt2)
    wt1[...] = jnp.zeros_like(wt1)
    wt3e[...] = jnp.zeros_like(wt3e)
    wt3o[...] = jnp.zeros_like(wt3o)
    for a in range(3):
        for b in range(3):
            first = jnp.concatenate([w1[0, a, b], w1[1, a, b]], axis=0)
            second = jnp.concatenate([w2[0, a, b], w2[1, a, b]], axis=0)
            for par in range(2):
                at = pl.ds(a * stack + (b + par) * c, c)
                wb1[pl.ds(par * c, c), at] = first
                wb2[pl.ds(par * c, c), at] = second
            turned = second.T
            first_turned = first.T
            half_turned = jnp.where(me == 0, first_turned[:h], first_turned[h:])
            for par in range(2):
                at = pl.ds((2 - a) * stack + (2 - b + par) * c, c)
                wt2[pl.ds(par * c, c), at] = turned
                wt1[pl.ds(par * h, h), at] = half_turned
            third = jnp.concatenate([w3[0, a, b].T, w3[1, a, b].T], axis=1)
            par = 0 if b == 1 else 1
            side = 1 if b == 0 else 0
            if a == 1:
                wt3e[pl.ds(par * c, c), pl.ds(side * 2 * c, 2 * c)] = third
            else:
                back = 0 if a == 2 else 1
                wt3o[pl.ds(par * c, c), pl.ds((back * 2 + side) * 2 * c, 2 * c)] = third

    def input_row(ref, at):
        lo, hi = ref[0, at], ref[1, at]
        return jnp.concatenate([lo[:, :m], hi[:, :m], lo[:, m:], hi[:, m:]], axis=0).astype(F32)

    def input_stack(at, base):
        put_stack(tx, base * stack, input_row(*at))

    for j in range(3):
        input_stack((before, j), j)
    for j in range(rows):
        input_stack((own, j), 3 + j)
    for j in range(3):
        input_stack((after, j), 3 + rows + j)

    def cotangent_stack(ref, at, base):
        lo, hi = ref[0, at], ref[1, at]
        full = jnp.concatenate([lo[:, :m], lo[:, m:], hi[:, :m], hi[:, m:]], axis=0)
        tu[pl.ds(base * stack, 2 * c), :] = full
        tu[pl.ds(base * stack + 2 * c, 2 * c), :] = moved_left(full.astype(F32)).astype(BF)

    cotangent_stack(before, 3, 0)
    for j in range(rows // 2):
        cotangent_stack(own, rows + j, 1 + j)
    cotangent_stack(after, 3, 1 + rows // 2)

    def first_conv(k, _):
        z = dot(wb1[...], tx[pl.ds(pl.multiple_of(k * stack, stack), 3 * stack), :])
        act, slope = gelu_parts(z)
        put_stack(th1, pl.multiple_of(k * stack, stack), act)
        dz1[pl.ds(pl.multiple_of(k * 2 * c, 2 * c), 2 * c), :] = slope
        return 0

    lax.fori_loop(0, rows + 4, first_conv, 0)

    def second_conv(k, _):
        z = dot(wb2[...], th1[pl.ds(pl.multiple_of(k * stack, stack), 3 * stack), :])
        act, slope = gelu_parts(z)
        at = pl.multiple_of(k * 3 * c, c)
        th2[pl.ds(at, c), :] = moved_right(act[c:]).astype(BF)
        th2[pl.ds(at + c, 2 * c), :] = act.astype(BF)
        dz2[pl.ds(pl.multiple_of(k * 2 * c, 2 * c), 2 * c), :] = slope
        return 0

    lax.fori_loop(0, rows + 2, second_conv, 0)

    for a in range(3):
        total = jnp.zeros((c, 3 * c), F32)
        for r in range(rows // 2):
            mine = tu[pl.ds(pl.multiple_of((r + 1) * stack + me * c, c), c), :]
            total = total + dot_t(mine, th2[pl.ds((2 * r + a) * 3 * c, 3 * c), :])
        for b in range(3):
            dw[pl.ds((a * 3 + b) * c, c), :] = total[:, b * c : (b + 1) * c].astype(BF)

    s2[...] = jnp.zeros_like(s2)
    s1[...] = jnp.zeros_like(s1)
    td1[...] = jnp.zeros_like(td1)

    def second_delta(back, k):
        delta = back * dz2[pl.ds(pl.multiple_of(k * 2 * c, 2 * c), 2 * c), :]
        put_stack(td2, pl.multiple_of(k * stack, stack), delta)

    def third_back(q, _):
        odd = dot(wt3o[...], tu[pl.ds(pl.multiple_of(q * stack, stack), 2 * stack), :])
        second_delta(odd, 2 * q)
        even = dot(wt3e[...], tu[pl.ds(pl.multiple_of((q + 1) * stack, stack), stack), :])
        second_delta(even, 2 * q + 1)
        return 0

    lax.fori_loop(0, rows // 2 + 1, third_back, 0)

    def own_rows(ref, out, first):
        for r in range(rows):
            for par in range(2):
                at = pl.multiple_of((first + r) * stack + (1 + par) * c + me * h, h)
                out[par, pl.ds((rows + 1 - r) * h, h), :] = ref[pl.ds(at, h), :]

    def kernel_grad(deltas, stacks, first, at):
        total = jnp.zeros((3 * h, 3 * c), F32)
        for q in range(rows + 2):
            for par in range(2):
                mine = deltas[par, pl.ds((rows + 1 - q) * h, 3 * h), :]
                total = total + dot_t(mine, stacks[pl.ds((q + first) * stack + par * c, 3 * c), :])
        for a in range(3):
            for b in range(3):
                dw[pl.ds(at + (a * 3 + b) * h, h), :] = total[a * h : (a + 1) * h, b * c : (b + 1) * c].astype(BF)

    own_rows(td2, s2, 1)
    kernel_grad(s2, th1, 1, 9 * c)

    def first_delta(k, _):
        back = dot(wt2[...], td2[pl.ds(pl.multiple_of(k * stack, stack), 3 * stack), :])
        delta = back * dz1[pl.ds(pl.multiple_of((k + 2) * 2 * c, 2 * c), 2 * c), :]
        put_stack(td1, pl.multiple_of((k + 2) * stack, stack), delta)
        return 0

    lax.fori_loop(0, rows, first_delta, 0)
    own_rows(td1, s1, 2)
    kernel_grad(s1, tx, 2, 9 * c + 9 * h)

    for k in range(rows + 2):
        back = dot(wt1[...], td1[pl.ds(k * stack, 3 * stack), :])
        flat = jnp.concatenate([back[:h], back[h:]], axis=1)
        if k == 0:
            rims[0] = flat.astype(BF)
        elif k == rows + 1:
            rims[1] = flat.astype(BF)
        else:
            main[k - 1] = flat


def block(core, own, before, after, w1, w2, w3):
    c = w1.shape[-1]
    h = c // 2
    rows = own.shape[1] // 3 * 2
    m = own.shape[3] // 2
    stack = 4 * c
    vmem = pl.BlockSpec(memory_space=pltpu.VMEM)
    return pl.pallas_call(
        block_kernel,
        out_shape=(
            jax.ShapeDtypeStruct((9 * (c + 2 * h), c), BF),
            jax.ShapeDtypeStruct((rows, h, 2 * m), F32),
            jax.ShapeDtypeStruct((2, h, 2 * m), BF),
        ),
        in_specs=[pl.BlockSpec(memory_space=pltpu.SMEM)] + [vmem] * 6,
        out_specs=(vmem, vmem, vmem),
        scratch_shapes=[
            pltpu.VMEM(((rows + 6) * stack, m), BF),
            pltpu.VMEM(((rows + 4) * stack, m), BF),
            pltpu.VMEM(((rows + 2) * 3 * c, m), BF),
            pltpu.VMEM(((rows // 2 + 2) * stack, m), BF),
            pltpu.VMEM(((rows + 2) * stack, m), BF),
            pltpu.VMEM(((rows + 4) * stack, m), BF),
            pltpu.VMEM((2, (rows + 4) * h, m), BF),
            pltpu.VMEM((2, (rows + 4) * h, m), BF),
            pltpu.VMEM(((rows + 4) * 2 * c, m), F32),
            pltpu.VMEM(((rows + 2) * 2 * c, m), F32),
            pltpu.VMEM((2 * c, 3 * stack), BF),
            pltpu.VMEM((2 * c, 3 * stack), BF),
            pltpu.VMEM((2 * c, 3 * stack), BF),
            pltpu.VMEM((c, 3 * stack), BF),
            pltpu.VMEM((2 * c, stack), BF),
            pltpu.VMEM((2 * c, 2 * stack), BF),
        ],
        compiler_params=pltpu.CompilerParams(vmem_limit_bytes=48 * 1024 * 1024),
        cost_estimate=pl.CostEstimate(flops=7 * 10**9, bytes_accessed=8 * 10**6, transcendentals=10**6),
        name="block",
    )(core, own, before, after, w1, w2, w3)


def shards(inputs, w_first, w_second, w_third, cotangent, mirror):
    h, rows, cols = inputs.shape
    outs = cotangent.shape[0]
    m = cols // 2
    c = 2 * h
    tiles = lax.axis_size("blk")
    up = [(i, (i + 1) % tiles) for i in range(tiles)]
    down = [(j, i) for i, j in up]

    to = lax.broadcasted_iota(jnp.int32, (cols, cols), 1)
    place = 2 * (to % m) + to // m
    place = jnp.where(mirror[0] == 1, cols - 1 - place, place)
    split = (lax.broadcasted_iota(jnp.int32, (cols, cols), 0) == place).astype(BF)
    to = lax.broadcasted_iota(jnp.int32, (m, m), 1)
    place = jnp.where(mirror[0] == 1, m - 1 - to, to)
    turn = (lax.broadcasted_iota(jnp.int32, (m, m), 0) == place).astype(BF)

    x = jnp.einsum("irc,cn->rin", inputs, split, preferred_element_type=F32).astype(BF)
    u = jnp.einsum("orc,cn->ron", cotangent, turn, preferred_element_type=F32).astype(BF)
    u = jnp.concatenate([u[:, : outs // 2], u[:, outs // 2 :]], axis=2)
    before = lax.ppermute(jnp.concatenate([x[rows - 3 :], u[rows // 2 - 1 :]]), "blk", up)
    after = lax.ppermute(jnp.concatenate([x[:3], u[:1]]), "blk", down)
    own = lax.all_gather(jnp.concatenate([x, u]), "chan")
    w1 = lax.all_gather(w_first, "chan")
    w2 = lax.all_gather(w_second, "chan")
    w3 = lax.all_gather(w_third, "chan")
    before = lax.all_gather(before, "chan")
    after = lax.all_gather(after, "chan")
    core = lax.axis_index("chan").astype(jnp.int32).reshape(1)

    dw, main, rims = block(core, own, before, after, w1, w2, w3)

    from_next = lax.ppermute(rims[0], "blk", down).astype(F32)
    from_prev = lax.ppermute(rims[1], "blk", up).astype(F32)
    main = jnp.concatenate([main[:1] + from_prev, main[1:-1], main[-1:] + from_next]).astype(BF)
    grad_inputs = jnp.einsum("rin,cn->irc", main, split, preferred_element_type=F32).astype(BF)

    count = dw.shape[0] // tiles
    parts = lax.all_to_all(dw.reshape(tiles, count, c), "blk", 0, 0)
    mine = jnp.sum(parts.astype(F32), axis=0).astype(BF)
    sums = lax.all_to_all(jnp.broadcast_to(mine, (tiles, count, c)), "blk", 0, 0)
    sums = sums.reshape(tiles * count, c).astype(F32)
    cells = rows * cols * tiles
    third = sums[: 9 * c].reshape(3, 3, c, c) / math.sqrt(cells // 4)
    second = sums[9 * c : 9 * c + 9 * h].reshape(3, 3, h, c) / math.sqrt(cells)
    first = sums[9 * c + 9 * h :].reshape(3, 3, h, c) / math.sqrt(cells)
    return grad_inputs, first, second, third


def solution(mesh):
    placed = (
        P("chan", "blk", None),
        P(None, None, "chan", None),
        P(None, None, "chan", None),
        P(None, None, "chan", None),
        P("chan", "blk", None),
        P("blk"),
    )
    return jax.shard_map(
        shards,
        mesh=mesh,
        in_specs=placed,
        out_specs=(
            P("chan", "blk", None),
            P(None, None, "chan", None),
            P(None, None, "chan", None),
            P(None, None, "chan", None),
        ),
        check_vma=False,
    )
```

```python
import functools
import math

import jax
import jax.numpy as jnp
from jax import lax
from jax.experimental import pallas as pl
from jax.experimental.pallas import tpu as pltpu
from jax.sharding import PartitionSpec as P

BF = jnp.bfloat16
F32 = jnp.float32
ROOT = math.sqrt(2.0 / math.pi)
CUBIC = 0.044715


def dot(a, b):
    return jnp.dot(a, b, preferred_element_type=F32)


def dot_t(a, b):
    return lax.dot_general(a, b, (((1,), (1,)), ((), ())), preferred_element_type=F32)


def moved_right(v):
    lane = lax.broadcasted_iota(jnp.int32, v.shape, 1)
    return jnp.where(lane == 0, 0.0, pltpu.roll(v, 1, 1))


def moved_left(v):
    lane = lax.broadcasted_iota(jnp.int32, v.shape, 1)
    width = v.shape[1]
    return jnp.where(lane == width - 1, 0.0, pltpu.roll(v, width - 1, 1))


def put_stack(ref, base, row):
    c = row.shape[0] // 2
    even, odd = row[:c], row[c:]
    ref[pl.ds(base, c), :] = moved_right(odd).astype(BF)
    ref[pl.ds(base + c, 2 * c), :] = row.astype(BF)
    ref[pl.ds(base + 3 * c, c), :] = moved_left(even).astype(BF)


def gelu_parts(v):
    square = v * v
    t = jnp.tanh(v * (ROOT + (ROOT * CUBIC) * square))
    half = 0.5 * v
    return half + half * t, 0.5 + 0.5 * t + half * (1.0 - t * t) * (ROOT + (3.0 * ROOT * CUBIC) * square)


def weights_kernel(core, packed, wb1, wb2, wt2, wt1, wt3e, wt3o):
    me = core[0]
    c = 128
    h = c // 2
    stack = 4 * c
    for out in (wb1, wb2, wt2, wt1, wt3e, wt3o):
        out[...] = jnp.zeros_like(out)
    for a in range(3):
        for b in range(3):
            tap = a * 3 + b
            first = jnp.concatenate([packed[g, pl.ds(tap * h, h), :] for g in range(2)], axis=0)
            second = jnp.concatenate([packed[g, pl.ds((9 + tap) * h, h), :] for g in range(2)], axis=0)
            for par in range(2):
                at = pl.ds(a * stack + (b + par) * c, c)
                wb1[pl.ds(par * c, c), at] = first
                wb2[pl.ds(par * c, c), at] = second
            turned = second.T
            first_turned = first.T
            half_turned = jnp.where(me == 0, first_turned[:h], first_turned[h:])
            for par in range(2):
                at = pl.ds((2 - a) * stack + (2 - b + par) * c, c)
                wt2[pl.ds(par * c, c), at] = turned
                wt1[pl.ds(par * h, h), at] = half_turned
            third = jnp.concatenate([packed[g, pl.ds(9 * c + tap * c, c), :].T for g in range(2)], axis=1)
            par = 0 if b == 1 else 1
            side = 1 if b == 0 else 0
            if a == 1:
                wt3e[pl.ds(par * c, c), pl.ds(side * 2 * c, 2 * c)] = third
            else:
                back = 0 if a == 2 else 1
                wt3o[pl.ds(par * c, c), pl.ds((back * 2 + side) * 2 * c, 2 * c)] = third


def kernel_grad(dw, at, deltas, stacks, first, rows, h, c):
    stack = 4 * c
    total = jnp.zeros((3 * h, 3 * c), F32)
    for q in range(rows + 2):
        for par in range(2):
            mine = deltas[par, pl.ds((rows + 1 - q) * h, 3 * h), :]
            total = total + dot_t(mine, stacks[pl.ds((q + first) * stack + par * c, 3 * c), :])
    for a in range(3):
        for b in range(3):
            dw[pl.ds(at + (a * 3 + b) * h, h), :] = total[a * h : (a + 1) * h, b * c : (b + 1) * c].astype(BF)


def own_rows(ref, out, first, rows, h, c, me):
    for par in range(2):
        out[par, pl.ds(0, 2 * h), :] = jnp.zeros((2 * h, out.shape[2]), BF)
        out[par, pl.ds((rows + 2) * h, 2 * h), :] = jnp.zeros((2 * h, out.shape[2]), BF)
    for r in range(rows):
        for par in range(2):
            at = pl.multiple_of((first + r) * 4 * c + (1 + par) * c + me * h, h)
            out[par, pl.ds((rows + 1 - r) * h, h), :] = ref[pl.ds(at, h), :]


def second_kernel(
    core, own, before, after, wb1, wb2, wt3e, wt3o,
    dw, tx, td2, dz1,
    th1, th2, tu, s2, dz2,
):
    me = core[0]
    c = wb1.shape[0] // 2
    h = c // 2
    m = tx.shape[1]
    stack = 4 * c
    rows = own.shape[1] // 3 * 2

    def input_stack(ref, at, base):
        lo, hi = ref[0, at], ref[1, at]
        full = jnp.concatenate([lo[:, :m], hi[:, :m], lo[:, m:], hi[:, m:]], axis=0)
        put_stack(tx, base * stack, full.astype(F32))

    for j in range(3):
        input_stack(before, j, j)
    for j in range(rows):
        input_stack(own, j, 3 + j)
    for j in range(3):
        input_stack(after, j, 3 + rows + j)

    def cotangent_stack(ref, at, base):
        lo, hi = ref[0, at], ref[1, at]
        full = jnp.concatenate([lo[:, :m], lo[:, m:], hi[:, :m], hi[:, m:]], axis=0)
        tu[pl.ds(base * stack, 2 * c), :] = full
        tu[pl.ds(base * stack + 2 * c, 2 * c), :] = moved_left(full.astype(F32)).astype(BF)

    cotangent_stack(before, 3, 0)
    for j in range(rows // 2):
        cotangent_stack(own, rows + j, 1 + j)
    cotangent_stack(after, 3, 1 + rows // 2)

    def first_conv(k, _):
        z = dot(wb1[...], tx[pl.ds(pl.multiple_of(k * stack, stack), 3 * stack), :])
        act, slope = gelu_parts(z)
        put_stack(th1, pl.multiple_of(k * stack, stack), act)
        dz1[pl.ds(pl.multiple_of(k * 2 * c, 2 * c), 2 * c), :] = slope
        return 0

    lax.fori_loop(0, rows + 4, first_conv, 0)

    def second_conv(k, _):
        z = dot(wb2[...], th1[pl.ds(pl.multiple_of(k * stack, stack), 3 * stack), :])
        act, slope = gelu_parts(z)
        at = pl.multiple_of(k * 3 * c, c)
        th2[pl.ds(at, c), :] = moved_right(act[c:]).astype(BF)
        th2[pl.ds(at + c, 2 * c), :] = act.astype(BF)
        dz2[pl.ds(pl.multiple_of(k * 2 * c, 2 * c), 2 * c), :] = slope
        return 0

    lax.fori_loop(0, rows + 2, second_conv, 0)

    for a in range(3):
        total = jnp.zeros((c, 3 * c), F32)
        for r in range(rows // 2):
            mine = tu[pl.ds(pl.multiple_of((r + 1) * stack + me * c, c), c), :]
            total = total + dot_t(mine, th2[pl.ds((2 * r + a) * 3 * c, 3 * c), :])
        for b in range(3):
            dw[pl.ds((a * 3 + b) * c, c), :] = total[:, b * c : (b + 1) * c].astype(BF)

    def second_delta(back, k):
        delta = back * dz2[pl.ds(pl.multiple_of(k * 2 * c, 2 * c), 2 * c), :]
        put_stack(td2, pl.multiple_of(k * stack, stack), delta)

    def third_back(q, _):
        odd = dot(wt3o[...], tu[pl.ds(pl.multiple_of(q * stack, stack), 2 * stack), :])
        second_delta(odd, 2 * q)
        even = dot(wt3e[...], tu[pl.ds(pl.multiple_of((q + 1) * stack, stack), stack), :])
        second_delta(even, 2 * q + 1)
        return 0

    lax.fori_loop(0, rows // 2 + 1, third_back, 0)
    own_rows(td2, s2, 1, rows, h, c, me)
    kernel_grad(dw, 9 * c, s2, th1, 1, rows, h, c)
    used = 9 * (c + h)
    if dw.shape[0] > used:
        dw[pl.ds(used, dw.shape[0] - used), :] = jnp.zeros((dw.shape[0] - used, c), BF)


def first_kernel(core, td2, dz1, tx, wt2, dw, td1, s1):
    me = core[0]
    c = wt2.shape[0] // 2
    h = c // 2
    stack = 4 * c
    rows = td1.shape[0] // stack - 4
    for k in (0, 1, rows + 2, rows + 3):
        td1[pl.ds(k * stack, stack), :] = jnp.zeros((stack, td1.shape[1]), BF)

    def first_delta(k, _):
        back = dot(wt2[...], td2[pl.ds(pl.multiple_of(k * stack, stack), 3 * stack), :])
        delta = back * dz1[pl.ds(pl.multiple_of((k + 2) * 2 * c, 2 * c), 2 * c), :]
        put_stack(td1, pl.multiple_of((k + 2) * stack, stack), delta)
        return 0

    lax.fori_loop(0, rows, first_delta, 0)
    own_rows(td1, s1, 2, rows, h, c, me)
    kernel_grad(dw, 0, s1, tx, 2, rows, h, c)
    used = 9 * h
    if dw.shape[0] > used:
        dw[pl.ds(used, dw.shape[0] - used), :] = jnp.zeros((dw.shape[0] - used, c), BF)


def inputs_kernel(td1, wt1, main, rims):
    h = wt1.shape[0] // 2
    stack = 8 * h
    rows = main.shape[0]
    for k in range(rows + 2):
        back = dot(wt1[...], td1[pl.ds(k * stack, 3 * stack), :])
        flat = jnp.concatenate([back[:h], back[h:]], axis=1)
        if k == 0:
            rims[0] = flat.astype(BF)
        elif k == rows + 1:
            rims[1] = flat.astype(BF)
        else:
            main[k - 1] = flat


def call(body, name, flops, outs, scratch, limit, *args):
    vmem = pl.BlockSpec(memory_space=pltpu.VMEM)
    scalar = pl.BlockSpec(memory_space=pltpu.SMEM)
    size = sum(math.prod(a.shape) * a.dtype.itemsize for a in args)
    size += sum(math.prod(shape) * jnp.dtype(kind).itemsize for shape, kind in outs)
    return pl.pallas_call(
        body,
        out_shape=tuple(jax.ShapeDtypeStruct(shape, kind) for shape, kind in outs),
        in_specs=[scalar if a.dtype == jnp.int32 else vmem for a in args],
        out_specs=tuple(vmem for _ in outs),
        scratch_shapes=[pltpu.VMEM(shape, kind) for shape, kind in scratch],
        compiler_params=pltpu.CompilerParams(vmem_limit_bytes=limit * 1024 * 1024),
        cost_estimate=pl.CostEstimate(flops=int(flops), bytes_accessed=size, transcendentals=0),
        name=name,
    )(*args)


def chunk(rows, parts):
    return -(-rows // (8 * parts)) * 8


def scattered(dw, parts):
    pieces = dw.reshape(parts, dw.shape[0] // parts, dw.shape[1])
    pieces = lax.all_to_all(pieces, "blk", 0, 0)
    return jnp.sum(pieces.astype(F32), axis=0).astype(BF)


def shards(inputs, w_first, w_second, w_third, cotangent, mirror):
    h, rows, cols = inputs.shape
    outs = cotangent.shape[0]
    m = cols // 2
    c = 2 * h
    stack = 4 * c
    tiles = lax.axis_size("blk")
    up = [(i, (i + 1) % tiles) for i in range(tiles)]
    down = [(j, i) for i, j in up]
    core = lax.axis_index("chan").astype(jnp.int32).reshape(1)

    to = lax.broadcasted_iota(jnp.int32, (cols, cols), 1)
    place = 2 * (to % m) + to // m
    place = jnp.where(mirror[0] == 1, cols - 1 - place, place)
    split = (lax.broadcasted_iota(jnp.int32, (cols, cols), 0) == place).astype(BF)
    to = lax.broadcasted_iota(jnp.int32, (m, m), 1)
    place = jnp.where(mirror[0] == 1, m - 1 - to, to)
    turn = (lax.broadcasted_iota(jnp.int32, (m, m), 0) == place).astype(BF)

    x = jnp.einsum("irc,cn->rin", inputs, split, preferred_element_type=F32).astype(BF)
    u = jnp.einsum("orc,cn->ron", cotangent, turn, preferred_element_type=F32).astype(BF)
    u = jnp.concatenate([u[:, : outs // 2], u[:, outs // 2 :]], axis=2)
    before = lax.ppermute(jnp.concatenate([x[rows - 3 :], u[rows // 2 - 1 :]]), "blk", up)
    after = lax.ppermute(jnp.concatenate([x[:3], u[:1]]), "blk", down)
    packed = jnp.concatenate([w.reshape(-1, c) for w in (w_first, w_second, w_third)])
    packed = lax.all_gather(packed, "chan")
    own = lax.all_gather(jnp.concatenate([x, u]), "chan")
    wb1, wb2, wt2, wt1, wt3e, wt3o = call(
        weights_kernel, "weights", 1.5e9,
        [((2 * c, 3 * stack), BF)] * 3 + [((c, 3 * stack), BF), ((2 * c, stack), BF), ((2 * c, 2 * stack), BF)],
        [], 16, core, packed,
    )
    before = lax.all_gather(before, "chan")
    after = lax.all_gather(after, "chan")

    late = chunk(9 * (c + h), tiles) * tiles
    last = chunk(9 * h, tiles) * tiles
    dw32, tx, td2, dz1 = call(
        second_kernel, "second", 6e9,
        [((late, c), BF), (((rows + 6) * stack, m), BF), (((rows + 2) * stack, m), BF), (((rows + 4) * 2 * c, m), F32)],
        [
            (((rows + 4) * stack, m), BF),
            (((rows + 2) * 3 * c, m), BF),
            (((rows // 2 + 2) * stack, m), BF),
            ((2, (rows + 4) * h, m), BF),
            (((rows + 2) * 2 * c, m), F32),
        ],
        32, core, own, before, after, wb1, wb2, wt3e, wt3o,
    )
    early = scattered(dw32, tiles)
    dw1, td1 = call(
        first_kernel, "first", 3e9,
        [((last, c), BF), (((rows + 4) * stack, m), BF)],
        [((2, (rows + 4) * h, m), BF)],
        24, core, td2, dz1, tx, wt2,
    )
    final = scattered(dw1, tiles)
    main, rims = call(
        inputs_kernel, "inputs", 2e9,
        [((rows, h, cols), F32), ((2, h, cols), BF)], [], 16, td1, wt1,
    )

    from_next = lax.ppermute(rims[0], "blk", down).astype(F32)
    from_prev = lax.ppermute(rims[1], "blk", up).astype(F32)
    main = jnp.concatenate([main[:1] + from_prev, main[1:-1], main[-1:] + from_next]).astype(BF)
    grad_inputs = jnp.einsum("rin,cn->irc", main, split, preferred_element_type=F32).astype(BF)

    early = lax.all_gather(early, "blk").reshape(-1, c).astype(F32)
    final = lax.all_gather(final, "blk").reshape(-1, c).astype(F32)
    cells = rows * cols * tiles
    third = early[: 9 * c].reshape(3, 3, c, c) / math.sqrt(cells // 4)
    second = early[9 * c : 9 * (c + h)].reshape(3, 3, h, c) / math.sqrt(cells)
    first = final[: 9 * h].reshape(3, 3, h, c) / math.sqrt(cells)
    return grad_inputs, first, second, third


def solution(mesh):
    placed = (
        P("chan", "blk", None),
        P(None, None, "chan", None),
        P(None, None, "chan", None),
        P(None, None, "chan", None),
        P("chan", "blk", None),
        P("blk"),
    )
    return jax.shard_map(
        shards,
        mesh=mesh,
        in_specs=placed,
        out_specs=(
            P("chan", "blk", None),
            P(None, None, "chan", None),
            P(None, None, "chan", None),
            P(None, None, "chan", None),
        ),
        check_vma=False,
    )
```

```python
import functools
import math

import jax
import jax.numpy as jnp
from jax import lax
from jax.experimental import pallas as pl
from jax.experimental.pallas import tpu as pltpu
from jax.sharding import PartitionSpec as P

BF = jnp.bfloat16
F32 = jnp.float32
ROOT = math.sqrt(2.0 / math.pi)
CUBIC = 0.044715


def dot(a, b):
    return jnp.dot(a, b, preferred_element_type=F32)


def dot_t(a, b):
    return lax.dot_general(a, b, (((1,), (1,)), ((), ())), preferred_element_type=F32)


def moved_right(v):
    lane = lax.broadcasted_iota(jnp.int32, v.shape, 1)
    return jnp.where(lane == 0, 0.0, pltpu.roll(v, 1, 1))


def moved_left(v):
    lane = lax.broadcasted_iota(jnp.int32, v.shape, 1)
    width = v.shape[1]
    return jnp.where(lane == width - 1, 0.0, pltpu.roll(v, width - 1, 1))


def put_stack(ref, base, row):
    c = row.shape[0] // 2
    even, odd = row[:c], row[c:]
    ref[pl.ds(base, c), :] = moved_right(odd).astype(BF)
    ref[pl.ds(base + c, 2 * c), :] = row.astype(BF)
    ref[pl.ds(base + 3 * c, c), :] = moved_left(even).astype(BF)


def gelu_parts(v):
    square = v * v
    t = jnp.tanh(v * (ROOT + (ROOT * CUBIC) * square))
    half = 0.5 * v
    return half + half * t, 0.5 + 0.5 * t + half * (1.0 - t * t) * (ROOT + (3.0 * ROOT * CUBIC) * square)


def weights_kernel(core, packed, thirds, wb1, wb2, wt2, wt1, wt3e, wt3o):
    me = core[0]
    c = 128
    h = c // 2
    stack = 4 * c
    for out in (wb1, wb2, wt2, wt1, wt3e, wt3o):
        out[...] = jnp.zeros_like(out)
    for a in range(3):
        for b in range(3):
            tap = a * 3 + b
            first = jnp.concatenate([packed[g, pl.ds(tap * h, h), :] for g in range(2)], axis=0)
            second = jnp.concatenate([packed[g, pl.ds((9 + tap) * h, h), :] for g in range(2)], axis=0)
            for par in range(2):
                at = pl.ds(a * stack + (b + par) * c, c)
                wb1[pl.ds(par * c, c), at] = first
                wb2[pl.ds(par * c, c), at] = second
            turned = second.T
            first_turned = first.T
            half_turned = jnp.where(me == 0, first_turned[:h], first_turned[h:])
            for par in range(2):
                at = pl.ds((2 - a) * stack + (2 - b + par) * c, c)
                wt2[pl.ds(par * c, c), at] = turned
                wt1[pl.ds(par * h, h), at] = half_turned
            third = jnp.concatenate([thirds[g, pl.ds(tap * c, c), :].T for g in range(2)], axis=1)
            par = 0 if b == 1 else 1
            side = 1 if b == 0 else 0
            if a == 1:
                wt3e[pl.ds(par * c, c), pl.ds(side * 2 * c, 2 * c)] = third
            else:
                back = 0 if a == 2 else 1
                wt3o[pl.ds(par * c, c), pl.ds((back * 2 + side) * 2 * c, 2 * c)] = third


def kernel_grad(dw, at, deltas, stacks, first, rows, h, c):
    stack = 4 * c
    total = jnp.zeros((3 * h, 3 * c), F32)
    for q in range(rows + 2):
        for par in range(2):
            mine = deltas[par, pl.ds((rows + 1 - q) * h, 3 * h), :]
            total = total + dot_t(mine, stacks[pl.ds((q + first) * stack + par * c, 3 * c), :])
    for a in range(3):
        for b in range(3):
            dw[pl.ds(at + (a * 3 + b) * h, h), :] = total[a * h : (a + 1) * h, b * c : (b + 1) * c].astype(BF)


def own_rows(ref, out, first, rows, h, c, me):
    for par in range(2):
        out[par, pl.ds(0, 2 * h), :] = jnp.zeros((2 * h, out.shape[2]), BF)
        out[par, pl.ds((rows + 2) * h, 2 * h), :] = jnp.zeros((2 * h, out.shape[2]), BF)
    for r in range(rows):
        for par in range(2):
            at = pl.multiple_of((first + r) * 4 * c + (1 + par) * c + me * h, h)
            out[par, pl.ds((rows + 1 - r) * h, h), :] = ref[pl.ds(at, h), :]


def second_kernel(
    core, own, before, after, wb1, wb2, wt3e, wt3o,
    dw, tx, td2, dz1,
    th1, th2, tu, s2, dz2,
):
    me = core[0]
    c = wb1.shape[0] // 2
    h = c // 2
    m = tx.shape[1]
    stack = 4 * c
    rows = own.shape[1] // 3 * 2

    def input_stack(ref, at, base):
        lo, hi = ref[0, at], ref[1, at]
        full = jnp.concatenate([lo[:, :m], hi[:, :m], lo[:, m:], hi[:, m:]], axis=0)
        put_stack(tx, base * stack, full.astype(F32))

    for j in range(3):
        input_stack(before, j, j)
    for j in range(rows):
        input_stack(own, j, 3 + j)
    for j in range(3):
        input_stack(after, j, 3 + rows + j)

    def cotangent_stack(ref, at, base):
        lo, hi = ref[0, at], ref[1, at]
        full = jnp.concatenate([lo[:, :m], lo[:, m:], hi[:, :m], hi[:, m:]], axis=0)
        tu[pl.ds(base * stack, 2 * c), :] = full
        tu[pl.ds(base * stack + 2 * c, 2 * c), :] = moved_left(full.astype(F32)).astype(BF)

    cotangent_stack(before, 3, 0)
    for j in range(rows // 2):
        cotangent_stack(own, rows + j, 1 + j)
    cotangent_stack(after, 3, 1 + rows // 2)

    def first_conv(k, _):
        z = dot(wb1[...], tx[pl.ds(pl.multiple_of(k * stack, stack), 3 * stack), :])
        act, slope = gelu_parts(z)
        put_stack(th1, pl.multiple_of(k * stack, stack), act)
        dz1[pl.ds(pl.multiple_of(k * 2 * c, 2 * c), 2 * c), :] = slope
        return 0

    lax.fori_loop(0, rows + 4, first_conv, 0)

    def second_conv(k, _):
        z = dot(wb2[...], th1[pl.ds(pl.multiple_of(k * stack, stack), 3 * stack), :])
        act, slope = gelu_parts(z)
        at = pl.multiple_of(k * 3 * c, c)
        th2[pl.ds(at, c), :] = moved_right(act[c:]).astype(BF)
        th2[pl.ds(at + c, 2 * c), :] = act.astype(BF)
        dz2[pl.ds(pl.multiple_of(k * 2 * c, 2 * c), 2 * c), :] = slope
        return 0

    lax.fori_loop(0, rows + 2, second_conv, 0)

    for a in range(3):
        total = jnp.zeros((c, 3 * c), F32)
        for r in range(rows // 2):
            mine = tu[pl.ds(pl.multiple_of((r + 1) * stack + me * c, c), c), :]
            total = total + dot_t(mine, th2[pl.ds((2 * r + a) * 3 * c, 3 * c), :])
        for b in range(3):
            dw[pl.ds((a * 3 + b) * c, c), :] = total[:, b * c : (b + 1) * c].astype(BF)

    def second_delta(back, k):
        delta = back * dz2[pl.ds(pl.multiple_of(k * 2 * c, 2 * c), 2 * c), :]
        put_stack(td2, pl.multiple_of(k * stack, stack), delta)

    def third_back(q, _):
        odd = dot(wt3o[...], tu[pl.ds(pl.multiple_of(q * stack, stack), 2 * stack), :])
        second_delta(odd, 2 * q)
        even = dot(wt3e[...], tu[pl.ds(pl.multiple_of((q + 1) * stack, stack), stack), :])
        second_delta(even, 2 * q + 1)
        return 0

    lax.fori_loop(0, rows // 2 + 1, third_back, 0)
    own_rows(td2, s2, 1, rows, h, c, me)
    kernel_grad(dw, 9 * c, s2, th1, 1, rows, h, c)
    used = 9 * (c + h)
    if dw.shape[0] > used:
        dw[pl.ds(used, dw.shape[0] - used), :] = jnp.zeros((dw.shape[0] - used, c), BF)


def first_kernel(core, td2, dz1, tx, wt2, dw, td1, s1):
    me = core[0]
    c = wt2.shape[0] // 2
    h = c // 2
    stack = 4 * c
    rows = td1.shape[0] // stack - 4
    for k in (0, 1, rows + 2, rows + 3):
        td1[pl.ds(k * stack, stack), :] = jnp.zeros((stack, td1.shape[1]), BF)

    def first_delta(k, _):
        back = dot(wt2[...], td2[pl.ds(pl.multiple_of(k * stack, stack), 3 * stack), :])
        delta = back * dz1[pl.ds(pl.multiple_of((k + 2) * 2 * c, 2 * c), 2 * c), :]
        put_stack(td1, pl.multiple_of((k + 2) * stack, stack), delta)
        return 0

    lax.fori_loop(0, rows, first_delta, 0)
    own_rows(td1, s1, 2, rows, h, c, me)
    kernel_grad(dw, 0, s1, tx, 2, rows, h, c)
    used = 9 * h
    if dw.shape[0] > used:
        dw[pl.ds(used, dw.shape[0] - used), :] = jnp.zeros((dw.shape[0] - used, c), BF)


def inputs_kernel(td1, wt1, main, rims):
    h = wt1.shape[0] // 2
    stack = 8 * h
    rows = main.shape[0]
    for k in range(rows + 2):
        back = dot(wt1[...], td1[pl.ds(k * stack, 3 * stack), :])
        flat = jnp.concatenate([back[:h], back[h:]], axis=1)
        if k == 0:
            rims[0] = flat.astype(BF)
        elif k == rows + 1:
            rims[1] = flat.astype(BF)
        else:
            main[k - 1] = flat


def call(body, name, flops, outs, scratch, limit, *args):
    vmem = pl.BlockSpec(memory_space=pltpu.VMEM)
    scalar = pl.BlockSpec(memory_space=pltpu.SMEM)
    size = sum(math.prod(a.shape) * a.dtype.itemsize for a in args)
    size += sum(math.prod(shape) * jnp.dtype(kind).itemsize for shape, kind in outs)
    return pl.pallas_call(
        body,
        out_shape=tuple(jax.ShapeDtypeStruct(shape, kind) for shape, kind in outs),
        in_specs=[scalar if a.dtype == jnp.int32 else vmem for a in args],
        out_specs=tuple(vmem for _ in outs),
        scratch_shapes=[pltpu.VMEM(shape, kind) for shape, kind in scratch],
        compiler_params=pltpu.CompilerParams(vmem_limit_bytes=limit * 1024 * 1024),
        cost_estimate=pl.CostEstimate(flops=int(flops), bytes_accessed=size, transcendentals=0),
        name=name,
    )(*args)


def chunk(rows, parts):
    return -(-rows // (8 * parts)) * 8


def groups_of(tiles):
    inner = math.gcd(tiles, 4)
    near = [list(range(i, i + inner)) for i in range(0, tiles, inner)]
    far = [list(range(i, tiles, inner)) for i in range(inner)]
    return near, far


def exchanged(pieces, groups):
    return lax.all_to_all(pieces, "blk", 0, 0, axis_index_groups=groups)


def scattered(dw, tiles):
    near, far = groups_of(tiles)
    inner, outer = len(near[0]), len(far[0])
    pieces = dw.reshape(inner, outer * (dw.shape[0] // tiles), dw.shape[1])
    pieces = exchanged(pieces, near)
    pieces = jnp.sum(pieces.astype(F32), axis=0).astype(BF)
    pieces = exchanged(pieces.reshape(outer, -1, dw.shape[1]), far)
    return jnp.sum(pieces.astype(F32), axis=0).astype(BF)


def collected(mine, tiles):
    near, far = groups_of(tiles)
    inner, outer = len(near[0]), len(far[0])
    rows, c = mine.shape
    part = exchanged(jnp.broadcast_to(mine, (outer, rows, c)), far).reshape(outer * rows, c)
    whole = exchanged(jnp.broadcast_to(part, (inner, outer * rows, c)), near)
    return whole.reshape(tiles * rows, c)


def shards(inputs, w_first, w_second, w_third, cotangent, mirror):
    h, rows, cols = inputs.shape
    outs = cotangent.shape[0]
    m = cols // 2
    c = 2 * h
    stack = 4 * c
    tiles = lax.axis_size("blk")
    up = [(i, (i + 1) % tiles) for i in range(tiles)]
    down = [(j, i) for i, j in up]
    core = lax.axis_index("chan").astype(jnp.int32).reshape(1)

    to = lax.broadcasted_iota(jnp.int32, (cols, cols), 1)
    place = 2 * (to % m) + to // m
    place = jnp.where(mirror[0] == 1, cols - 1 - place, place)
    split = (lax.broadcasted_iota(jnp.int32, (cols, cols), 0) == place).astype(BF)
    to = lax.broadcasted_iota(jnp.int32, (m, m), 1)
    place = jnp.where(mirror[0] == 1, m - 1 - to, to)
    turn = (lax.broadcasted_iota(jnp.int32, (m, m), 0) == place).astype(BF)

    x = jnp.einsum("irc,cn->rin", inputs, split, preferred_element_type=F32).astype(BF)
    u = jnp.einsum("orc,cn->ron", cotangent, turn, preferred_element_type=F32).astype(BF)
    u = jnp.concatenate([u[:, : outs // 2], u[:, outs // 2 :]], axis=2)
    before = lax.ppermute(jnp.concatenate([x[rows - 3 :], u[rows // 2 - 1 :]]), "blk", up)
    after = lax.ppermute(jnp.concatenate([x[:3], u[:1]]), "blk", down)
    own = lax.all_gather(jnp.concatenate([x, u]), "chan")
    packed = lax.all_gather(jnp.concatenate([w.reshape(-1, c) for w in (w_first, w_second)]), "chan")
    thirds = lax.all_gather(w_third.reshape(-1, c), "chan")
    wb1, wb2, wt2, wt1, wt3e, wt3o = call(
        weights_kernel, "weights", 1e6,
        [((2 * c, 3 * stack), BF)] * 3 + [((c, 3 * stack), BF), ((2 * c, stack), BF), ((2 * c, 2 * stack), BF)],
        [], 16, core, packed, thirds,
    )
    before = lax.all_gather(before, "chan")
    after = lax.all_gather(after, "chan")

    late = chunk(9 * (c + h), tiles) * tiles
    last = chunk(9 * h, tiles) * tiles
    dw32, tx, td2, dz1 = call(
        second_kernel, "second", 1e6,
        [((late, c), BF), (((rows + 6) * stack, m), BF), (((rows + 2) * stack, m), BF), (((rows + 4) * 2 * c, m), F32)],
        [
            (((rows + 4) * stack, m), BF),
            (((rows + 2) * 3 * c, m), BF),
            (((rows // 2 + 2) * stack, m), BF),
            ((2, (rows + 4) * h, m), BF),
            (((rows + 2) * 2 * c, m), F32),
        ],
        32, core, own, before, after, wb1, wb2, wt3e, wt3o,
    )
    early = scattered(dw32, tiles)
    dw1, td1 = call(
        first_kernel, "first", 1e6,
        [((last, c), BF), (((rows + 4) * stack, m), BF)],
        [((2, (rows + 4) * h, m), BF)],
        24, core, td2, dz1, tx, wt2,
    )
    final = scattered(dw1, tiles)
    main, rims = call(
        inputs_kernel, "inputs", 1e6,
        [((rows, h, cols), F32), ((2, h, cols), BF)], [], 16, td1, wt1,
    )

    from_next = lax.ppermute(rims[0], "blk", down).astype(F32)
    from_prev = lax.ppermute(rims[1], "blk", up).astype(F32)
    main = jnp.concatenate([main[:1] + from_prev, main[1:-1], main[-1:] + from_next]).astype(BF)
    grad_inputs = jnp.einsum("rin,cn->irc", main, split, preferred_element_type=F32).astype(BF)

    early = collected(early, tiles).astype(F32)
    final = collected(final, tiles).astype(F32)
    cells = rows * cols * tiles
    third = early[: 9 * c].reshape(3, 3, c, c) / math.sqrt(cells // 4)
    second = early[9 * c : 9 * (c + h)].reshape(3, 3, h, c) / math.sqrt(cells)
    first = final[: 9 * h].reshape(3, 3, h, c) / math.sqrt(cells)
    return grad_inputs, first, second, third


def solution(mesh):
    placed = (
        P("chan", "blk", None),
        P(None, None, "chan", None),
        P(None, None, "chan", None),
        P(None, None, "chan", None),
        P("chan", "blk", None),
        P("blk"),
    )
    return jax.shard_map(
        shards,
        mesh=mesh,
        in_specs=placed,
        out_specs=(
            P("chan", "blk", None),
            P(None, None, "chan", None),
            P(None, None, "chan", None),
            P(None, None, "chan", None),
        ),
        check_vma=False,
    )
```

```python
import functools
import math

import jax
import jax.numpy as jnp
from jax import lax
from jax.experimental import pallas as pl
from jax.experimental.pallas import tpu as pltpu
from jax.sharding import PartitionSpec as P

BF = jnp.bfloat16
F32 = jnp.float32
ROOT = math.sqrt(2.0 / math.pi)
CUBIC = 0.044715


def dot(a, b):
    return jnp.dot(a, b, preferred_element_type=F32)


def dot_t(a, b):
    return lax.dot_general(a, b, (((1,), (1,)), ((), ())), preferred_element_type=F32)


def moved_right(v):
    lane = lax.broadcasted_iota(jnp.int32, v.shape, 1)
    return jnp.where(lane == 0, 0.0, pltpu.roll(v, 1, 1))


def moved_left(v):
    lane = lax.broadcasted_iota(jnp.int32, v.shape, 1)
    width = v.shape[1]
    return jnp.where(lane == width - 1, 0.0, pltpu.roll(v, width - 1, 1))


def put_stack(ref, base, row):
    c = row.shape[0] // 2
    even, odd = row[:c], row[c:]
    ref[pl.ds(base, c), :] = moved_right(odd).astype(BF)
    ref[pl.ds(base + c, 2 * c), :] = row.astype(BF)
    ref[pl.ds(base + 3 * c, c), :] = moved_left(even).astype(BF)


def gelu_parts(v):
    square = v * v
    t = jnp.tanh(v * (ROOT + (ROOT * CUBIC) * square))
    half = 0.5 * v
    return half + half * t, 0.5 + 0.5 * t + half * (1.0 - t * t) * (ROOT + (3.0 * ROOT * CUBIC) * square)


def weights_kernel(core, packed, thirds, wb1, wb2, wt2, wt1, wt3e, wt3o):
    me = core[0]
    c = 128
    h = c // 2
    stack = 4 * c
    for out in (wb1, wb2, wt2, wt1, wt3e, wt3o):
        out[...] = jnp.zeros_like(out)
    for a in range(3):
        for b in range(3):
            tap = a * 3 + b
            first = jnp.concatenate([packed[g, pl.ds(tap * h, h), :] for g in range(2)], axis=0)
            second = jnp.concatenate([packed[g, pl.ds((9 + tap) * h, h), :] for g in range(2)], axis=0)
            for par in range(2):
                at = pl.ds(a * stack + (b + par) * c, c)
                wb1[pl.ds(par * c, c), at] = first
                wb2[pl.ds(par * c, c), at] = second
            turned = second.T
            first_turned = first.T
            half_turned = jnp.where(me == 0, first_turned[:h], first_turned[h:])
            for par in range(2):
                at = pl.ds((2 - a) * stack + (2 - b + par) * c, c)
                wt2[pl.ds(par * c, c), at] = turned
                wt1[pl.ds(par * h, h), at] = half_turned
            third = jnp.concatenate([thirds[g, pl.ds(tap * c, c), :].T for g in range(2)], axis=1)
            par = 0 if b == 1 else 1
            side = 1 if b == 0 else 0
            if a == 1:
                wt3e[pl.ds(par * c, c), pl.ds(side * 2 * c, 2 * c)] = third
            else:
                back = 0 if a == 2 else 1
                wt3o[pl.ds(par * c, c), pl.ds((back * 2 + side) * 2 * c, 2 * c)] = third


def kernel_grad(dw, at, deltas, stacks, first, rows, h, c):
    stack = 4 * c
    total = jnp.zeros((3 * h, 3 * c), F32)
    for q in range(rows + 2):
        for par in range(2):
            mine = deltas[par, pl.ds((rows + 1 - q) * h, 3 * h), :]
            total = total + dot_t(mine, stacks[pl.ds((q + first) * stack + par * c, 3 * c), :])
    for a in range(3):
        for b in range(3):
            dw[pl.ds(at + (a * 3 + b) * h, h), :] = total[a * h : (a + 1) * h, b * c : (b + 1) * c].astype(BF)


def own_rows(ref, out, first, rows, h, c, me):
    for par in range(2):
        out[par, pl.ds(0, 2 * h), :] = jnp.zeros((2 * h, out.shape[2]), BF)
        out[par, pl.ds((rows + 2) * h, 2 * h), :] = jnp.zeros((2 * h, out.shape[2]), BF)
    for r in range(rows):
        for par in range(2):
            at = pl.multiple_of((first + r) * 4 * c + (1 + par) * c + me * h, h)
            out[par, pl.ds((rows + 1 - r) * h, h), :] = ref[pl.ds(at, h), :]


def levels(tiles):
    found, shift = [], 0
    while (tiles >> shift) > 1:
        bits = min(2, (tiles >> shift).bit_length() - 1)
        found.append((shift, 1 << bits))
        shift += bits
    return found


def piece_at(tile, shift, count, k):
    return lax.bitwise_xor(lax.rem(lax.shift_right_logical(tile, shift), count), k)


def deal(whole, pieces, tile, shift):
    size = pieces[0].shape[0]
    for k, piece in enumerate(pieces):
        at = piece_at(tile, shift, len(pieces), k) * size
        piece[...] = whole[pl.ds(pl.multiple_of(at, 16), size), :]


def sum_kernel(parts, shift, core, *rest):
    count = sum(parts)
    took, pieces, whole = rest[:count], rest[count:-1], rest[-1]
    at = 0
    for some in parts:
        group, took = took[:some], took[some:]
        total = group[0][...].astype(F32)
        for piece in group[1:]:
            total = total + piece[...].astype(F32)
        whole[pl.ds(at, total.shape[0]), :] = total.astype(BF)
        at += total.shape[0]
    if at < whole.shape[0]:
        whole[pl.ds(at, whole.shape[0] - at), :] = jnp.zeros((whole.shape[0] - at, whole.shape[1]), BF)
    if len(pieces) == 1:
        pieces[0][...] = whole[...]
    else:
        deal(whole, pieces, core[1], shift)


def join_kernel(shift, core, *rest):
    pieces, whole = rest[:-1], rest[-1]
    size = pieces[0].shape[0]
    for k, piece in enumerate(pieces):
        at = piece_at(core[1], shift, len(pieces), k) * size
        whole[pl.ds(pl.multiple_of(at, 16), size), :] = piece[...]


def last_kernel(shift, scales, core, *rest):
    pieces, (first, second, third, late, last) = rest[:-5], rest[-5:]
    count = len(pieces)
    for k, piece in enumerate(pieces):
        at = piece_at(core[1], shift, count, k)
        big, small = late.shape[0] // count, last.shape[0] // count
        late[pl.ds(pl.multiple_of(at * big, 16), big), :] = piece[pl.ds(0, big), :]
        last[pl.ds(pl.multiple_of(at * small, 16), small), :] = piece[pl.ds(big, small), :]
    n = third.shape[0]
    third[...] = late[pl.ds(0, n), :].astype(F32) * scales[1]
    second[...] = late[pl.ds(n, second.shape[0]), :].astype(F32) * scales[0]
    first[...] = last[...].astype(F32) * scales[0]


def swapped(pieces, shift, tiles, own):
    got = [own]
    for k, piece in enumerate(pieces, 1):
        got.append(lax.ppermute(piece, "blk", [(i, i ^ (k << shift)) for i in range(tiles)]))
    return got


def second_kernel(
    core, own, before, after, wb1, wb2, wt3e, wt3o,
    *rest,
):
    pieces, (tx, td2, dz1, th1, th2, tu, s2, dz2, dw) = rest[:-9], rest[-9:]
    me = core[0]
    c = wb1.shape[0] // 2
    h = c // 2
    m = tx.shape[1]
    stack = 4 * c
    rows = own.shape[1] // 3 * 2

    def input_stack(ref, at, base):
        lo, hi = ref[0, at], ref[1, at]
        full = jnp.concatenate([lo[:, :m], hi[:, :m], lo[:, m:], hi[:, m:]], axis=0)
        put_stack(tx, base * stack, full.astype(F32))

    for j in range(3):
        input_stack(before, j, j)
    for j in range(rows):
        input_stack(own, j, 3 + j)
    for j in range(3):
        input_stack(after, j, 3 + rows + j)

    def cotangent_stack(ref, at, base):
        lo, hi = ref[0, at], ref[1, at]
        full = jnp.concatenate([lo[:, :m], lo[:, m:], hi[:, :m], hi[:, m:]], axis=0)
        tu[pl.ds(base * stack, 2 * c), :] = full
        tu[pl.ds(base * stack + 2 * c, 2 * c), :] = moved_left(full.astype(F32)).astype(BF)

    cotangent_stack(before, 3, 0)
    for j in range(rows // 2):
        cotangent_stack(own, rows + j, 1 + j)
    cotangent_stack(after, 3, 1 + rows // 2)

    def first_conv(k, _):
        z = dot(wb1[...], tx[pl.ds(pl.multiple_of(k * stack, stack), 3 * stack), :])
        act, slope = gelu_parts(z)
        put_stack(th1, pl.multiple_of(k * stack, stack), act)
        dz1[pl.ds(pl.multiple_of(k * 2 * c, 2 * c), 2 * c), :] = slope
        return 0

    lax.fori_loop(0, rows + 4, first_conv, 0)

    def second_conv(k, _):
        z = dot(wb2[...], th1[pl.ds(pl.multiple_of(k * stack, stack), 3 * stack), :])
        act, slope = gelu_parts(z)
        at = pl.multiple_of(k * 3 * c, c)
        th2[pl.ds(at, c), :] = moved_right(act[c:]).astype(BF)
        th2[pl.ds(at + c, 2 * c), :] = act.astype(BF)
        dz2[pl.ds(pl.multiple_of(k * 2 * c, 2 * c), 2 * c), :] = slope
        return 0

    lax.fori_loop(0, rows + 2, second_conv, 0)

    for a in range(3):
        total = jnp.zeros((c, 3 * c), F32)
        for r in range(rows // 2):
            mine = tu[pl.ds(pl.multiple_of((r + 1) * stack + me * c, c), c), :]
            total = total + dot_t(mine, th2[pl.ds((2 * r + a) * 3 * c, 3 * c), :])
        for b in range(3):
            dw[pl.ds((a * 3 + b) * c, c), :] = total[:, b * c : (b + 1) * c].astype(BF)

    def second_delta(back, k):
        delta = back * dz2[pl.ds(pl.multiple_of(k * 2 * c, 2 * c), 2 * c), :]
        put_stack(td2, pl.multiple_of(k * stack, stack), delta)

    def third_back(q, _):
        odd = dot(wt3o[...], tu[pl.ds(pl.multiple_of(q * stack, stack), 2 * stack), :])
        second_delta(odd, 2 * q)
        even = dot(wt3e[...], tu[pl.ds(pl.multiple_of((q + 1) * stack, stack), stack), :])
        second_delta(even, 2 * q + 1)
        return 0

    lax.fori_loop(0, rows // 2 + 1, third_back, 0)
    own_rows(td2, s2, 1, rows, h, c, me)
    kernel_grad(dw, 9 * c, s2, th1, 1, rows, h, c)
    deal(dw, pieces, core[1], 0)


def first_kernel(core, td2, dz1, tx, wt2, *rest):
    pieces, (td1, s1, dw) = rest[:-3], rest[-3:]
    me = core[0]
    c = wt2.shape[0] // 2
    h = c // 2
    stack = 4 * c
    rows = td1.shape[0] // stack - 4
    for k in (0, 1, rows + 2, rows + 3):
        td1[pl.ds(k * stack, stack), :] = jnp.zeros((stack, td1.shape[1]), BF)

    def first_delta(k, _):
        back = dot(wt2[...], td2[pl.ds(pl.multiple_of(k * stack, stack), 3 * stack), :])
        delta = back * dz1[pl.ds(pl.multiple_of((k + 2) * 2 * c, 2 * c), 2 * c), :]
        put_stack(td1, pl.multiple_of((k + 2) * stack, stack), delta)
        return 0

    lax.fori_loop(0, rows, first_delta, 0)
    own_rows(td1, s1, 2, rows, h, c, me)
    kernel_grad(dw, 0, s1, tx, 2, rows, h, c)
    deal(dw, pieces, core[1], 0)


def inputs_kernel(td1, wt1, main, rims):
    h = wt1.shape[0] // 2
    stack = 8 * h
    rows = main.shape[0]
    for k in range(rows + 2):
        back = dot(wt1[...], td1[pl.ds(k * stack, 3 * stack), :])
        flat = jnp.concatenate([back[:h], back[h:]], axis=1)
        if k == 0:
            rims[0] = flat.astype(BF)
        elif k == rows + 1:
            rims[1] = flat.astype(BF)
        else:
            main[k - 1] = flat


def call(body, name, outs, scratch, limit, *args):
    vmem = pl.BlockSpec(memory_space=pltpu.VMEM)
    scalar = pl.BlockSpec(memory_space=pltpu.SMEM)
    return pl.pallas_call(
        body,
        out_shape=tuple(jax.ShapeDtypeStruct(shape, kind) for shape, kind in outs),
        in_specs=[scalar if a.dtype == jnp.int32 else vmem for a in args],
        out_specs=tuple(vmem for _ in outs),
        scratch_shapes=[pltpu.VMEM(shape, kind) for shape, kind in scratch],
        compiler_params=pltpu.CompilerParams(vmem_limit_bytes=limit * 1024 * 1024),
        cost_estimate=pl.CostEstimate(flops=10**6, bytes_accessed=10**5, transcendentals=0),
        name=name,
    )(*args)


def shards(inputs, w_first, w_second, w_third, cotangent, mirror):
    h, rows, cols = inputs.shape
    outs = cotangent.shape[0]
    m = cols // 2
    c = 2 * h
    stack = 4 * c
    tiles = lax.axis_size("blk")
    up = [(i, (i + 1) % tiles) for i in range(tiles)]
    down = [(j, i) for i, j in up]
    core = jnp.stack([lax.axis_index("chan"), lax.axis_index("blk")]).astype(jnp.int32)

    to = lax.broadcasted_iota(jnp.int32, (cols, cols), 1)
    place = 2 * (to % m) + to // m
    place = jnp.where(mirror[0] == 1, cols - 1 - place, place)
    split = (lax.broadcasted_iota(jnp.int32, (cols, cols), 0) == place).astype(BF)
    to = lax.broadcasted_iota(jnp.int32, (m, m), 1)
    place = jnp.where(mirror[0] == 1, m - 1 - to, to)
    turn = (lax.broadcasted_iota(jnp.int32, (m, m), 0) == place).astype(BF)

    x = jnp.einsum("irc,cn->rin", inputs, split, preferred_element_type=F32).astype(BF)
    u = jnp.einsum("orc,cn->ron", cotangent, turn, preferred_element_type=F32).astype(BF)
    u = jnp.concatenate([u[:, : outs // 2], u[:, outs // 2 :]], axis=2)
    before = lax.ppermute(jnp.concatenate([x[rows - 3 :], u[rows // 2 - 1 :]]), "blk", up)
    after = lax.ppermute(jnp.concatenate([x[:3], u[:1]]), "blk", down)
    own = lax.all_gather(jnp.concatenate([x, u]), "chan")
    packed = lax.all_gather(jnp.concatenate([w.reshape(-1, c) for w in (w_first, w_second)]), "chan")
    thirds = lax.all_gather(w_third.reshape(-1, c), "chan")
    wb1, wb2, wt2, wt1, wt3e, wt3o = call(
        weights_kernel, "weights",
        [((2 * c, 3 * stack), BF)] * 3 + [((c, 3 * stack), BF), ((2 * c, stack), BF), ((2 * c, 2 * stack), BF)],
        [], 16, core, packed, thirds,
    )
    before = lax.all_gather(before, "chan")
    after = lax.all_gather(after, "chan")

    steps = levels(tiles)
    fan = steps[0][1]
    late, last = 9 * (c + h), 9 * h
    *dw32, tx, td2, dz1 = call(
        second_kernel, "second",
        [((late // fan, c), BF)] * fan
        + [(((rows + 6) * stack, m), BF), (((rows + 2) * stack, m), BF), (((rows + 4) * 2 * c, m), F32)],
        [
            (((rows + 4) * stack, m), BF),
            (((rows + 2) * 3 * c, m), BF),
            (((rows // 2 + 2) * stack, m), BF),
            ((2, (rows + 4) * h, m), BF),
            (((rows + 2) * 2 * c, m), F32),
            ((late, c), BF),
        ],
        32, core, own, before, after, wb1, wb2, wt3e, wt3o,
    )
    early = swapped(dw32[1:], 0, tiles, dw32[0])
    *dw1, td1 = call(
        first_kernel, "first",
        [((last // fan, c), BF)] * fan + [(((rows + 4) * stack, m), BF)],
        [((2, (rows + 4) * h, m), BF), ((last, c), BF)],
        24, core, td2, dz1, tx, wt2,
    )
    final = swapped(dw1[1:], 0, tiles, dw1[0])
    main, rims = call(
        inputs_kernel, "inputs",
        [((rows, h, cols), F32), ((2, h, cols), BF)], [], 16, td1, wt1,
    )
    from_next = lax.ppermute(rims[0], "blk", down).astype(F32)
    from_prev = lax.ppermute(rims[1], "blk", up).astype(F32)
    main = jnp.concatenate([main[:1] + from_prev, main[1:-1], main[-1:] + from_next]).astype(BF)
    grad_inputs = jnp.einsum("rin,cn->irc", main, split, preferred_element_type=F32).astype(BF)

    parts, got = (fan, fan), early + final
    size = (late + last) // fan
    block = 16 * (tiles // fan)
    size = -(-size // block) * block
    for shift, count in steps[1:]:
        pieces = call(
            functools.partial(sum_kernel, parts, shift), "sum",
            [((size // count, c), BF)] * count, [((size, c), BF)], 8, core, *got,
        )
        got = swapped(pieces[1:], shift, tiles, pieces[0])
        parts, size = (count,), size // count
    (mine,) = call(
        functools.partial(sum_kernel, parts, 0), "sum",
        [((size, c), BF)], [((size, c), BF)], 8, core, *got,
    )
    for shift, count in steps[:0:-1]:
        got = swapped([mine] * (count - 1), shift, tiles, mine)
        size = size * count
        (mine,) = call(functools.partial(join_kernel, shift), "join", [((size, c), BF)], [], 8, core, *got)
    got = swapped([mine] * (fan - 1), 0, tiles, mine)
    cells = rows * cols * tiles
    scales = (1.0 / math.sqrt(cells), 1.0 / math.sqrt(cells // 4))
    first, second, third = call(
        functools.partial(last_kernel, 0, scales), "last",
        [((9 * h, c), F32), ((9 * h, c), F32), ((9 * c, c), F32)],
        [((late, c), BF), ((last, c), BF)], 16, core, *got,
    )
    return grad_inputs, first.reshape(3, 3, h, c), second.reshape(3, 3, h, c), third.reshape(3, 3, c, c)


def solution(mesh):
    placed = (
        P("chan", "blk", None),
        P(None, None, "chan", None),
        P(None, None, "chan", None),
        P(None, None, "chan", None),
        P("chan", "blk", None),
        P("blk"),
    )
    return jax.shard_map(
        shards,
        mesh=mesh,
        in_specs=placed,
        out_specs=(
            P("chan", "blk", None),
            P(None, None, "chan", None),
            P(None, None, "chan", None),
            P(None, None, "chan", None),
        ),
        check_vma=False,
    )
```

```python
import functools
import math

import jax
import jax.numpy as jnp
from jax import lax
from jax.experimental import pallas as pl
from jax.experimental.pallas import tpu as pltpu
from jax.sharding import PartitionSpec as P

BF = jnp.bfloat16
F32 = jnp.float32
ROOT = math.sqrt(2.0 / math.pi)
CUBIC = 0.044715


def dot(a, b):
    return jnp.dot(a, b, preferred_element_type=F32)


def dot_t(a, b):
    return lax.dot_general(a, b, (((1,), (1,)), ((), ())), preferred_element_type=F32)


def moved_right(v):
    lane = lax.broadcasted_iota(jnp.int32, v.shape, 1)
    return jnp.where(lane == 0, 0.0, pltpu.roll(v, 1, 1))


def moved_left(v):
    lane = lax.broadcasted_iota(jnp.int32, v.shape, 1)
    width = v.shape[1]
    return jnp.where(lane == width - 1, 0.0, pltpu.roll(v, width - 1, 1))


def gelu_parts(v):
    square = v * v
    t = jnp.tanh(v * (ROOT + (ROOT * CUBIC) * square))
    half = 0.5 * v
    return half + half * t, 0.5 + 0.5 * t + half * (1.0 - t * t) * (ROOT + (3.0 * ROOT * CUBIC) * square)


def either(me, own, other):
    return jnp.where(me == 0, own, other), jnp.where(me == 0, other, own)


def weights_kernel(core, own, other, own3, other3, wb1, wb2, wt2, wt1, wt3e, wt3o):
    me = core[0]
    c = own.shape[1]
    h = c // 2
    stack = 4 * c
    for out in (wb1, wb2, wt2, wt1, wt3e, wt3o):
        out[...] = jnp.zeros_like(out)
    for a in range(3):
        for b in range(3):
            tap = a * 3 + b
            at = pl.ds(tap * h, h)
            first = jnp.concatenate(either(me, own[at, :], other[at, :]), axis=0)
            at = pl.ds((9 + tap) * h, h)
            second = jnp.concatenate(either(me, own[at, :], other[at, :]), axis=0)
            for par in range(2):
                at = pl.ds(a * stack + (b + par) * c, c)
                wb1[pl.ds(par * c, c), at] = first
                wb2[pl.ds(par * c, c), at] = second
            turned = second.T
            first_turned = first.T
            half_turned = jnp.where(me == 0, first_turned[:h], first_turned[h:])
            for par in range(2):
                at = pl.ds((2 - a) * stack + (2 - b + par) * c, c)
                wt2[pl.ds(par * c, c), at] = turned
                wt1[pl.ds(par * h, h), at] = half_turned
            at = pl.ds(tap * c, c)
            third = jnp.concatenate([w.T for w in either(me, own3[at, :], other3[at, :])], axis=1)
            par = 0 if b == 1 else 1
            side = 1 if b == 0 else 0
            if a == 1:
                wt3e[pl.ds(par * c, c), pl.ds(side * 2 * c, 2 * c)] = third
            else:
                back = 0 if a == 2 else 1
                wt3o[pl.ds(par * c, c), pl.ds((back * 2 + side) * 2 * c, 2 * c)] = third


def put_stack(ref, base, row):
    c = row.shape[0] // 2
    even, odd = row[:c], row[c:]
    ref[pl.ds(base, c), :] = moved_right(odd).astype(BF)
    ref[pl.ds(base + c, 2 * c), :] = row.astype(BF)
    ref[pl.ds(base + 3 * c, c), :] = moved_left(even).astype(BF)


def main_kernel(
    core, own, other, own_before, before, own_after, after, wb1, wb2, wt2, wt3e, wt3o,
    *rest,
):
    pieces, (td1, tx, th1, th2, tu, td2, s2, s1, dz1, dz2, dw1, dw2, dw3) = rest[:-13], rest[-13:]
    me = core[0]
    c = wb1.shape[0] // 2
    h = c // 2
    m = tx.shape[1]
    stack = 4 * c
    rows = own.shape[0] // 3 * 2
    halves = ((me, own_before, own, own_after), (1 - me, before, other, after))

    def source(j, part):
        _, left, here, right = part
        if j < 3:
            return left[j]
        return here[j - 3] if j < 3 + rows else right[j - 3 - rows]

    def input_stack(j):
        for part in halves:
            row = source(j, part)
            even, odd = row[:, :m], row[:, m:]
            blocks = (moved_right(odd.astype(F32)).astype(BF), even, odd, moved_left(even.astype(F32)).astype(BF))
            for k, block in enumerate(blocks):
                tx[pl.ds(pl.multiple_of(j * stack + k * c + part[0] * h, h), h), :] = block

    def cotangent_stack(j):
        for part in halves:
            at, left, here, right = part
            if j == 0:
                row = left[3]
            else:
                row = here[rows + j - 1] if j < 1 + rows // 2 else right[3]
            for k in range(2):
                block = row[:, k * m : (k + 1) * m]
                base = j * stack + at * c + k * h
                tu[pl.ds(pl.multiple_of(base, h), h), :] = block
                tu[pl.ds(pl.multiple_of(base + 2 * c, h), h), :] = moved_left(block.astype(F32)).astype(BF)

    def own_channels(ref, index, out, r):
        for par in range(2):
            at = pl.multiple_of(index * stack + (1 + par) * c + me * h, h)
            out[par, pl.ds((rows + 1 - r) * h, h), :] = ref[pl.ds(at, h), :]

    def first_dot(k):
        return dot(wb1[...], tx[pl.ds(k * stack, 3 * stack), :])

    def first_use(k, z):
        act, slope = gelu_parts(z)
        put_stack(th1, k * stack, act)
        if 2 <= k < rows + 2:
            dz1[pl.ds((k - 2) * 2 * c, 2 * c), :] = slope
        if k + 4 < rows + 6:
            input_stack(k + 4)

    def second_dot(k):
        return dot(wb2[...], th1[pl.ds(k * stack, 3 * stack), :])

    def second_use(k, z):
        act, slope = gelu_parts(z)
        dz2[pl.ds(k * 2 * c, 2 * c), :] = slope
        if k <= rows:
            th2[pl.ds(k * 3 * c, c), :] = moved_right(act[c:]).astype(BF)
            th2[pl.ds(k * 3 * c + c, 2 * c), :] = act.astype(BF)

    def third_dot(k):
        q = k // 2
        if k % 2 == 0:
            return dot(wt3o[...], tu[pl.ds(q * stack, 2 * stack), :])
        return dot(wt3e[...], tu[pl.ds((q + 1) * stack, stack), :])

    def third_use(k, back):
        put_stack(td2, k * stack, back * dz2[pl.ds(k * 2 * c, 2 * c), :])
        if 1 <= k <= rows:
            own_channels(td2, k, s2, k - 1)

    def back_dot(k):
        return dot(wt2[...], td2[pl.ds(k * stack, 3 * stack), :])

    def back_use(k, back):
        put_stack(td1, (k + 2) * stack, back * dz1[pl.ds(k * 2 * c, 2 * c), :])
        own_channels(td1, k + 2, s1, k)

    def third_grad(a):
        total = jnp.zeros((c, 3 * c), F32)
        for r in range(rows // 2):
            mine = tu[pl.ds(pl.multiple_of((r + 1) * stack + me * c, c), c), :]
            total = total + dot_t(mine, th2[pl.ds((2 * r + a) * 3 * c, 3 * c), :])
        return total

    def third_grad_use(a, total):
        for b in range(3):
            dw3[pl.ds((a * 3 + b) * c, c), :] = total[:, b * c : (b + 1) * c].astype(BF)

    def kernel_grad(deltas, stacks, first):
        total = jnp.zeros((3 * h, 3 * c), F32)
        for q in range(rows + 2):
            for par in range(2):
                mine = deltas[par, pl.ds((rows + 1 - q) * h, 3 * h), :]
                total = total + dot_t(mine, stacks[pl.ds((q + first) * stack + par * c, 3 * c), :])
        return total

    def kernel_grad_use(out, total):
        for a in range(3):
            for b in range(3):
                out[pl.ds((a * 3 + b) * h, h), :] = total[a * h : (a + 1) * h, b * c : (b + 1) * c].astype(BF)

    z1 = [(functools.partial(first_dot, k), functools.partial(first_use, k)) for k in range(rows + 4)]
    z2 = [(functools.partial(second_dot, k), functools.partial(second_use, k)) for k in range(rows + 2)]
    g2 = [(functools.partial(third_dot, k), functools.partial(third_use, k)) for k in range(rows + 2)]
    g1 = [(functools.partial(back_dot, k), functools.partial(back_use, k)) for k in range(rows)]
    w3 = [(functools.partial(third_grad, a), functools.partial(third_grad_use, a)) for a in range(3)]
    w2 = (lambda: kernel_grad(s2, th1, 1), functools.partial(kernel_grad_use, dw2))
    w1 = (lambda: kernel_grad(s1, tx, 2), functools.partial(kernel_grad_use, dw1))
    tasks = z1[:4]
    for k in range(rows):
        tasks += [z2[k], z1[k + 4]]
    tasks += [z2[rows], g2[0], z2[rows + 1], g2[1]]
    for k in range(2, rows + 2):
        tasks += [g2[k]] + ([w3[k - 2]] if k < 5 else []) + ([g1[k - 3]] if k > 2 else [])
    tasks += [w2, g1[rows - 1], w1]

    for j in range(4):
        input_stack(j)
    for j in range(rows // 2 + 2):
        cotangent_stack(j)
    for out in (s2, s1):
        for par in range(2):
            out[par, pl.ds(0, 2 * h), :] = jnp.zeros((2 * h, m), BF)
            out[par, pl.ds((rows + 2) * h, 2 * h), :] = jnp.zeros((2 * h, m), BF)
    for k in (0, 1, rows + 2, rows + 3):
        td1[pl.ds(k * stack, stack), :] = jnp.zeros((stack, m), BF)

    waiting = None
    for task in tasks:
        if task is w1:
            waiting[0](waiting[1])
            waiting = None
        value = task[0]()
        if waiting:
            waiting[0](waiting[1])
        waiting = (task[1], value)
    waiting[0](waiting[1])

    for k, piece in enumerate(pieces):
        at = piece_at(core[1], 0, len(pieces), k)
        base = 0
        for grad in (dw3, dw2, dw1):
            size = grad.shape[0] // len(pieces)
            piece[pl.ds(base, size), :] = grad[pl.ds(pl.multiple_of(at * size, 16), size), :]
            base += size


def inputs_kernel(td1, wt1, main, rims):
    h = wt1.shape[0] // 2
    stack = 8 * h
    rows = main.shape[0]
    for k in range(rows + 2):
        back = dot(wt1[...], td1[pl.ds(k * stack, 3 * stack), :])
        flat = jnp.concatenate([back[:h], back[h:]], axis=1)
        if k == 0:
            rims[0] = flat.astype(BF)
        elif k == rows + 1:
            rims[1] = flat.astype(BF)
        else:
            main[k - 1] = flat


def piece_at(tile, shift, count, k):
    return lax.bitwise_xor(lax.rem(lax.shift_right_logical(tile, shift), count), k)


def sum_kernel(*refs):
    total = refs[0][...].astype(F32)
    for piece in refs[1:-1]:
        total = total + piece[...].astype(F32)
    refs[-1][...] = total.astype(BF)


def last_kernel(scales, core, *rest):
    pieces, outs = rest[:-3], rest[-3:]
    for k, piece in enumerate(pieces):
        at = piece_at(core[1], 0, len(pieces), k)
        base = 0
        for out, scale in zip(outs, scales):
            size = out.shape[0] // len(pieces)
            out[pl.ds(pl.multiple_of(at * size, 16), size), :] = piece[pl.ds(base, size), :].astype(F32) * scale
            base += size


def call(body, name, outs, scratch, limit, *args):
    vmem = pl.BlockSpec(memory_space=pltpu.VMEM)
    scalar = pl.BlockSpec(memory_space=pltpu.SMEM)
    return pl.pallas_call(
        body,
        out_shape=tuple(jax.ShapeDtypeStruct(shape, kind) for shape, kind in outs),
        in_specs=[scalar if a.dtype == jnp.int32 else vmem for a in args],
        out_specs=tuple(vmem for _ in outs),
        scratch_shapes=[pltpu.VMEM(shape, kind) for shape, kind in scratch],
        compiler_params=pltpu.CompilerParams(vmem_limit_bytes=limit * 1024 * 1024),
        cost_estimate=pl.CostEstimate(flops=10**6, bytes_accessed=10**5, transcendentals=0),
        name=name,
    )(*args)


def shards(inputs, w_first, w_second, w_third, cotangent, mirror):
    h, rows, cols = inputs.shape
    outs = cotangent.shape[0]
    m = cols // 2
    c = 2 * h
    stack = 4 * c
    tiles = lax.axis_size("blk")
    up = [(i, (i + 1) % tiles) for i in range(tiles)]
    down = [(j, i) for i, j in up]
    core = jnp.stack([lax.axis_index("chan"), lax.axis_index("blk")]).astype(jnp.int32)

    def across(piece):
        return lax.ppermute(piece, "chan", [(0, 1), (1, 0)])

    def swapped(piece, k):
        return lax.ppermute(piece, "blk", [(i, i ^ k) for i in range(tiles)])

    to = lax.broadcasted_iota(jnp.int32, (cols, cols), 1)
    place = 2 * (to % m) + to // m
    place = jnp.where(mirror[0] == 1, cols - 1 - place, place)
    split = (lax.broadcasted_iota(jnp.int32, (cols, cols), 0) == place).astype(BF)
    to = lax.broadcasted_iota(jnp.int32, (m, m), 1)
    place = jnp.where(mirror[0] == 1, m - 1 - to, to)
    turn = (lax.broadcasted_iota(jnp.int32, (m, m), 0) == place).astype(BF)

    x = jnp.einsum("irc,cn->rin", inputs, split, preferred_element_type=F32).astype(BF)
    u = jnp.einsum("orc,cn->ron", cotangent, turn, preferred_element_type=F32).astype(BF)
    u = jnp.concatenate([u[:, : outs // 2], u[:, outs // 2 :]], axis=2)
    before = lax.ppermute(jnp.concatenate([x[rows - 3 :], u[rows // 2 - 1 :]]), "blk", up)
    after = lax.ppermute(jnp.concatenate([x[:3], u[:1]]), "blk", down)
    own = jnp.concatenate([x, u])
    w12 = jnp.concatenate([w.reshape(-1, c) for w in (w_first, w_second)])
    w3 = w_third.reshape(-1, c)
    wb1, wb2, wt2, wt1, wt3e, wt3o = call(
        weights_kernel, "weights",
        [((2 * c, 3 * stack), BF)] * 3 + [((c, 3 * stack), BF), ((2 * c, stack), BF), ((2 * c, 2 * stack), BF)],
        [], 16, core, w12, across(w12), w3, across(w3),
    )

    fan = math.gcd(tiles, 4)
    size = 9 * (c + 2 * h) // fan
    *parts, td1 = call(
        main_kernel, "main",
        [((size, c), BF)] * fan + [(((rows + 4) * stack, m), BF)],
        [
            (((rows + 6) * stack, m), BF),
            (((rows + 4) * stack, m), BF),
            (((rows + 1) * 3 * c, m), BF),
            (((rows // 2 + 2) * stack, m), BF),
            (((rows + 2) * stack, m), BF),
            ((2, (rows + 4) * h, m), BF),
            ((2, (rows + 4) * h, m), BF),
            ((rows * 2 * c, m), F32),
            (((rows + 2) * 2 * c, m), F32),
            ((9 * h, c), BF),
            ((9 * h, c), BF),
            ((9 * c, c), BF),
        ],
        40, core, own, across(own), before, across(before), after, across(after), wb1, wb2, wt2, wt3e, wt3o,
    )
    parts = parts[:1] + [swapped(piece, k) for k, piece in enumerate(parts[1:], 1)]
    main, rims = call(
        inputs_kernel, "inputs",
        [((rows, h, cols), F32), ((2, h, cols), BF)], [], 16, td1, wt1,
    )
    bit = fan
    while bit < 2 * tiles:
        (mine,) = call(sum_kernel, "sum", [((size, c), BF)], [], 8, *parts)
        if bit == 2 * fan or bit >= tiles and tiles <= fan:
            mine, rims = lax.optimization_barrier((mine, rims))
        if bit < tiles:
            parts = [mine, swapped(mine, bit)]
        bit *= 2
    from_next = lax.ppermute(rims[0], "blk", down).astype(F32)
    from_prev = lax.ppermute(rims[1], "blk", up).astype(F32)
    main = jnp.concatenate([main[:1] + from_prev, main[1:-1], main[-1:] + from_next]).astype(BF)
    grad_inputs = jnp.einsum("rin,cn->irc", main, split, preferred_element_type=F32).astype(BF)

    parts = [mine] + [swapped(mine, k) for k in range(1, fan)]
    cells = rows * cols * tiles
    wide, narrow = 1.0 / math.sqrt(cells // 4), 1.0 / math.sqrt(cells)
    third, second, first = call(
        functools.partial(last_kernel, (wide, narrow, narrow)), "last",
        [((9 * c, c), F32), ((9 * h, c), F32), ((9 * h, c), F32)], [], 16, core, *parts,
    )
    return grad_inputs, first.reshape(3, 3, h, c), second.reshape(3, 3, h, c), third.reshape(3, 3, c, c)


def solution(mesh):
    placed = (
        P("chan", "blk", None),
        P(None, None, "chan", None),
        P(None, None, "chan", None),
        P(None, None, "chan", None),
        P("chan", "blk", None),
        P("blk"),
    )
    return jax.shard_map(
        shards,
        mesh=mesh,
        in_specs=placed,
        out_specs=(
            P("chan", "blk", None),
            P(None, None, "chan", None),
            P(None, None, "chan", None),
            P(None, None, "chan", None),
        ),
        check_vma=False,
    )
```

```python
import functools
import math

import jax
import jax.numpy as jnp
from jax import lax
from jax.experimental import pallas as pl
from jax.experimental.pallas import tpu as pltpu
from jax.sharding import PartitionSpec as P

BF = jnp.bfloat16
F32 = jnp.float32
ROOT = math.sqrt(2.0 / math.pi)
CUBIC = 0.044715


def dot(a, b):
    return jnp.dot(a, b, preferred_element_type=F32)


def dot_t(a, b):
    return lax.dot_general(a, b, (((1,), (1,)), ((), ())), preferred_element_type=F32)


def moved_right(v):
    lane = lax.broadcasted_iota(jnp.int32, v.shape, 1)
    return jnp.where(lane == 0, 0.0, pltpu.roll(v, 1, 1))


def moved_left(v):
    lane = lax.broadcasted_iota(jnp.int32, v.shape, 1)
    width = v.shape[1]
    return jnp.where(lane == width - 1, 0.0, pltpu.roll(v, width - 1, 1))


def gelu_parts(v):
    square = v * v
    t = jnp.tanh(v * (ROOT + (ROOT * CUBIC) * square))
    half = 0.5 * v
    return half + half * t, 0.5 + 0.5 * t + half * (1.0 - t * t) * (ROOT + (3.0 * ROOT * CUBIC) * square)


def orient_kernel(mirror, inputs, cotangent, own, last, lead):
    h, rows, cols = inputs.shape
    m = cols // 2
    turned = mirror[0] == 1
    to = lax.broadcasted_iota(jnp.int32, (cols, cols), 1)
    at = lax.broadcasted_iota(jnp.int32, (cols, cols), 0)
    place = jnp.where(to < m, 2 * to, 2 * (to - m) + 1)
    split = (at == jnp.where(turned, cols - 1 - place, place)).astype(F32).astype(BF)
    to = lax.broadcasted_iota(jnp.int32, (m, m), 1)
    at = lax.broadcasted_iota(jnp.int32, (m, m), 0)
    turn = (at == jnp.where(turned, m - 1 - to, to)).astype(F32).astype(BF)
    for r in range(rows):
        row = dot(inputs[:, r, :], split).astype(BF)
        own[r] = row
        if r >= rows - 3:
            last[r - (rows - 3)] = row
        if r < 3:
            lead[r] = row
    for r in range(rows // 2):
        row = dot(cotangent[:, r, :], turn).astype(BF)
        for k in range(2):
            part = row[k * h : (k + 1) * h]
            at = pl.ds(k * m, m)
            own[rows + r, :, at] = part
            if r == rows // 2 - 1:
                last[3, :, at] = part
            if r == 0:
                lead[3, :, at] = part


def either(me, own, other):
    return jnp.where(me == 0, own, other), jnp.where(me == 0, other, own)


def weights_kernel(core, own, other, own3, other3, wb1, wb2, wt2, wt1, wt3e, wt3o):
    me = core[0]
    c = own.shape[1]
    h = c // 2
    stack = 4 * c
    for out in (wb1, wb2, wt2, wt1, wt3e, wt3o):
        out[...] = jnp.zeros_like(out)
    for a in range(3):
        for b in range(3):
            tap = a * 3 + b
            at = pl.ds(tap * h, h)
            first = jnp.concatenate(either(me, own[at, :], other[at, :]), axis=0)
            at = pl.ds((9 + tap) * h, h)
            second = jnp.concatenate(either(me, own[at, :], other[at, :]), axis=0)
            for par in range(2):
                at = pl.ds(a * stack + (b + par) * c, c)
                wb1[pl.ds(par * c, c), at] = first
                wb2[pl.ds(par * c, c), at] = second
            turned = second.T
            first_turned = first.T
            half_turned = jnp.where(me == 0, first_turned[:h], first_turned[h:])
            for par in range(2):
                at = pl.ds((2 - a) * stack + (2 - b + par) * c, c)
                wt2[pl.ds(par * c, c), at] = turned
                wt1[pl.ds(par * h, h), at] = half_turned
            at = pl.ds(tap * c, c)
            third = jnp.concatenate([w.T for w in either(me, own3[at, :], other3[at, :])], axis=1)
            par = 0 if b == 1 else 1
            side = 1 if b == 0 else 0
            if a == 1:
                wt3e[pl.ds(par * c, c), pl.ds(side * 2 * c, 2 * c)] = third
            else:
                back = 0 if a == 2 else 1
                wt3o[pl.ds(par * c, c), pl.ds((back * 2 + side) * 2 * c, 2 * c)] = third


def put_stack(ref, base, row):
    c = row.shape[0] // 2
    even, odd = row[:c], row[c:]
    ref[pl.ds(base, c), :] = moved_right(odd).astype(BF)
    ref[pl.ds(base + c, 2 * c), :] = row.astype(BF)
    ref[pl.ds(base + 3 * c, c), :] = moved_left(even).astype(BF)


def main_kernel(
    core, own, other, own_before, before, own_after, after, wb1, wb2, wt2, wt3e, wt3o,
    *rest,
):
    pieces, (td1, tx, th1, th2, tu, td2, s2, s1, dz1, dz2, dw1, dw2, dw3) = rest[:-13], rest[-13:]
    me = core[0]
    c = wb1.shape[0] // 2
    h = c // 2
    m = tx.shape[1]
    stack = 4 * c
    rows = own.shape[0] // 3 * 2
    halves = ((me, own_before, own, own_after), (1 - me, before, other, after))

    def source(j, part):
        _, left, here, right = part
        if j < 3:
            return left[j]
        return here[j - 3] if j < 3 + rows else right[j - 3 - rows]

    def input_stack(j):
        for part in halves:
            row = source(j, part)
            even, odd = row[:, :m], row[:, m:]
            blocks = (moved_right(odd.astype(F32)).astype(BF), even, odd, moved_left(even.astype(F32)).astype(BF))
            for k, block in enumerate(blocks):
                tx[pl.ds(pl.multiple_of(j * stack + k * c + part[0] * h, h), h), :] = block

    def cotangent_stack(j):
        for part in halves:
            at, left, here, right = part
            if j == 0:
                row = left[3]
            else:
                row = here[rows + j - 1] if j < 1 + rows // 2 else right[3]
            for k in range(2):
                block = row[:, k * m : (k + 1) * m]
                base = j * stack + at * c + k * h
                tu[pl.ds(pl.multiple_of(base, h), h), :] = block
                tu[pl.ds(pl.multiple_of(base + 2 * c, h), h), :] = moved_left(block.astype(F32)).astype(BF)

    def own_channels(ref, index, out, r):
        for par in range(2):
            at = pl.multiple_of(index * stack + (1 + par) * c + me * h, h)
            out[par, pl.ds((rows + 1 - r) * h, h), :] = ref[pl.ds(at, h), :]

    def first_dot(k):
        return dot(wb1[...], tx[pl.ds(k * stack, 3 * stack), :])

    def first_use(k, z):
        act, slope = gelu_parts(z)
        put_stack(th1, k * stack, act)
        if 2 <= k < rows + 2:
            dz1[pl.ds((k - 2) * 2 * c, 2 * c), :] = slope
        if k + 4 < rows + 6:
            input_stack(k + 4)

    def second_dot(k):
        return dot(wb2[...], th1[pl.ds(k * stack, 3 * stack), :])

    def second_use(k, z):
        act, slope = gelu_parts(z)
        dz2[pl.ds(k * 2 * c, 2 * c), :] = slope
        if k <= rows:
            th2[pl.ds(k * 3 * c, c), :] = moved_right(act[c:]).astype(BF)
            th2[pl.ds(k * 3 * c + c, 2 * c), :] = act.astype(BF)

    def third_dot(k):
        q = k // 2
        if k % 2 == 0:
            return dot(wt3o[...], tu[pl.ds(q * stack, 2 * stack), :])
        return dot(wt3e[...], tu[pl.ds((q + 1) * stack, stack), :])

    def third_use(k, back):
        put_stack(td2, k * stack, back * dz2[pl.ds(k * 2 * c, 2 * c), :])
        if 1 <= k <= rows:
            own_channels(td2, k, s2, k - 1)

    def back_dot(k):
        return dot(wt2[...], td2[pl.ds(k * stack, 3 * stack), :])

    def back_use(k, back):
        put_stack(td1, (k + 2) * stack, back * dz1[pl.ds(k * 2 * c, 2 * c), :])
        own_channels(td1, k + 2, s1, k)

    def third_grad(a):
        total = jnp.zeros((c, 3 * c), F32)
        for r in range(rows // 2):
            mine = tu[pl.ds(pl.multiple_of((r + 1) * stack + me * c, c), c), :]
            total = total + dot_t(mine, th2[pl.ds((2 * r + a) * 3 * c, 3 * c), :])
        return total

    def third_grad_use(a, total):
        for b in range(3):
            dw3[pl.ds((a * 3 + b) * c, c), :] = total[:, b * c : (b + 1) * c].astype(BF)

    def kernel_grad(deltas, stacks, first):
        total = jnp.zeros((3 * h, 3 * c), F32)
        for q in range(rows + 2):
            for par in range(2):
                mine = deltas[par, pl.ds((rows + 1 - q) * h, 3 * h), :]
                total = total + dot_t(mine, stacks[pl.ds((q + first) * stack + par * c, 3 * c), :])
        return total

    def kernel_grad_use(out, total):
        for a in range(3):
            for b in range(3):
                out[pl.ds((a * 3 + b) * h, h), :] = total[a * h : (a + 1) * h, b * c : (b + 1) * c].astype(BF)

    z1 = [(functools.partial(first_dot, k), functools.partial(first_use, k)) for k in range(rows + 4)]
    z2 = [(functools.partial(second_dot, k), functools.partial(second_use, k)) for k in range(rows + 2)]
    g2 = [(functools.partial(third_dot, k), functools.partial(third_use, k)) for k in range(rows + 2)]
    g1 = [(functools.partial(back_dot, k), functools.partial(back_use, k)) for k in range(rows)]
    w3 = [(functools.partial(third_grad, a), functools.partial(third_grad_use, a)) for a in range(3)]
    w2 = (lambda: kernel_grad(s2, th1, 1), functools.partial(kernel_grad_use, dw2))
    w1 = (lambda: kernel_grad(s1, tx, 2), functools.partial(kernel_grad_use, dw1))
    tasks = z1[:4]
    for k in range(rows):
        tasks += [z2[k], z1[k + 4]]
    tasks += [z2[rows], g2[0], z2[rows + 1], g2[1]]
    for k in range(2, rows + 2):
        tasks += [g2[k]] + ([w3[k - 2]] if k < 5 else []) + ([g1[k - 3]] if k > 2 else [])
    tasks += [w2, g1[rows - 1], w1]

    for j in range(4):
        input_stack(j)
    for j in range(rows // 2 + 2):
        cotangent_stack(j)
    for out in (s2, s1):
        for par in range(2):
            out[par, pl.ds(0, 2 * h), :] = jnp.zeros((2 * h, m), BF)
            out[par, pl.ds((rows + 2) * h, 2 * h), :] = jnp.zeros((2 * h, m), BF)
    for k in (0, 1, rows + 2, rows + 3):
        td1[pl.ds(k * stack, stack), :] = jnp.zeros((stack, m), BF)

    waiting = None
    for task in tasks:
        if task is w1:
            waiting[0](waiting[1])
            waiting = None
        value = task[0]()
        if waiting:
            waiting[0](waiting[1])
        waiting = (task[1], value)
    waiting[0](waiting[1])

    keep_a, send_a, keep_b, send_b = pieces
    for out, grads, first, second in (
        (keep_a, (dw3,), 0, 2), (send_a, (dw3,), 1, 3), (keep_b, (dw2, dw1), 0, 1), (send_b, (dw2, dw1), 2, 3),
    ):
        base = 0
        for k in (first, second):
            at = piece_at(core[1], k)
            for grad in grads:
                size = grad.shape[0] // 4
                out[pl.ds(base, size), :] = grad[pl.ds(pl.multiple_of(at * size, 16), size), :]
                base += size


def inputs_kernel(td1, wt1, main, rims):
    h = wt1.shape[0] // 2
    stack = 8 * h
    rows = main.shape[0]
    for k in range(rows + 2):
        back = dot(wt1[...], td1[pl.ds(k * stack, 3 * stack), :])
        flat = jnp.concatenate([back[:h], back[h:]], axis=1)
        if k == 0:
            rims[0] = flat.astype(BF)
        elif k == rows + 1:
            rims[1] = flat.astype(BF)
        else:
            main[k - 1] = flat


def piece_at(tile, k):
    return lax.bitwise_xor(lax.rem(tile, 4), k)


def halves_kernel(keep_a, got_a, keep_b, got_b, keep, send_a, send_b):
    n = send_a.shape[0]
    for k, (mine, got, send) in enumerate(((keep_a, got_a, send_a), (keep_b, got_b, send_b))):
        total = (mine[...].astype(F32) + got[...].astype(F32)).astype(BF)
        keep[pl.ds(k * n, n), :] = total[:n]
        send[...] = total[n:]


def quarters_kernel(keep, got_a, got_b, out):
    n = got_a.shape[0]
    for k, got in enumerate((got_a, got_b)):
        at = pl.ds(k * n, n)
        out[at, :] = (keep[at, :].astype(F32) + got[...].astype(F32)).astype(BF)


def sum_kernel(mine, got, out):
    out[...] = (mine[...].astype(F32) + got[...].astype(F32)).astype(BF)


def last_kernel(scales, core, *rest):
    pieces, outs = rest[:-3], rest[-3:]
    for k, piece in enumerate(pieces):
        at = piece_at(core[1], k)
        base = 0
        for out, scale in zip(outs, scales):
            size = out.shape[0] // len(pieces)
            out[pl.ds(pl.multiple_of(at * size, 16), size), :] = piece[pl.ds(base, size), :].astype(F32) * scale
            base += size


def call(body, name, outs, scratch, limit, *args):
    vmem = pl.BlockSpec(memory_space=pltpu.VMEM)
    scalar = pl.BlockSpec(memory_space=pltpu.SMEM)
    return pl.pallas_call(
        body,
        out_shape=tuple(jax.ShapeDtypeStruct(shape, kind) for shape, kind in outs),
        in_specs=[scalar if a.dtype == jnp.int32 else vmem for a in args],
        out_specs=tuple(vmem for _ in outs),
        scratch_shapes=[pltpu.VMEM(shape, kind) for shape, kind in scratch],
        compiler_params=pltpu.CompilerParams(vmem_limit_bytes=limit * 1024 * 1024),
        cost_estimate=pl.CostEstimate(flops=10**6, bytes_accessed=10**5, transcendentals=0),
        name=name,
    )(*args)


def shards(inputs, w_first, w_second, w_third, cotangent, mirror):
    h, rows, cols = inputs.shape
    outs = cotangent.shape[0]
    m = cols // 2
    c = 2 * h
    stack = 4 * c
    tiles = lax.axis_size("blk")
    up = [(i, (i + 1) % tiles) for i in range(tiles)]
    down = [(j, i) for i, j in up]
    core = jnp.stack([lax.axis_index("chan"), lax.axis_index("blk")]).astype(jnp.int32)

    def across(piece):
        return lax.ppermute(piece, "chan", [(0, 1), (1, 0)])

    def swapped(piece, k):
        return lax.ppermute(piece, "blk", [(i, i ^ k) for i in range(tiles)])

    to = lax.broadcasted_iota(jnp.int32, (cols, cols), 1)
    place = 2 * (to % m) + to // m
    place = jnp.where(mirror[0] == 1, cols - 1 - place, place)
    split = (lax.broadcasted_iota(jnp.int32, (cols, cols), 0) == place).astype(BF)

    own, last, lead = call(
        orient_kernel, "orient",
        [((rows + rows // 2, h, cols), BF), ((4, h, cols), BF), ((4, h, cols), BF)], [], 16, mirror, inputs, cotangent,
    )
    before = lax.ppermute(last, "blk", up)
    after = lax.ppermute(lead, "blk", down)
    w12 = jnp.concatenate([w.reshape(-1, c) for w in (w_first, w_second)])
    w3 = w_third.reshape(-1, c)
    wb1, wb2, wt2, wt1, wt3e, wt3o = call(
        weights_kernel, "weights",
        [((2 * c, 3 * stack), BF)] * 3 + [((c, 3 * stack), BF), ((2 * c, stack), BF), ((2 * c, 2 * stack), BF)],
        [], 16, core, w12, across(w12), w3, across(w3),
    )

    size = 9 * (c + 2 * h) // 4
    keep_a, send_a, keep_b, send_b, td1 = call(
        main_kernel, "main",
        [((size, c), BF)] * 4 + [(((rows + 4) * stack, m), BF)],
        [
            (((rows + 6) * stack, m), BF),
            (((rows + 4) * stack, m), BF),
            (((rows + 1) * 3 * c, m), BF),
            (((rows // 2 + 2) * stack, m), BF),
            (((rows + 2) * stack, m), BF),
            ((2, (rows + 4) * h, m), BF),
            ((2, (rows + 4) * h, m), BF),
            ((rows * 2 * c, m), F32),
            (((rows + 2) * 2 * c, m), F32),
            ((9 * h, c), BF),
            ((9 * h, c), BF),
            ((9 * c, c), BF),
        ],
        40, core, own, across(own), before, across(before), after, across(after), wb1, wb2, wt2, wt3e, wt3o,
    )
    half = ((size // 2, c), BF)
    keep, send_a, send_b = call(
        halves_kernel, "halves", [((size, c), BF), half, half], [], 8,
        keep_a, swapped(send_a, 1), keep_b, swapped(send_b, 2),
    )
    (mine,) = call(
        quarters_kernel, "quarters", [((size, c), BF)], [], 8, keep, swapped(send_a, 2), swapped(send_b, 1),
    )
    bit = 4
    while bit < tiles:
        if bit * 2 >= tiles:
            mine, td1 = lax.optimization_barrier((mine, td1))
        (mine,) = call(sum_kernel, "sum", [((size, c), BF)], [], 8, mine, swapped(mine, bit))
        bit *= 2
    main, rims = call(
        inputs_kernel, "inputs",
        [((rows, h, cols), F32), ((2, h, cols), BF)], [], 16, td1, wt1,
    )
    from_next = lax.ppermute(rims[0], "blk", down)
    from_prev = lax.ppermute(rims[1], "blk", up)
    from_next, from_prev, _ = lax.optimization_barrier((from_next, from_prev, mine))
    from_next, from_prev = from_next.astype(F32), from_prev.astype(F32)
    main = jnp.concatenate([main[:1] + from_prev, main[1:-1], main[-1:] + from_next]).astype(BF)
    grad_inputs = jnp.einsum("rin,cn->irc", main, split, preferred_element_type=F32).astype(BF)

    parts = [mine] + [swapped(mine, k) for k in range(1, 4)]
    cells = rows * cols * tiles
    wide, narrow = 1.0 / math.sqrt(cells // 4), 1.0 / math.sqrt(cells)
    third, second, first = call(
        functools.partial(last_kernel, (wide, narrow, narrow)), "last",
        [((9 * c, c), F32), ((9 * h, c), F32), ((9 * h, c), F32)], [], 16, core, *parts,
    )
    return grad_inputs, first.reshape(3, 3, h, c), second.reshape(3, 3, h, c), third.reshape(3, 3, c, c)


def solution(mesh):
    placed = (
        P("chan", "blk", None),
        P(None, None, "chan", None),
        P(None, None, "chan", None),
        P(None, None, "chan", None),
        P("chan", "blk", None),
        P("blk"),
    )
    return jax.shard_map(
        shards,
        mesh=mesh,
        in_specs=placed,
        out_specs=(
            P("chan", "blk", None),
            P(None, None, "chan", None),
            P(None, None, "chan", None),
            P(None, None, "chan", None),
        ),
        check_vma=False,
    )
```

```python
import functools
import math

import jax
import jax.numpy as jnp
from jax import lax
from jax.experimental import pallas as pl
from jax.experimental.pallas import tpu as pltpu
from jax.sharding import PartitionSpec as P

BF = jnp.bfloat16
F32 = jnp.float32
ROOT = math.sqrt(2.0 / math.pi)
CUBIC = 0.044715


def dot(a, b):
    return jnp.dot(a, b, preferred_element_type=F32)


def dot_t(a, b):
    return lax.dot_general(a, b, (((1,), (1,)), ((), ())), preferred_element_type=F32)


def moved_right(v):
    lane = lax.broadcasted_iota(jnp.int32, v.shape, 1)
    return jnp.where(lane == 0, 0.0, pltpu.roll(v, 1, 1))


def moved_left(v):
    lane = lax.broadcasted_iota(jnp.int32, v.shape, 1)
    width = v.shape[1]
    return jnp.where(lane == width - 1, 0.0, pltpu.roll(v, width - 1, 1))


def gelu_parts(v):
    square = v * v
    t = jnp.tanh(v * (ROOT + (ROOT * CUBIC) * square))
    half = 0.5 * v
    return half + half * t, 0.5 + 0.5 * t + half * (1.0 - t * t) * (ROOT + (3.0 * ROOT * CUBIC) * square)


def either(me, own, other):
    return jnp.where(me == 0, own, other), jnp.where(me == 0, other, own)


def weights_kernel(core, own, other, own3, other3, wb1, wb2, wt2, wt1, wt3e, wt3o):
    me = core[0]
    c = own.shape[1]
    h = c // 2
    stack = 4 * c
    for out in (wb1, wb2, wt2, wt1, wt3e, wt3o):
        out[...] = jnp.zeros_like(out)
    for a in range(3):
        for b in range(3):
            tap = a * 3 + b
            at = pl.ds(tap * h, h)
            first = jnp.concatenate(either(me, own[at, :], other[at, :]), axis=0)
            at = pl.ds((9 + tap) * h, h)
            second = jnp.concatenate(either(me, own[at, :], other[at, :]), axis=0)
            for par in range(2):
                at = pl.ds(a * stack + (b + par) * c, c)
                wb1[pl.ds(par * c, c), at] = first
                wb2[pl.ds(par * c, c), at] = second
            turned = second.T
            first_turned = first.T
            half_turned = jnp.where(me == 0, first_turned[:h], first_turned[h:])
            for par in range(2):
                at = pl.ds((2 - a) * stack + (2 - b + par) * c, c)
                wt2[pl.ds(par * c, c), at] = turned
                wt1[pl.ds(par * h, h), at] = half_turned
            at = pl.ds(tap * c, c)
            third = jnp.concatenate([w.T for w in either(me, own3[at, :], other3[at, :])], axis=1)
            par = 0 if b == 1 else 1
            side = 1 if b == 0 else 0
            if a == 1:
                wt3e[pl.ds(par * c, c), pl.ds(side * 2 * c, 2 * c)] = third
            else:
                back = 0 if a == 2 else 1
                wt3o[pl.ds(par * c, c), pl.ds((back * 2 + side) * 2 * c, 2 * c)] = third


def put_stack(ref, base, row):
    c = row.shape[0] // 2
    even, odd = row[:c], row[c:]
    ref[pl.ds(base, c), :] = moved_right(odd).astype(BF)
    ref[pl.ds(base + c, 2 * c), :] = row.astype(BF)
    ref[pl.ds(base + 3 * c, c), :] = moved_left(even).astype(BF)


def run(tasks):
    waiting = None
    for task in tasks:
        if len(task) > 2:
            waiting[0](waiting[1])
            waiting = None
        value = task[0]()
        if waiting:
            waiting[0](waiting[1])
        waiting = (task[1], value)
    waiting[0](waiting[1])


def deal(pieces, grads, tile):
    for k, piece in enumerate(pieces):
        at = piece_at(tile, k)
        base = 0
        for grad in grads:
            size = grad.shape[0] // 4
            piece[pl.ds(base, size), :] = grad[pl.ds(pl.multiple_of(at * size, 16), size), :]
            base += size


def forward_kernel(
    core, own, other, own_before, before, own_after, after, wb1, wb2,
    p0, p1, p2, p3, tx, th1, tu, dz1, dz2, th2, dw3,
):
    me = core[0]
    c = wb1.shape[0] // 2
    h = c // 2
    m = tx.shape[1]
    stack = 4 * c
    rows = own.shape[0] // 3 * 2
    halves = ((me, own_before, own, own_after), (1 - me, before, other, after))

    def source(j, part):
        _, left, here, right = part
        if j < 3:
            return left[j]
        return here[j - 3] if j < 3 + rows else right[j - 3 - rows]

    def input_stack(j):
        for part in halves:
            row = source(j, part)
            even, odd = row[:, :m], row[:, m:]
            blocks = (moved_right(odd.astype(F32)).astype(BF), even, odd, moved_left(even.astype(F32)).astype(BF))
            for k, block in enumerate(blocks):
                tx[pl.ds(pl.multiple_of(j * stack + k * c + part[0] * h, h), h), :] = block

    def cotangent_stack(j):
        for part in halves:
            at, left, here, right = part
            if j == 0:
                row = left[3]
            else:
                row = here[rows + j - 1] if j < 1 + rows // 2 else right[3]
            for k in range(2):
                block = row[:, k * m : (k + 1) * m]
                base = j * stack + at * c + k * h
                tu[pl.ds(pl.multiple_of(base, h), h), :] = block
                tu[pl.ds(pl.multiple_of(base + 2 * c, h), h), :] = moved_left(block.astype(F32)).astype(BF)

    def first_dot(k):
        return dot(wb1[...], tx[pl.ds(k * stack, 3 * stack), :])

    def first_use(k, z):
        act, slope = gelu_parts(z)
        put_stack(th1, k * stack, act)
        if 2 <= k < rows + 2:
            dz1[pl.ds((k - 2) * 2 * c, 2 * c), :] = slope
        if k + 4 < rows + 6:
            input_stack(k + 4)

    def second_dot(k):
        return dot(wb2[...], th1[pl.ds(k * stack, 3 * stack), :])

    def second_use(k, z):
        act, slope = gelu_parts(z)
        dz2[pl.ds(k * 2 * c, 2 * c), :] = slope
        if k <= rows:
            th2[pl.ds(k * 3 * c, c), :] = moved_right(act[c:]).astype(BF)
            th2[pl.ds(k * 3 * c + c, 2 * c), :] = act.astype(BF)

    def third_grad(a):
        total = jnp.zeros((c, 3 * c), F32)
        for r in range(rows // 2):
            mine = tu[pl.ds(pl.multiple_of((r + 1) * stack + me * c, c), c), :]
            total = total + dot_t(mine, th2[pl.ds((2 * r + a) * 3 * c, 3 * c), :])
        return total

    def third_grad_use(a, total):
        for b in range(3):
            dw3[pl.ds((a * 3 + b) * c, c), :] = total[:, b * c : (b + 1) * c].astype(BF)

    z1 = [(functools.partial(first_dot, k), functools.partial(first_use, k)) for k in range(rows + 4)]
    z2 = [(functools.partial(second_dot, k), functools.partial(second_use, k)) for k in range(rows + 2)]
    w3 = [(functools.partial(third_grad, a), functools.partial(third_grad_use, a)) for a in range(3)]
    tasks = z1[:4]
    for k in range(rows):
        tasks += [z2[k], z1[k + 4]]
    tasks += [z2[rows], w3[0], z2[rows + 1], w3[1], w3[2]]
    for j in range(4):
        input_stack(j)
    for j in range(rows // 2 + 2):
        cotangent_stack(j)
    run(tasks)
    deal((p0, p1, p2, p3), (dw3,), core[1])


def backward_kernel(
    core, tx, th1, tu, dz1, dz2, wt2, wt3e, wt3o,
    p0, p1, p2, p3, td1, td2, s2, s1, dw1, dw2,
):
    me = core[0]
    c = wt2.shape[0] // 2
    h = c // 2
    m = tx.shape[1]
    stack = 4 * c
    rows = td1.shape[0] // stack - 4

    def own_channels(ref, index, out, r):
        for par in range(2):
            at = pl.multiple_of(index * stack + (1 + par) * c + me * h, h)
            out[par, pl.ds((rows + 1 - r) * h, h), :] = ref[pl.ds(at, h), :]

    def third_dot(k):
        q = k // 2
        if k % 2 == 0:
            return dot(wt3o[...], tu[pl.ds(q * stack, 2 * stack), :])
        return dot(wt3e[...], tu[pl.ds((q + 1) * stack, stack), :])

    def third_use(k, back):
        put_stack(td2, k * stack, back * dz2[pl.ds(k * 2 * c, 2 * c), :])
        if 1 <= k <= rows:
            own_channels(td2, k, s2, k - 1)

    def back_dot(k):
        return dot(wt2[...], td2[pl.ds(k * stack, 3 * stack), :])

    def back_use(k, back):
        put_stack(td1, (k + 2) * stack, back * dz1[pl.ds(k * 2 * c, 2 * c), :])
        own_channels(td1, k + 2, s1, k)

    def kernel_grad(deltas, stacks, first):
        total = jnp.zeros((3 * h, 3 * c), F32)
        for q in range(rows + 2):
            for par in range(2):
                mine = deltas[par, pl.ds((rows + 1 - q) * h, 3 * h), :]
                total = total + dot_t(mine, stacks[pl.ds((q + first) * stack + par * c, 3 * c), :])
        return total

    def kernel_grad_use(out, total):
        for a in range(3):
            for b in range(3):
                out[pl.ds((a * 3 + b) * h, h), :] = total[a * h : (a + 1) * h, b * c : (b + 1) * c].astype(BF)

    g2 = [(functools.partial(third_dot, k), functools.partial(third_use, k)) for k in range(rows + 2)]
    g1 = [(functools.partial(back_dot, k), functools.partial(back_use, k)) for k in range(rows)]
    w2 = (lambda: kernel_grad(s2, th1, 1), functools.partial(kernel_grad_use, dw2))
    w1 = (lambda: kernel_grad(s1, tx, 2), functools.partial(kernel_grad_use, dw1), "after")
    tasks = g2[:3]
    for k in range(3, rows + 2):
        tasks += [g2[k], g1[k - 3]]
    tasks += [w2, g1[rows - 1], w1]
    for out in (s2, s1):
        for par in range(2):
            out[par, pl.ds(0, 2 * h), :] = jnp.zeros((2 * h, m), BF)
            out[par, pl.ds((rows + 2) * h, 2 * h), :] = jnp.zeros((2 * h, m), BF)
    for k in (0, 1, rows + 2, rows + 3):
        td1[pl.ds(k * stack, stack), :] = jnp.zeros((stack, m), BF)
    run(tasks)
    deal((p0, p1, p2, p3), (dw2, dw1), core[1])


def inputs_kernel(td1, wt1, main, rims):
    h = wt1.shape[0] // 2
    stack = 8 * h
    rows = main.shape[0]
    for k in range(rows + 2):
        back = dot(wt1[...], td1[pl.ds(k * stack, 3 * stack), :])
        flat = jnp.concatenate([back[:h], back[h:]], axis=1)
        if k == 0:
            rims[0] = flat.astype(BF)
        elif k == rows + 1:
            rims[1] = flat.astype(BF)
        else:
            main[k - 1] = flat


def piece_at(tile, k):
    return lax.bitwise_xor(lax.rem(tile, 4), k)


def sum_kernel(*refs):
    total = refs[0][...].astype(F32)
    for piece in refs[1:-1]:
        total = total + piece[...].astype(F32)
    refs[-1][...] = total.astype(BF)


def last_kernel(scale, core, p0, p1, p2, p3, *outs):
    for k, piece in enumerate((p0, p1, p2, p3)):
        at = piece_at(core[1], k)
        base = 0
        for out in outs:
            size = out.shape[0] // 4
            out[pl.ds(pl.multiple_of(at * size, 16), size), :] = piece[pl.ds(base, size), :].astype(F32) * scale
            base += size


def call(body, name, outs, scratch, limit, *args):
    vmem = pl.BlockSpec(memory_space=pltpu.VMEM)
    scalar = pl.BlockSpec(memory_space=pltpu.SMEM)
    return pl.pallas_call(
        body,
        out_shape=tuple(jax.ShapeDtypeStruct(shape, kind) for shape, kind in outs),
        in_specs=[scalar if a.dtype == jnp.int32 else vmem for a in args],
        out_specs=tuple(vmem for _ in outs),
        scratch_shapes=[pltpu.VMEM(shape, kind) for shape, kind in scratch],
        compiler_params=pltpu.CompilerParams(vmem_limit_bytes=limit * 1024 * 1024),
        cost_estimate=pl.CostEstimate(flops=10**6, bytes_accessed=10**5, transcendentals=0),
        name=name,
    )(*args)


def shards(inputs, w_first, w_second, w_third, cotangent, mirror):
    h, rows, cols = inputs.shape
    m = cols // 2
    c = 2 * h
    stack = 4 * c
    tiles = lax.axis_size("blk")
    up = [(i, (i + 1) % tiles) for i in range(tiles)]
    down = [(j, i) for i, j in up]
    core = jnp.stack([lax.axis_index("chan"), lax.axis_index("blk")]).astype(jnp.int32)

    def across(piece):
        return lax.ppermute(piece, "chan", [(0, 1), (1, 0)])

    def swapped(piece, k):
        return lax.ppermute(piece, "blk", [(i, i ^ k) for i in range(tiles)])

    def total(*parts):
        return call(sum_kernel, "sum", [(parts[0].shape, BF)], [], 8, *parts)[0]

    to = lax.broadcasted_iota(jnp.int32, (cols, cols), 1)
    place = 2 * (to % m) + to // m
    place = jnp.where(mirror[0] == 1, cols - 1 - place, place)
    split = (lax.broadcasted_iota(jnp.int32, (cols, cols), 0) == place).astype(BF)
    to = lax.broadcasted_iota(jnp.int32, (m, m), 1)
    place = jnp.where(mirror[0] == 1, m - 1 - to, to)
    turn = (lax.broadcasted_iota(jnp.int32, (m, m), 0) == place).astype(BF)

    x = jnp.einsum("irc,cn->rin", inputs, split, preferred_element_type=F32).astype(BF)
    u = jnp.einsum("orc,cn->ron", cotangent, turn, preferred_element_type=F32).astype(BF)
    u = jnp.concatenate([u[:, :h], u[:, h:]], axis=2)
    before = lax.ppermute(jnp.concatenate([x[rows - 3 :], u[rows // 2 - 1 :]]), "blk", up)
    after = lax.ppermute(jnp.concatenate([x[:3], u[:1]]), "blk", down)
    own = jnp.concatenate([x, u])
    w12 = jnp.concatenate([w.reshape(-1, c) for w in (w_first, w_second)])
    w3 = w_third.reshape(-1, c)
    wb1, wb2, wt2, wt1, wt3e, wt3o = call(
        weights_kernel, "weights",
        [((2 * c, 3 * stack), BF)] * 3 + [((c, 3 * stack), BF), ((2 * c, stack), BF), ((2 * c, 2 * stack), BF)],
        [], 16, core, w12, across(w12), w3, across(w3),
    )

    piece = ((9 * c // 4, c), BF)
    *p_parts, tx, th1, tu, dz1, dz2 = call(
        forward_kernel, "forward",
        [piece] * 4
        + [
            (((rows + 6) * stack, m), BF),
            (((rows + 4) * stack, m), BF),
            (((rows // 2 + 2) * stack, m), BF),
            ((rows * 2 * c, m), F32),
            (((rows + 2) * 2 * c, m), F32),
        ],
        [(((rows + 1) * 3 * c, m), BF), ((9 * c, c), BF)],
        32, core, own, across(own), before, across(before), after, across(after), wb1, wb2,
    )
    p_parts = p_parts[:1] + [swapped(part, k) for k, part in enumerate(p_parts[1:], 1)]
    *q_parts, td1 = call(
        backward_kernel, "backward",
        [piece] * 4 + [(((rows + 4) * stack, m), BF)],
        [
            (((rows + 2) * stack, m), BF),
            ((2, (rows + 4) * h, m), BF),
            ((2, (rows + 4) * h, m), BF),
            ((9 * h, c), BF),
            ((9 * h, c), BF),
        ],
        24, core, tx, th1, tu, dz1, dz2, wt2, wt3e, wt3o,
    )
    q_parts = q_parts[:1] + [swapped(part, k) for k, part in enumerate(q_parts[1:], 1)]
    p_sum = total(*p_parts)
    q_parts, _ = lax.optimization_barrier((q_parts, p_sum))
    q_sum = total(*q_parts)
    bit = 4
    while bit < tiles:
        if bit * 2 >= tiles:
            td1, _ = lax.optimization_barrier((td1, q_sum))
        p_got, q_got = swapped(p_sum, bit), swapped(q_sum, bit)
        p_sum = total(p_sum, p_got)
        ahead = p_sum
        if bit * 2 >= tiles:
            p_all = [p_sum] + [swapped(p_sum, k) for k in range(1, 4)]
            ahead = p_all[1]
        q_got, _ = lax.optimization_barrier((q_got, ahead))
        q_sum = total(q_sum, q_got)
        bit *= 2
    main, rims = call(
        inputs_kernel, "inputs",
        [((rows, h, cols), F32), ((2, h, cols), BF)], [], 16, td1, wt1,
    )
    from_next = lax.ppermute(rims[0], "blk", down)
    from_prev = lax.ppermute(rims[1], "blk", up)
    from_next, from_prev, _ = lax.optimization_barrier((from_next, from_prev, q_sum))
    from_next, from_prev = from_next.astype(F32), from_prev.astype(F32)
    main = jnp.concatenate([main[:1] + from_prev, main[1:-1], main[-1:] + from_next]).astype(BF)
    grad_inputs = jnp.einsum("rin,cn->irc", main, split, preferred_element_type=F32).astype(BF)

    cells = rows * cols * tiles
    (third,) = call(
        functools.partial(last_kernel, 1.0 / math.sqrt(cells // 4)), "third",
        [((9 * c, c), F32)], [], 8, core, *p_all,
    )
    second, first = call(
        functools.partial(last_kernel, 1.0 / math.sqrt(cells)), "last",
        [((9 * h, c), F32), ((9 * h, c), F32)], [], 8, core, q_sum, *[swapped(q_sum, k) for k in range(1, 4)],
    )
    return grad_inputs, first.reshape(3, 3, h, c), second.reshape(3, 3, h, c), third.reshape(3, 3, c, c)


def solution(mesh):
    placed = (
        P("chan", "blk", None),
        P(None, None, "chan", None),
        P(None, None, "chan", None),
        P(None, None, "chan", None),
        P("chan", "blk", None),
        P("blk"),
    )
    return jax.shard_map(
        shards,
        mesh=mesh,
        in_specs=placed,
        out_specs=(
            P("chan", "blk", None),
            P(None, None, "chan", None),
            P(None, None, "chan", None),
            P(None, None, "chan", None),
        ),
        check_vma=False,
    )
```

```python
import functools
import math

import jax
import jax.numpy as jnp
from jax import lax
from jax.experimental import pallas as pl
from jax.experimental.pallas import tpu as pltpu
from jax.sharding import PartitionSpec as P

BF = jnp.bfloat16
F32 = jnp.float32
ROOT = math.sqrt(2.0 / math.pi)
CUBIC = 0.044715


def dot(a, b):
    return jnp.dot(a, b, preferred_element_type=F32)


def dot_t(a, b):
    return lax.dot_general(a, b, (((1,), (1,)), ((), ())), preferred_element_type=F32)


def moved_right(v):
    lane = lax.broadcasted_iota(jnp.int32, v.shape, 1)
    return jnp.where(lane == 0, 0.0, pltpu.roll(v, 1, 1))


def moved_left(v):
    lane = lax.broadcasted_iota(jnp.int32, v.shape, 1)
    width = v.shape[1]
    return jnp.where(lane == width - 1, 0.0, pltpu.roll(v, width - 1, 1))


def gelu_parts(v):
    square = v * v
    t = jnp.tanh(v * (ROOT + (ROOT * CUBIC) * square))
    half = 0.5 * v
    return half + half * t, 0.5 + 0.5 * t + half * (1.0 - t * t) * (ROOT + (3.0 * ROOT * CUBIC) * square)


def either(me, own, other):
    return jnp.where(me == 0, own, other), jnp.where(me == 0, other, own)


def put_weights(me, own1, other1, own2, other2, own3, other3, wb1, wb2, wt2, wt1, wt3e, wt3o):
    c = own1.shape[1]
    h = c // 2
    stack = 4 * c
    for out in (wb1, wb2, wt2, wt1, wt3e, wt3o):
        out[...] = jnp.zeros_like(out)
    for a in range(3):
        for b in range(3):
            tap = a * 3 + b
            at = pl.ds(tap * h, h)
            first = jnp.concatenate(either(me, own1[at, :], other1[at, :]), axis=0)
            second = jnp.concatenate(either(me, own2[at, :], other2[at, :]), axis=0)
            for par in range(2):
                at = pl.ds(a * stack + (b + par) * c, c)
                wb1[pl.ds(par * c, c), at] = first
                wb2[pl.ds(par * c, c), at] = second
            turned = second.T
            first_turned = first.T
            half_turned = jnp.where(me == 0, first_turned[:h], first_turned[h:])
            for par in range(2):
                at = pl.ds((2 - a) * stack + (2 - b + par) * c, c)
                wt2[pl.ds(par * c, c), at] = turned
                wt1[pl.ds(par * h, h), at] = half_turned
            at = pl.ds(tap * c, c)
            third = jnp.concatenate([w.T for w in either(me, own3[at, :], other3[at, :])], axis=1)
            par = 0 if b == 1 else 1
            side = 1 if b == 0 else 0
            if a == 1:
                wt3e[pl.ds(par * c, c), pl.ds(side * 2 * c, 2 * c)] = third
            else:
                back = 0 if a == 2 else 1
                wt3o[pl.ds(par * c, c), pl.ds((back * 2 + side) * 2 * c, 2 * c)] = third


def put_stack(ref, base, row):
    c = row.shape[0] // 2
    even, odd = row[:c], row[c:]
    ref[pl.ds(base, c), :] = moved_right(odd).astype(BF)
    ref[pl.ds(base + c, 2 * c), :] = row.astype(BF)
    ref[pl.ds(base + 3 * c, c), :] = moved_left(even).astype(BF)


def run(tasks):
    waiting = None
    for task in tasks:
        value = task[0]()
        if waiting:
            waiting[0](waiting[1])
        waiting = (task[1], value)
    waiting[0](waiting[1])


def deal(pieces, grads, tile):
    for k, piece in enumerate(pieces):
        at = piece_at(tile, k)
        base = 0
        for grad in grads:
            size = grad.shape[0] // 4
            piece[pl.ds(base, size), :] = grad[pl.ds(pl.multiple_of(at * size, 16), size), :]
            base += size


def put_input(ref, base, me, own, other):
    m = own.shape[1] // 2
    h = own.shape[0]
    for at, row in ((me, own), (1 - me, other)):
        even, odd = row[:, :m], row[:, m:]
        blocks = (moved_right(odd.astype(F32)).astype(BF), even, odd, moved_left(even.astype(F32)).astype(BF))
        for k, block in enumerate(blocks):
            ref[pl.ds(pl.multiple_of(base + k * 2 * h + at * h, h), h), :] = block


def put_cotangent(ref, base, me, own, other):
    m = own.shape[1] // 2
    h = own.shape[0]
    for at, row in ((me, own), (1 - me, other)):
        for k in range(2):
            block = row[:, k * m : (k + 1) * m]
            to = base + at * 2 * h + k * h
            ref[pl.ds(pl.multiple_of(to, h), h), :] = block
            ref[pl.ds(pl.multiple_of(to + 4 * h, h), h), :] = moved_left(block.astype(F32)).astype(BF)


def inner_kernel(
    core, own, other, w1, other1, w2, other2, w3, other3,
    wb1, wb2, wt2, wt1, wt3e, wt3o, tx, tu, th1, dz1, g2,
):
    me = core[0]
    c = wb1.shape[0] // 2
    stack = 4 * c
    rows = own.shape[0] // 3 * 2
    put_weights(me, w1, other1, w2, other2, w3, other3, wb1, wb2, wt2, wt1, wt3e, wt3o)
    for r in range(rows):
        put_input(tx, r * stack, me, own[r], other[r])
    for r in range(rows // 2):
        put_cotangent(tu, r * stack, me, own[rows + r], other[rows + r])

    def first_dot(r):
        return dot(wb1[...], tx[pl.ds((r - 1) * stack, 3 * stack), :])

    def first_use(r, z):
        act, slope = gelu_parts(z)
        put_stack(th1, (r - 1) * stack, act)
        dz1[pl.ds((r - 1) * 2 * c, 2 * c), :] = slope

    def third_dot(r):
        if r % 2 == 0:
            return dot(wt3e[...], tu[pl.ds(r // 2 * stack, stack), :])
        return dot(wt3o[...], tu[pl.ds(r // 2 * stack, 2 * stack), :])

    def third_use(r, back):
        g2[pl.ds(r * 2 * c, 2 * c), :] = back

    z1 = [(functools.partial(first_dot, r), functools.partial(first_use, r)) for r in range(1, rows - 1)]
    back = [(functools.partial(third_dot, r), functools.partial(third_use, r)) for r in range(rows - 1)]
    run(z1 + back)


def main_kernel(
    core, own_before, before, own_after, after, wb1, wb2, wt2, wt3e, wt3o, txi, tui, th1i, dz1i, g2i,
    p0, p1, p2, p3, td1, txo, tuo, th1o, dz1o, dz2, th2, td2, s2, s1, dw1, dw2, dw3,
):
    me = core[0]
    c = wb1.shape[0] // 2
    h = c // 2
    m = td1.shape[1]
    stack = 4 * c
    rows = td1.shape[0] // stack - 4

    def input_at(r):
        if 0 <= r < rows:
            return txi, r * stack
        return txo, (r + 3 if r < 0 else r - rows + 3) * stack

    def first_at(r):
        if 1 <= r < rows - 1:
            return th1i, (r - 1) * stack
        return th1o, (r + 2 if r < 1 else r - rows + 4) * stack

    def cotangent_at(r):
        if 0 <= r < rows // 2:
            return tui, r * stack
        return tuo, 0 if r < 0 else stack

    def window(at, first, count):
        places = [at(r) for r in range(first, first + count)]
        return jnp.concatenate([ref[pl.ds(base, stack), :] for ref, base in places], axis=0)

    def own_channels(ref, index, out, r):
        for par in range(2):
            at = pl.multiple_of(index * stack + (1 + par) * c + me * h, h)
            out[par, pl.ds((rows + 1 - r) * h, h), :] = ref[pl.ds(at, h), :]

    def first_dot(r):
        return dot(wb1[...], window(input_at, r - 1, 3))

    def first_use(r, z):
        act, slope = gelu_parts(z)
        ref, base = first_at(r)
        put_stack(ref, base, act)
        if r in (0, rows - 1):
            dz1o[pl.ds((r > 0) * 2 * c, 2 * c), :] = slope

    def second_dot(r):
        return dot(wb2[...], window(first_at, r - 1, 3))

    def second_use(r, z):
        act, slope = gelu_parts(z)
        k = r + 1
        dz2[pl.ds(k * 2 * c, 2 * c), :] = slope
        if r < rows:
            th2[pl.ds(k * 3 * c, c), :] = moved_right(act[c:]).astype(BF)
            th2[pl.ds(k * 3 * c + c, 2 * c), :] = act.astype(BF)

    def third_dot(r):
        if 0 <= r < rows - 1:
            return None
        if r % 2 == 0:
            return dot(wt3e[...], window(cotangent_at, r // 2, 1))
        return dot(wt3o[...], window(cotangent_at, (r - 1) // 2 if r > 0 else -1, 2))

    def third_use(r, back):
        if back is None:
            back = g2i[pl.ds(r * 2 * c, 2 * c), :]
        k = r + 1
        put_stack(td2, k * stack, back * dz2[pl.ds(k * 2 * c, 2 * c), :])
        if 0 <= r < rows:
            own_channels(td2, k, s2, r)

    def back_dot(r):
        return dot(wt2[...], td2[pl.ds(r * stack, 3 * stack), :])

    def back_use(r, back):
        if 0 < r < rows - 1:
            slope = dz1i[pl.ds((r - 1) * 2 * c, 2 * c), :]
        else:
            slope = dz1o[pl.ds((r > 0) * 2 * c, 2 * c), :]
        put_stack(td1, (r + 2) * stack, back * slope)
        own_channels(td1, r + 2, s1, r)

    def third_grad(a):
        total = jnp.zeros((c, 3 * c), F32)
        for r in range(rows // 2):
            mine = tui[pl.ds(pl.multiple_of(r * stack + me * c, c), c), :]
            total = total + dot_t(mine, th2[pl.ds((2 * r + a) * 3 * c, 3 * c), :])
        return total

    def third_grad_use(a, total):
        for b in range(3):
            dw3[pl.ds((a * 3 + b) * c, c), :] = total[:, b * c : (b + 1) * c].astype(BF)

    def kernel_grad(deltas, at):
        total = jnp.zeros((3 * h, 3 * c), F32)
        for q in range(rows + 2):
            ref, base = at(q - 1)
            for par in range(2):
                mine = deltas[par, pl.ds((rows + 1 - q) * h, 3 * h), :]
                total = total + dot_t(mine, ref[pl.ds(base + par * c, 3 * c), :])
        return total

    def kernel_grad_use(out, total):
        for a in range(3):
            for b in range(3):
                out[pl.ds((a * 3 + b) * h, h), :] = total[a * h : (a + 1) * h, b * c : (b + 1) * c].astype(BF)

    def task(does, uses, r):
        return functools.partial(does, r), functools.partial(uses, r)

    z1 = {r: task(first_dot, first_use, r) for r in range(-2, rows + 2)}
    z2 = {r: task(second_dot, second_use, r) for r in range(-1, rows + 1)}
    g2 = {r: task(third_dot, third_use, r) for r in range(-1, rows + 1)}
    g1 = {r: task(back_dot, back_use, r) for r in range(rows)}
    w3 = {a: task(third_grad, third_grad_use, a) for a in range(3)}
    w2 = (lambda: kernel_grad(s2, first_at), functools.partial(kernel_grad_use, dw2))
    w1 = (lambda: kernel_grad(s1, input_at), functools.partial(kernel_grad_use, dw1))
    tasks = [z1[-2], z1[-1], z1[0], z1[rows - 1], z2[-1], z1[rows], z2[0], z1[rows + 1]]
    tasks += [z2[r] for r in range(1, rows)] + [g2[-1], z2[rows]] + [g2[r] for r in range(rows)]
    tasks += [w3[0], g1[0], g2[rows], w3[1]] + [g1[r] for r in range(1, rows - 1)] + [w3[2], g1[rows - 1], w2, w1]

    for r in (-3, -2, -1):
        ref, base = input_at(r)
        put_input(ref, base, me, own_before[r + 3], before[r + 3])
    for r in range(rows, rows + 3):
        ref, base = input_at(r)
        put_input(ref, base, me, own_after[r - rows], after[r - rows])
    put_cotangent(tuo, 0, me, own_before[3], before[3])
    put_cotangent(tuo, stack, me, own_after[3], after[3])
    for out in (s2, s1):
        for par in range(2):
            out[par, pl.ds(0, 2 * h), :] = jnp.zeros((2 * h, m), BF)
            out[par, pl.ds((rows + 2) * h, 2 * h), :] = jnp.zeros((2 * h, m), BF)
    for k in (0, 1, rows + 2, rows + 3):
        td1[pl.ds(k * stack, stack), :] = jnp.zeros((stack, m), BF)
    run(tasks)
    deal((p0, p1, p2, p3), (dw3, dw2, dw1), core[1])


def inputs_kernel(td1, wt1, main, rims):
    h = wt1.shape[0] // 2
    stack = 8 * h
    rows = main.shape[0]
    for k in range(rows + 2):
        back = dot(wt1[...], td1[pl.ds(k * stack, 3 * stack), :])
        flat = jnp.concatenate([back[:h], back[h:]], axis=1)
        if k == 0:
            rims[0] = flat.astype(BF)
        elif k == rows + 1:
            rims[1] = flat.astype(BF)
        else:
            main[k - 1] = flat


def piece_at(tile, k):
    return lax.bitwise_xor(lax.rem(tile, 4), k)


def sum_kernel(*refs):
    total = refs[0][...].astype(F32)
    for piece in refs[1:-1]:
        total = total + piece[...].astype(F32)
    refs[-1][...] = total.astype(BF)


def last_kernel(scales, core, p0, p1, p2, p3, *outs):
    for k, piece in enumerate((p0, p1, p2, p3)):
        at = piece_at(core[1], k)
        base = 0
        for out, scale in zip(outs, scales):
            size = out.shape[0] // 4
            out[pl.ds(pl.multiple_of(at * size, 16), size), :] = piece[pl.ds(base, size), :].astype(F32) * scale
            base += size


def call(body, name, outs, scratch, limit, *args):
    vmem = pl.BlockSpec(memory_space=pltpu.VMEM)
    scalar = pl.BlockSpec(memory_space=pltpu.SMEM)
    return pl.pallas_call(
        body,
        out_shape=tuple(jax.ShapeDtypeStruct(shape, kind) for shape, kind in outs),
        in_specs=[scalar if a.dtype == jnp.int32 else vmem for a in args],
        out_specs=tuple(vmem for _ in outs),
        scratch_shapes=[pltpu.VMEM(shape, kind) for shape, kind in scratch],
        compiler_params=pltpu.CompilerParams(vmem_limit_bytes=limit * 1024 * 1024),
        cost_estimate=pl.CostEstimate(flops=10**6, bytes_accessed=10**5, transcendentals=0),
        name=name,
    )(*args)


def shards(inputs, w_first, w_second, w_third, cotangent, mirror):
    h, rows, cols = inputs.shape
    m = cols // 2
    c = 2 * h
    stack = 4 * c
    tiles = lax.axis_size("blk")
    up = [(i, (i + 1) % tiles) for i in range(tiles)]
    down = [(j, i) for i, j in up]
    core = jnp.stack([lax.axis_index("chan"), lax.axis_index("blk")]).astype(jnp.int32)

    def across(piece):
        return lax.ppermute(piece, "chan", [(0, 1), (1, 0)])

    def swapped(piece, k):
        return lax.ppermute(piece, "blk", [(i, i ^ k) for i in range(tiles)])

    def total(*parts):
        return call(sum_kernel, "sum", [(parts[0].shape, BF)], [], 8, *parts)[0]

    to = lax.broadcasted_iota(jnp.int32, (cols, cols), 1)
    place = 2 * (to % m) + to // m
    place = jnp.where(mirror[0] == 1, cols - 1 - place, place)
    split = (lax.broadcasted_iota(jnp.int32, (cols, cols), 0) == place).astype(BF)
    to = lax.broadcasted_iota(jnp.int32, (m, m), 1)
    place = jnp.where(mirror[0] == 1, m - 1 - to, to)
    turn = (lax.broadcasted_iota(jnp.int32, (m, m), 0) == place).astype(BF)

    x = jnp.einsum("irc,cn->rin", inputs, split, preferred_element_type=F32).astype(BF)
    u = jnp.einsum("orc,cn->ron", cotangent, turn, preferred_element_type=F32).astype(BF)
    u = jnp.concatenate([u[:, :h], u[:, h:]], axis=2)
    before = lax.ppermute(jnp.concatenate([x[rows - 3 :], u[rows // 2 - 1 :]]), "blk", up)
    after = lax.ppermute(jnp.concatenate([x[:3], u[:1]]), "blk", down)
    own = jnp.concatenate([x, u])
    weights = []
    for w in (w_first, w_second, w_third):
        w = w.reshape(-1, c)
        weights += [w, across(w)]
    wb1, wb2, wt2, wt1, wt3e, wt3o, tx, tu, th1, dz1, g2 = call(
        inner_kernel, "inner",
        [
            ((2 * c, 3 * stack), BF),
            ((2 * c, 3 * stack), BF),
            ((2 * c, 3 * stack), BF),
            ((c, 3 * stack), BF),
            ((2 * c, stack), BF),
            ((2 * c, 2 * stack), BF),
            ((rows * stack, m), BF),
            ((rows // 2 * stack, m), BF),
            (((rows - 2) * stack, m), BF),
            (((rows - 2) * 2 * c, m), F32),
            (((rows - 1) * 2 * c, m), F32),
        ],
        [], 24, core, own, across(own), *weights,
    )
    before, after, _ = lax.optimization_barrier((before, after, g2))

    size = 9 * (c + 2 * h) // 4
    *parts, td1 = call(
        main_kernel, "main",
        [((size, c), BF)] * 4 + [(((rows + 4) * stack, m), BF)],
        [
            ((6 * stack, m), BF),
            ((2 * stack, m), BF),
            ((6 * stack, m), BF),
            ((2 * 2 * c, m), F32),
            (((rows + 2) * 2 * c, m), F32),
            (((rows + 1) * 3 * c, m), BF),
            (((rows + 2) * stack, m), BF),
            ((2, (rows + 4) * h, m), BF),
            ((2, (rows + 4) * h, m), BF),
            ((9 * h, c), BF),
            ((9 * h, c), BF),
            ((9 * c, c), BF),
        ],
        32, core, before, across(before), after, across(after), wb1, wb2, wt2, wt3e, wt3o, tx, tu, th1, dz1, g2,
    )
    mine = total(parts[0], *[swapped(part, k) for k, part in enumerate(parts[1:], 1)])
    bit = 4
    while bit < tiles:
        if bit * 2 >= tiles:
            mine, td1 = lax.optimization_barrier((mine, td1))
        mine = total(mine, swapped(mine, bit))
        bit *= 2
    main, rims = call(
        inputs_kernel, "inputs",
        [((rows, h, cols), F32), ((2, h, cols), BF)], [], 16, td1, wt1,
    )
    from_next = lax.ppermute(rims[0], "blk", down)
    from_prev = lax.ppermute(rims[1], "blk", up)
    from_next, from_prev, _ = lax.optimization_barrier((from_next, from_prev, mine))
    from_next, from_prev = from_next.astype(F32), from_prev.astype(F32)
    main = jnp.concatenate([main[:1] + from_prev, main[1:-1], main[-1:] + from_next]).astype(BF)
    grad_inputs = jnp.einsum("rin,cn->irc", main, split, preferred_element_type=F32).astype(BF)

    cells = rows * cols * tiles
    wide, narrow = 1.0 / math.sqrt(cells // 4), 1.0 / math.sqrt(cells)
    third, second, first = call(
        functools.partial(last_kernel, (wide, narrow, narrow)), "last",
        [((9 * c, c), F32), ((9 * h, c), F32), ((9 * h, c), F32)], [], 16,
        core, mine, *[swapped(mine, k) for k in range(1, 4)],
    )
    return grad_inputs, first.reshape(3, 3, h, c), second.reshape(3, 3, h, c), third.reshape(3, 3, c, c)


def solution(mesh):
    placed = (
        P("chan", "blk", None),
        P(None, None, "chan", None),
        P(None, None, "chan", None),
        P(None, None, "chan", None),
        P("chan", "blk", None),
        P("blk"),
    )
    return jax.shard_map(
        shards,
        mesh=mesh,
        in_specs=placed,
        out_specs=(
            P("chan", "blk", None),
            P(None, None, "chan", None),
            P(None, None, "chan", None),
            P(None, None, "chan", None),
        ),
        check_vma=False,
    )
```

```python
import functools
import math

import jax
import jax.numpy as jnp
from jax import lax
from jax.experimental import pallas as pl
from jax.experimental.pallas import tpu as pltpu
from jax.sharding import PartitionSpec as P

BF = jnp.bfloat16
F32 = jnp.float32
ROOT = math.sqrt(2.0 / math.pi)
CUBIC = 0.044715
FAN = 8


def dot(a, b):
    return jnp.dot(a, b, preferred_element_type=F32)


def dot_t(a, b):
    return lax.dot_general(a, b, (((1,), (1,)), ((), ())), preferred_element_type=F32)


def moved_right(v):
    lane = lax.broadcasted_iota(jnp.int32, v.shape, 1)
    return jnp.where(lane == 0, 0.0, pltpu.roll(v, 1, 1))


def moved_left(v):
    lane = lax.broadcasted_iota(jnp.int32, v.shape, 1)
    width = v.shape[1]
    return jnp.where(lane == width - 1, 0.0, pltpu.roll(v, width - 1, 1))


def gelu_parts(v):
    square = v * v
    t = jnp.tanh(v * (ROOT + (ROOT * CUBIC) * square))
    half = 0.5 * v
    return half + half * t, 0.5 + 0.5 * t + half * (1.0 - t * t) * (ROOT + (3.0 * ROOT * CUBIC) * square)


def either(me, own, other):
    return jnp.where(me == 0, own, other), jnp.where(me == 0, other, own)


def put_weights(me, own1, other1, own2, other2, own3, other3, wb1, wb2, wt2, wt1, wt3e, wt3o):
    c = own1.shape[1]
    h = c // 2
    stack = 4 * c
    for out in (wb1, wb2, wt2, wt1, wt3e, wt3o):
        out[...] = jnp.zeros_like(out)
    for a in range(3):
        for b in range(3):
            tap = a * 3 + b
            at = pl.ds(tap * h, h)
            first = jnp.concatenate(either(me, own1[at, :], other1[at, :]), axis=0)
            second = jnp.concatenate(either(me, own2[at, :], other2[at, :]), axis=0)
            for par in range(2):
                at = pl.ds(a * stack + (b + par) * c, c)
                wb1[pl.ds(par * c, c), at] = first
                wb2[pl.ds(par * c, c), at] = second
            turned = second.T
            first_turned = first.T
            half_turned = jnp.where(me == 0, first_turned[:h], first_turned[h:])
            for par in range(2):
                at = pl.ds((2 - a) * stack + (2 - b + par) * c, c)
                wt2[pl.ds(par * c, c), at] = turned
                wt1[pl.ds(par * h, h), at] = half_turned
            at = pl.ds(tap * c, c)
            third = jnp.concatenate([w.T for w in either(me, own3[at, :], other3[at, :])], axis=1)
            par = 0 if b == 1 else 1
            side = 1 if b == 0 else 0
            if a == 1:
                wt3e[pl.ds(par * c, c), pl.ds(side * 2 * c, 2 * c)] = third
            else:
                back = 0 if a == 2 else 1
                wt3o[pl.ds(par * c, c), pl.ds((back * 2 + side) * 2 * c, 2 * c)] = third


def put_stack(ref, base, row):
    c = row.shape[0] // 2
    even, odd = row[:c], row[c:]
    ref[pl.ds(base, c), :] = moved_right(odd).astype(BF)
    ref[pl.ds(base + c, 2 * c), :] = row.astype(BF)
    ref[pl.ds(base + 3 * c, c), :] = moved_left(even).astype(BF)


def run(tasks):
    waiting = None
    for task in tasks:
        value = task[0]()
        if waiting:
            waiting[0](waiting[1])
        waiting = (task[1], value)
    waiting[0](waiting[1])


def deal(pieces, grads, tile):
    for k, piece in enumerate(pieces):
        at = piece_at(tile, k)
        base = 0
        for grad in grads:
            size = grad.shape[0] // FAN
            piece[pl.ds(base, size), :] = grad[pl.ds(pl.multiple_of(at * size, 16), size), :]
            base += size


def put_input(ref, base, me, own, other):
    m = own.shape[1] // 2
    h = own.shape[0]
    for at, row in ((me, own), (1 - me, other)):
        even, odd = row[:, :m], row[:, m:]
        blocks = (moved_right(odd.astype(F32)).astype(BF), even, odd, moved_left(even.astype(F32)).astype(BF))
        for k, block in enumerate(blocks):
            ref[pl.ds(pl.multiple_of(base + k * 2 * h + at * h, h), h), :] = block


def put_cotangent(ref, base, me, own, other):
    m = own.shape[1] // 2
    h = own.shape[0]
    for at, row in ((me, own), (1 - me, other)):
        for k in range(2):
            block = row[:, k * m : (k + 1) * m]
            to = base + at * 2 * h + k * h
            ref[pl.ds(pl.multiple_of(to, h), h), :] = block
            ref[pl.ds(pl.multiple_of(to + 4 * h, h), h), :] = moved_left(block.astype(F32)).astype(BF)


def inner_kernel(
    core, own, other, w1, other1, w2, other2, w3, other3,
    wb1, wb2, wt2, wt1, wt3e, wt3o, tx, tu, th1, dz1, g2,
):
    me = core[0]
    c = wb1.shape[0] // 2
    stack = 4 * c
    rows = own.shape[0] // 3 * 2
    put_weights(me, w1, other1, w2, other2, w3, other3, wb1, wb2, wt2, wt1, wt3e, wt3o)
    for r in range(rows):
        put_input(tx, r * stack, me, own[r], other[r])
    for r in range(rows // 2):
        put_cotangent(tu, r * stack, me, own[rows + r], other[rows + r])

    def first_dot(r):
        return dot(wb1[...], tx[pl.ds((r - 1) * stack, 3 * stack), :])

    def first_use(r, z):
        act, slope = gelu_parts(z)
        put_stack(th1, (r - 1) * stack, act)
        dz1[pl.ds((r - 1) * 2 * c, 2 * c), :] = slope

    def third_dot(r):
        if r % 2 == 0:
            return dot(wt3e[...], tu[pl.ds(r // 2 * stack, stack), :])
        return dot(wt3o[...], tu[pl.ds(r // 2 * stack, 2 * stack), :])

    def third_use(r, back):
        g2[pl.ds(r * 2 * c, 2 * c), :] = back

    z1 = [(functools.partial(first_dot, r), functools.partial(first_use, r)) for r in range(1, rows - 1)]
    back = [(functools.partial(third_dot, r), functools.partial(third_use, r)) for r in range(rows - 1)]
    run(z1 + back)


def main_kernel(
    core, own_before, before, own_after, after, wb1, wb2, wt2, wt3e, wt3o, txi, tui, th1i, dz1i, g2i,
    *rest,
):
    pieces, (td1, txo, tuo, th1o, dz1o, dz2, th2, td2, s2, s1, dw21, dw3) = rest[:FAN], rest[FAN:]
    me = core[0]
    c = wb1.shape[0] // 2
    h = c // 2
    m = td1.shape[1]
    stack = 4 * c
    rows = td1.shape[0] // stack - 4

    def input_at(r):
        if 0 <= r < rows:
            return txi, r * stack
        return txo, (r + 3 if r < 0 else r - rows + 3) * stack

    def first_at(r):
        if 1 <= r < rows - 1:
            return th1i, (r - 1) * stack
        return th1o, (r + 2 if r < 1 else r - rows + 4) * stack

    def cotangent_at(r):
        if 0 <= r < rows // 2:
            return tui, r * stack
        return tuo, 0 if r < 0 else stack

    def window(at, first, count):
        places = [at(r) for r in range(first, first + count)]
        return jnp.concatenate([ref[pl.ds(base, stack), :] for ref, base in places], axis=0)

    def own_channels(ref, index, out, r):
        for par in range(2):
            at = pl.multiple_of(index * stack + (1 + par) * c + me * h, h)
            out[par, pl.ds((rows + 1 - r) * h, h), :] = ref[pl.ds(at, h), :]

    def first_dot(r):
        return dot(wb1[...], window(input_at, r - 1, 3))

    def first_use(r, z):
        act, slope = gelu_parts(z)
        ref, base = first_at(r)
        put_stack(ref, base, act)
        if r in (0, rows - 1):
            dz1o[pl.ds((r > 0) * 2 * c, 2 * c), :] = slope

    def second_dot(r):
        return dot(wb2[...], window(first_at, r - 1, 3))

    def second_use(r, z):
        act, slope = gelu_parts(z)
        k = r + 1
        dz2[pl.ds(k * 2 * c, 2 * c), :] = slope
        if r < rows:
            th2[pl.ds(k * 3 * c, c), :] = moved_right(act[c:]).astype(BF)
            th2[pl.ds(k * 3 * c + c, 2 * c), :] = act.astype(BF)

    def third_dot(r):
        if 0 <= r < rows - 1:
            return None
        if r % 2 == 0:
            return dot(wt3e[...], window(cotangent_at, r // 2, 1))
        return dot(wt3o[...], window(cotangent_at, (r - 1) // 2 if r > 0 else -1, 2))

    def third_use(r, back):
        if back is None:
            back = g2i[pl.ds(r * 2 * c, 2 * c), :]
        k = r + 1
        put_stack(td2, k * stack, back * dz2[pl.ds(k * 2 * c, 2 * c), :])
        if 0 <= r < rows:
            own_channels(td2, k, s2, r)

    def back_dot(r):
        return dot(wt2[...], td2[pl.ds(r * stack, 3 * stack), :])

    def back_use(r, back):
        if 0 < r < rows - 1:
            slope = dz1i[pl.ds((r - 1) * 2 * c, 2 * c), :]
        else:
            slope = dz1o[pl.ds((r > 0) * 2 * c, 2 * c), :]
        put_stack(td1, (r + 2) * stack, back * slope)
        own_channels(td1, r + 2, s1, r)

    def third_grad(a):
        total = jnp.zeros((c, 3 * c), F32)
        for r in range(rows // 2):
            mine = tui[pl.ds(pl.multiple_of(r * stack + me * c, c), c), :]
            total = total + dot_t(mine, th2[pl.ds((2 * r + a) * 3 * c, 3 * c), :])
        return total

    def third_grad_use(a, total):
        for b in range(3):
            dw3[pl.ds((a * 3 + b) * c, c), :] = total[:, b * c : (b + 1) * c].astype(BF)

    def kernel_grad(deltas, at):
        total = jnp.zeros((3 * h, 3 * c), F32)
        for q in range(rows + 2):
            ref, base = at(q - 1)
            for par in range(2):
                mine = deltas[par, pl.ds((rows + 1 - q) * h, 3 * h), :]
                total = total + dot_t(mine, ref[pl.ds(base + par * c, 3 * c), :])
        return total

    def kernel_grad_use(base, total):
        for a in range(3):
            for b in range(3):
                dw21[pl.ds(base + (a * 3 + b) * h, h), :] = total[a * h : (a + 1) * h, b * c : (b + 1) * c].astype(BF)

    def task(does, uses, r):
        return functools.partial(does, r), functools.partial(uses, r)

    z1 = {r: task(first_dot, first_use, r) for r in range(-2, rows + 2)}
    z2 = {r: task(second_dot, second_use, r) for r in range(-1, rows + 1)}
    g2 = {r: task(third_dot, third_use, r) for r in range(-1, rows + 1)}
    g1 = {r: task(back_dot, back_use, r) for r in range(rows)}
    w3 = {a: task(third_grad, third_grad_use, a) for a in range(3)}
    w2 = (lambda: kernel_grad(s2, first_at), functools.partial(kernel_grad_use, 0))
    w1 = (lambda: kernel_grad(s1, input_at), functools.partial(kernel_grad_use, 9 * h))
    tasks = [z1[-2], z1[-1], z1[0], z1[rows - 1], z2[-1], z1[rows], z2[0], z1[rows + 1]]
    tasks += [z2[r] for r in range(1, rows)] + [g2[-1], z2[rows]] + [g2[r] for r in range(rows)]
    tasks += [w3[0], g1[0], g2[rows], w3[1]] + [g1[r] for r in range(1, rows - 1)] + [w3[2], g1[rows - 1], w2, w1]

    for r in (-3, -2, -1):
        ref, base = input_at(r)
        put_input(ref, base, me, own_before[r + 3], before[r + 3])
    for r in range(rows, rows + 3):
        ref, base = input_at(r)
        put_input(ref, base, me, own_after[r - rows], after[r - rows])
    put_cotangent(tuo, 0, me, own_before[3], before[3])
    put_cotangent(tuo, stack, me, own_after[3], after[3])
    for out in (s2, s1):
        for par in range(2):
            out[par, pl.ds(0, 2 * h), :] = jnp.zeros((2 * h, m), BF)
            out[par, pl.ds((rows + 2) * h, 2 * h), :] = jnp.zeros((2 * h, m), BF)
    for k in (0, 1, rows + 2, rows + 3):
        td1[pl.ds(k * stack, stack), :] = jnp.zeros((stack, m), BF)
    run(tasks)
    deal(pieces, (dw3, dw21), core[1])


def inputs_kernel(td1, wt1, main, rims):
    h = wt1.shape[0] // 2
    stack = 8 * h
    rows = main.shape[0]
    for k in range(rows + 2):
        back = dot(wt1[...], td1[pl.ds(k * stack, 3 * stack), :])
        flat = jnp.concatenate([back[:h], back[h:]], axis=1)
        if k == 0:
            rims[0] = flat.astype(BF)
        elif k == rows + 1:
            rims[1] = flat.astype(BF)
        else:
            main[k - 1] = flat


def piece_at(tile, k):
    return lax.bitwise_xor(lax.rem(tile, FAN), k)


def sum_kernel(*refs):
    total = refs[0][...].astype(F32)
    for piece in refs[1:-1]:
        total = total + piece[...].astype(F32)
    refs[-1][...] = total.astype(BF)


def last_kernel(scales, core, *rest):
    pieces, (third, second, first, both) = rest[:FAN], rest[FAN:]
    for k, piece in enumerate(pieces):
        at = piece_at(core[1], k)
        size = piece.shape[0] // 2
        at = pl.ds(pl.multiple_of(at * size, 16), size)
        third[at, :] = piece[pl.ds(0, size), :].astype(F32) * scales[0]
        both[at, :] = piece[pl.ds(size, size), :].astype(F32) * scales[1]
    n = second.shape[0]
    second[...] = both[pl.ds(0, n), :]
    first[...] = both[pl.ds(n, n), :]


def call(body, name, outs, scratch, limit, *args):
    vmem = pl.BlockSpec(memory_space=pltpu.VMEM)
    scalar = pl.BlockSpec(memory_space=pltpu.SMEM)
    return pl.pallas_call(
        body,
        out_shape=tuple(jax.ShapeDtypeStruct(shape, kind) for shape, kind in outs),
        in_specs=[scalar if a.dtype == jnp.int32 else vmem for a in args],
        out_specs=tuple(vmem for _ in outs),
        scratch_shapes=[pltpu.VMEM(shape, kind) for shape, kind in scratch],
        compiler_params=pltpu.CompilerParams(vmem_limit_bytes=limit * 1024 * 1024),
        cost_estimate=pl.CostEstimate(flops=10**6, bytes_accessed=10**5, transcendentals=0),
        name=name,
    )(*args)


def shards(inputs, w_first, w_second, w_third, cotangent, mirror):
    h, rows, cols = inputs.shape
    m = cols // 2
    c = 2 * h
    stack = 4 * c
    tiles = lax.axis_size("blk")
    up = [(i, (i + 1) % tiles) for i in range(tiles)]
    down = [(j, i) for i, j in up]
    core = jnp.stack([lax.axis_index("chan"), lax.axis_index("blk")]).astype(jnp.int32)

    def across(piece):
        return lax.ppermute(piece, "chan", [(0, 1), (1, 0)])

    def swapped(piece, k):
        return lax.ppermute(piece, "blk", [(i, i ^ k) for i in range(tiles)])

    def total(*parts):
        return call(sum_kernel, "sum", [(parts[0].shape, BF)], [], 8, *parts)[0]

    to = lax.broadcasted_iota(jnp.int32, (cols, cols), 1)
    place = 2 * (to % m) + to // m
    place = jnp.where(mirror[0] == 1, cols - 1 - place, place)
    split = (lax.broadcasted_iota(jnp.int32, (cols, cols), 0) == place).astype(BF)
    to = lax.broadcasted_iota(jnp.int32, (m, m), 1)
    place = jnp.where(mirror[0] == 1, m - 1 - to, to)
    turn = (lax.broadcasted_iota(jnp.int32, (m, m), 0) == place).astype(BF)

    x = jnp.einsum("irc,cn->rin", inputs, split, preferred_element_type=F32).astype(BF)
    u = jnp.einsum("orc,cn->ron", cotangent, turn, preferred_element_type=F32).astype(BF)
    u = jnp.concatenate([u[:, :h], u[:, h:]], axis=2)
    before = lax.ppermute(jnp.concatenate([x[rows - 3 :], u[rows // 2 - 1 :]]), "blk", up)
    after = lax.ppermute(jnp.concatenate([x[:3], u[:1]]), "blk", down)
    own = jnp.concatenate([x, u])
    weights = []
    for w in (w_first, w_second, w_third):
        w = w.reshape(-1, c)
        weights += [w, across(w)]
    wb1, wb2, wt2, wt1, wt3e, wt3o, tx, tu, th1, dz1, g2 = call(
        inner_kernel, "inner",
        [
            ((2 * c, 3 * stack), BF),
            ((2 * c, 3 * stack), BF),
            ((2 * c, 3 * stack), BF),
            ((c, 3 * stack), BF),
            ((2 * c, stack), BF),
            ((2 * c, 2 * stack), BF),
            ((rows * stack, m), BF),
            ((rows // 2 * stack, m), BF),
            (((rows - 2) * stack, m), BF),
            (((rows - 2) * 2 * c, m), F32),
            (((rows - 1) * 2 * c, m), F32),
        ],
        [], 24, core, own, across(own), *weights,
    )
    before, _ = lax.optimization_barrier((before, g2))
    other_before = across(before)
    after, _, _ = lax.optimization_barrier((after, before, g2))

    size = 9 * (c + 2 * h) // FAN
    *parts, td1 = call(
        main_kernel, "main",
        [((size, c), BF)] * FAN + [(((rows + 4) * stack, m), BF)],
        [
            ((6 * stack, m), BF),
            ((2 * stack, m), BF),
            ((6 * stack, m), BF),
            ((2 * 2 * c, m), F32),
            (((rows + 2) * 2 * c, m), F32),
            (((rows + 1) * 3 * c, m), BF),
            (((rows + 2) * stack, m), BF),
            ((2, (rows + 4) * h, m), BF),
            ((2, (rows + 4) * h, m), BF),
            ((9 * c, c), BF),
            ((9 * c, c), BF),
        ],
        32, core, before, other_before, after, across(after), wb1, wb2, wt2, wt3e, wt3o, tx, tu, th1, dz1, g2,
    )
    mine = total(parts[0], *[swapped(part, k) for k, part in enumerate(parts[1:], 1)])
    bit = FAN
    while bit < tiles:
        if bit * 2 >= tiles:
            mine, td1 = lax.optimization_barrier((mine, td1))
        mine = total(mine, swapped(mine, bit))
        bit *= 2
    main, rims = call(
        inputs_kernel, "inputs",
        [((rows, h, cols), F32), ((2, h, cols), BF)], [], 16, td1, wt1,
    )
    from_next = lax.ppermute(rims[0], "blk", down)
    from_prev = lax.ppermute(rims[1], "blk", up)
    from_next, from_prev, _ = lax.optimization_barrier((from_next, from_prev, mine))
    from_next, from_prev = from_next.astype(F32), from_prev.astype(F32)
    main = jnp.concatenate([main[:1] + from_prev, main[1:-1], main[-1:] + from_next]).astype(BF)
    grad_inputs = jnp.einsum("rin,cn->irc", main, split, preferred_element_type=F32).astype(BF)

    cells = rows * cols * tiles
    scales = (1.0 / math.sqrt(cells // 4), 1.0 / math.sqrt(cells))
    third, second, first = call(
        functools.partial(last_kernel, scales), "last",
        [((9 * c, c), F32), ((9 * h, c), F32), ((9 * h, c), F32)], [((9 * c, c), F32)], 16,
        core, mine, *[swapped(mine, k) for k in range(1, FAN)],
    )
    return grad_inputs, first.reshape(3, 3, h, c), second.reshape(3, 3, h, c), third.reshape(3, 3, c, c)


def solution(mesh):
    placed = (
        P("chan", "blk", None),
        P(None, None, "chan", None),
        P(None, None, "chan", None),
        P(None, None, "chan", None),
        P("chan", "blk", None),
        P("blk"),
    )
    return jax.shard_map(
        shards,
        mesh=mesh,
        in_specs=placed,
        out_specs=(
            P("chan", "blk", None),
            P(None, None, "chan", None),
            P(None, None, "chan", None),
            P(None, None, "chan", None),
        ),
        check_vma=False,
    )
```

```python
import functools
import math

import jax
import jax.numpy as jnp
from jax import lax
from jax.experimental import pallas as pl
from jax.experimental.pallas import tpu as pltpu
from jax.sharding import PartitionSpec as P

BF = jnp.bfloat16
F32 = jnp.float32
ROOT = math.sqrt(2.0 / math.pi)
CUBIC = 0.044715


def dot(a, b):
    return jnp.dot(a, b, preferred_element_type=F32)


def dot_t(a, b):
    return lax.dot_general(a, b, (((1,), (1,)), ((), ())), preferred_element_type=F32)


def moved_right(v):
    lane = lax.broadcasted_iota(jnp.int32, v.shape, 1)
    return jnp.where(lane == 0, 0.0, pltpu.roll(v, 1, 1))


def moved_left(v):
    lane = lax.broadcasted_iota(jnp.int32, v.shape, 1)
    width = v.shape[1]
    return jnp.where(lane == width - 1, 0.0, pltpu.roll(v, width - 1, 1))


def gelu_parts(v):
    square = v * v
    t = jnp.tanh(v * (ROOT + (ROOT * CUBIC) * square))
    half = 0.5 * v
    return half + half * t, 0.5 + 0.5 * t + half * (1.0 - t * t) * (ROOT + (3.0 * ROOT * CUBIC) * square)


def either(me, own, other):
    return jnp.where(me == 0, own, other), jnp.where(me == 0, other, own)


def put_weights(me, own1, other1, own2, other2, own3, other3, wb1, wb2, wt2, wt1, wt3e, wt3o):
    c = own1.shape[1]
    h = c // 2
    stack = 4 * c
    for out in (wb1, wb2, wt2, wt1, wt3e, wt3o):
        out[...] = jnp.zeros_like(out)
    for a in range(3):
        for b in range(3):
            tap = a * 3 + b
            at = pl.ds(tap * h, h)
            first = jnp.concatenate(either(me, own1[at, :], other1[at, :]), axis=0)
            second = jnp.concatenate(either(me, own2[at, :], other2[at, :]), axis=0)
            for par in range(2):
                at = pl.ds(a * stack + (b + par) * c, c)
                wb1[pl.ds(par * c, c), at] = first
                wb2[pl.ds(par * c, c), at] = second
            turned = second.T
            first_turned = first.T
            half_turned = jnp.where(me == 0, first_turned[:h], first_turned[h:])
            for par in range(2):
                at = pl.ds((2 - a) * stack + (2 - b + par) * c, c)
                wt2[pl.ds(par * c, c), at] = turned
                wt1[pl.ds(par * h, h), at] = half_turned
            at = pl.ds(tap * c, c)
            third = jnp.concatenate([w.T for w in either(me, own3[at, :], other3[at, :])], axis=1)
            par = 0 if b == 1 else 1
            side = 1 if b == 0 else 0
            if a == 1:
                wt3e[pl.ds(par * c, c), pl.ds(side * 2 * c, 2 * c)] = third
            else:
                back = 0 if a == 2 else 1
                wt3o[pl.ds(par * c, c), pl.ds((back * 2 + side) * 2 * c, 2 * c)] = third


def put_stack(ref, base, row):
    c = row.shape[0] // 2
    even, odd = row[:c], row[c:]
    ref[pl.ds(base, c), :] = moved_right(odd).astype(BF)
    ref[pl.ds(base + c, 2 * c), :] = row.astype(BF)
    ref[pl.ds(base + 3 * c, c), :] = moved_left(even).astype(BF)


def run(tasks):
    waiting = None
    for task in tasks:
        value = task[0]()
        if waiting:
            waiting[0](waiting[1])
        waiting = (task[1], value)
    waiting[0](waiting[1])


def deal(pieces, grads, tile):
    for k, piece in enumerate(pieces):
        at = piece_at(tile, k)
        base = 0
        for grad in grads:
            size = grad.shape[0] // 4
            piece[pl.ds(base, size), :] = grad[pl.ds(pl.multiple_of(at * size, 16), size), :]
            base += size


def put_input(ref, base, me, own, other):
    m = own.shape[1] // 2
    h = own.shape[0]
    for at, row in ((me, own), (1 - me, other)):
        even, odd = row[:, :m], row[:, m:]
        blocks = (moved_right(odd.astype(F32)).astype(BF), even, odd, moved_left(even.astype(F32)).astype(BF))
        for k, block in enumerate(blocks):
            ref[pl.ds(pl.multiple_of(base + k * 2 * h + at * h, h), h), :] = block


def put_cotangent(ref, base, me, own, other):
    m = own.shape[1] // 2
    h = own.shape[0]
    for at, row in ((me, own), (1 - me, other)):
        for k in range(2):
            block = row[:, k * m : (k + 1) * m]
            to = base + at * 2 * h + k * h
            ref[pl.ds(pl.multiple_of(to, h), h), :] = block
            ref[pl.ds(pl.multiple_of(to + 4 * h, h), h), :] = moved_left(block.astype(F32)).astype(BF)


def inner_kernel(
    core, own, other, w1, other1, w2, other2, w3, other3,
    wb1, wb2, wt2, wt1, wt3e, wt3o, tx, tu, th1, dz1, g2,
):
    me = core[0]
    c = wb1.shape[0] // 2
    stack = 4 * c
    rows = own.shape[0] // 3 * 2
    put_weights(me, w1, other1, w2, other2, w3, other3, wb1, wb2, wt2, wt1, wt3e, wt3o)
    for r in range(rows):
        put_input(tx, r * stack, me, own[r], other[r])
    for r in range(rows // 2):
        put_cotangent(tu, r * stack, me, own[rows + r], other[rows + r])

    def first_dot(r):
        return dot(wb1[...], tx[pl.ds((r - 1) * stack, 3 * stack), :])

    def first_use(r, z):
        act, slope = gelu_parts(z)
        put_stack(th1, (r - 1) * stack, act)
        dz1[pl.ds((r - 1) * 2 * c, 2 * c), :] = slope

    def third_dot(r):
        if r % 2 == 0:
            return dot(wt3e[...], tu[pl.ds(r // 2 * stack, stack), :])
        return dot(wt3o[...], tu[pl.ds(r // 2 * stack, 2 * stack), :])

    def third_use(r, back):
        g2[pl.ds(r * 2 * c, 2 * c), :] = back

    z1 = [(functools.partial(first_dot, r), functools.partial(first_use, r)) for r in range(1, rows - 1)]
    back = [(functools.partial(third_dot, r), functools.partial(third_use, r)) for r in range(rows - 1)]
    run(z1 + back)


def main_kernel(
    core, own, other, wb1, wb2, wt2, wt3e, wt3o, txi, tui, th1i, dz1i, g2i,
    p0, p1, p2, p3, td1, txo, tuo, th1o, dz1o, dz2, th2, td2, s2, s1, dw1, dw2, dw3,
):
    me = core[0]
    c = wb1.shape[0] // 2
    h = c // 2
    m = td1.shape[1]
    stack = 4 * c
    rows = td1.shape[0] // stack - 4

    def input_at(r):
        if 0 <= r < rows:
            return txi, r * stack
        return txo, (r + 3 if r < 0 else r - rows + 3) * stack

    def first_at(r):
        if 1 <= r < rows - 1:
            return th1i, (r - 1) * stack
        return th1o, (r + 2 if r < 1 else r - rows + 4) * stack

    def cotangent_at(r):
        if 0 <= r < rows // 2:
            return tui, r * stack
        return tuo, 0 if r < 0 else stack

    def window(at, first, count):
        places = [at(r) for r in range(first, first + count)]
        return jnp.concatenate([ref[pl.ds(base, stack), :] for ref, base in places], axis=0)

    def own_channels(ref, index, out, r):
        for par in range(2):
            at = pl.multiple_of(index * stack + (1 + par) * c + me * h, h)
            out[par, pl.ds((rows + 1 - r) * h, h), :] = ref[pl.ds(at, h), :]

    def first_dot(r):
        return dot(wb1[...], window(input_at, r - 1, 3))

    def first_use(r, z):
        act, slope = gelu_parts(z)
        ref, base = first_at(r)
        put_stack(ref, base, act)
        if r <= 0:
            ref, base = input_at(rows + r + 2)
            put_input(ref, base, me, own[r + 6], other[r + 6])
        if r in (0, rows - 1):
            dz1o[pl.ds((r > 0) * 2 * c, 2 * c), :] = slope

    def second_dot(r):
        return dot(wb2[...], window(first_at, r - 1, 3))

    def second_use(r, z):
        act, slope = gelu_parts(z)
        k = r + 1
        dz2[pl.ds(k * 2 * c, 2 * c), :] = slope
        if r == -1:
            put_cotangent(tuo, 0, me, own[3], other[3])
        if r == 0:
            put_cotangent(tuo, stack, me, own[7], other[7])
        if r < rows:
            th2[pl.ds(k * 3 * c, c), :] = moved_right(act[c:]).astype(BF)
            th2[pl.ds(k * 3 * c + c, 2 * c), :] = act.astype(BF)

    def third_dot(r):
        if 0 <= r < rows - 1:
            return None
        if r % 2 == 0:
            return dot(wt3e[...], window(cotangent_at, r // 2, 1))
        return dot(wt3o[...], window(cotangent_at, (r - 1) // 2 if r > 0 else -1, 2))

    def third_use(r, back):
        if back is None:
            back = g2i[pl.ds(r * 2 * c, 2 * c), :]
        k = r + 1
        put_stack(td2, k * stack, back * dz2[pl.ds(k * 2 * c, 2 * c), :])
        if 0 <= r < rows:
            own_channels(td2, k, s2, r)

    def back_dot(r):
        return dot(wt2[...], td2[pl.ds(r * stack, 3 * stack), :])

    def back_use(r, back):
        if 0 < r < rows - 1:
            slope = dz1i[pl.ds((r - 1) * 2 * c, 2 * c), :]
        else:
            slope = dz1o[pl.ds((r > 0) * 2 * c, 2 * c), :]
        put_stack(td1, (r + 2) * stack, back * slope)
        own_channels(td1, r + 2, s1, r)

    def third_grad(a):
        total = jnp.zeros((c, 3 * c), F32)
        for r in range(rows // 2):
            mine = tui[pl.ds(pl.multiple_of(r * stack + me * c, c), c), :]
            total = total + dot_t(mine, th2[pl.ds((2 * r + a) * 3 * c, 3 * c), :])
        return total

    def third_grad_use(a, total):
        for b in range(3):
            dw3[pl.ds((a * 3 + b) * c, c), :] = total[:, b * c : (b + 1) * c].astype(BF)

    def kernel_grad(deltas, at):
        total = jnp.zeros((3 * h, 3 * c), F32)
        for q in range(rows + 2):
            ref, base = at(q - 1)
            for par in range(2):
                mine = deltas[par, pl.ds((rows + 1 - q) * h, 3 * h), :]
                total = total + dot_t(mine, ref[pl.ds(base + par * c, 3 * c), :])
        return total

    def kernel_grad_use(out, total):
        for a in range(3):
            for b in range(3):
                out[pl.ds((a * 3 + b) * h, h), :] = total[a * h : (a + 1) * h, b * c : (b + 1) * c].astype(BF)

    def task(does, uses, r):
        return functools.partial(does, r), functools.partial(uses, r)

    z1 = {r: task(first_dot, first_use, r) for r in range(-2, rows + 2)}
    z2 = {r: task(second_dot, second_use, r) for r in range(-1, rows + 1)}
    g2 = {r: task(third_dot, third_use, r) for r in range(-1, rows + 1)}
    g1 = {r: task(back_dot, back_use, r) for r in range(rows)}
    w3 = {a: task(third_grad, third_grad_use, a) for a in range(3)}
    w2 = (lambda: kernel_grad(s2, first_at), functools.partial(kernel_grad_use, dw2))
    w1 = (lambda: kernel_grad(s1, input_at), functools.partial(kernel_grad_use, dw1))
    tasks = [z1[-2], z1[-1], z1[0], z1[rows - 1], z2[-1], z1[rows], z2[0], z1[rows + 1]]
    tasks += [z2[r] for r in range(1, rows)] + [g2[-1], z2[rows]] + [g2[r] for r in range(rows)]
    tasks += [w3[0], g1[0], g2[rows], w3[1]] + [g1[r] for r in range(1, rows - 1)] + [w3[2], g1[rows - 1], w2, w1]

    for r in (-3, -2, -1):
        ref, base = input_at(r)
        put_input(ref, base, me, own[r + 3], other[r + 3])
    for out in (s2, s1):
        for par in range(2):
            out[par, pl.ds(0, 2 * h), :] = jnp.zeros((2 * h, m), BF)
            out[par, pl.ds((rows + 2) * h, 2 * h), :] = jnp.zeros((2 * h, m), BF)
    for k in (0, 1, rows + 2, rows + 3):
        td1[pl.ds(k * stack, stack), :] = jnp.zeros((stack, m), BF)
    run(tasks)
    deal((p0, p1, p2, p3), (dw3, dw2, dw1), core[1])


def inputs_kernel(td1, wt1, main, rims):
    h = wt1.shape[0] // 2
    stack = 8 * h
    rows = main.shape[0]
    for k in range(rows + 2):
        back = dot(wt1[...], td1[pl.ds(k * stack, 3 * stack), :])
        flat = jnp.concatenate([back[:h], back[h:]], axis=1)
        if k == 0:
            rims[0] = flat.astype(BF)
        elif k == rows + 1:
            rims[1] = flat.astype(BF)
        else:
            main[k - 1] = flat


def piece_at(tile, k):
    return lax.bitwise_xor(lax.rem(tile, 4), k)


def sum_kernel(*refs):
    total = refs[0][...].astype(F32)
    for piece in refs[1:-1]:
        total = total + piece[...].astype(F32)
    refs[-1][...] = total.astype(BF)


def last_kernel(scales, core, p0, p1, p2, p3, third, second, first, wide, narrow, sems):
    copies = []
    for k, piece in enumerate((p0, p1, p2, p3)):
        at = piece_at(core[1], k)
        base = 0
        for j, (out, held, scale) in enumerate(zip((third, second, first), (wide, narrow, narrow), scales)):
            size = out.shape[0] // 4
            here = held.at[pl.ds((k if j < 2 else 4 + k) * size, size)]
            here[...] = piece[pl.ds(base, size), :].astype(F32) * scale
            there = out.at[pl.ds(pl.multiple_of(at * size, 16), size)]
            copies.append(pltpu.make_async_copy(here, there, sems.at[k, j]))
            copies[-1].start()
            base += size
    for copy in copies:
        copy.wait()


def call(body, name, outs, scratch, limit, *args, far=False):
    vmem = pl.BlockSpec(memory_space=pltpu.VMEM)
    to = pl.BlockSpec(memory_space=pl.ANY) if far else vmem
    scalar = pl.BlockSpec(memory_space=pltpu.SMEM)
    return pl.pallas_call(
        body,
        out_shape=tuple(jax.ShapeDtypeStruct(shape, kind) for shape, kind in outs),
        in_specs=[scalar if a.dtype == jnp.int32 else vmem for a in args],
        out_specs=tuple(to for _ in outs),
        scratch_shapes=[pltpu.VMEM(*some) if isinstance(some, tuple) else some for some in scratch],
        compiler_params=pltpu.CompilerParams(vmem_limit_bytes=limit * 1024 * 1024),
        cost_estimate=pl.CostEstimate(flops=10**6, bytes_accessed=10**5, transcendentals=0),
        name=name,
    )(*args)


def shards(inputs, w_first, w_second, w_third, cotangent, mirror):
    h, rows, cols = inputs.shape
    m = cols // 2
    c = 2 * h
    stack = 4 * c
    tiles = lax.axis_size("blk")
    up = [(i, (i + 1) % tiles) for i in range(tiles)]
    down = [(j, i) for i, j in up]
    core = jnp.stack([lax.axis_index("chan"), lax.axis_index("blk")]).astype(jnp.int32)

    def across(piece):
        return lax.ppermute(piece, "chan", [(0, 1), (1, 0)])

    def swapped(piece, k):
        return lax.ppermute(piece, "blk", [(i, i ^ k) for i in range(tiles)])

    def total(*parts):
        return call(sum_kernel, "sum", [(parts[0].shape, BF)], [], 8, *parts)[0]

    to = lax.broadcasted_iota(jnp.int32, (cols, cols), 1)
    place = 2 * (to % m) + to // m
    place = jnp.where(mirror[0] == 1, cols - 1 - place, place)
    split = (lax.broadcasted_iota(jnp.int32, (cols, cols), 0) == place).astype(BF)
    to = lax.broadcasted_iota(jnp.int32, (m, m), 1)
    place = jnp.where(mirror[0] == 1, m - 1 - to, to)
    turn = (lax.broadcasted_iota(jnp.int32, (m, m), 0) == place).astype(BF)

    x = jnp.einsum("irc,cn->rin", inputs, split, preferred_element_type=F32).astype(BF)
    u = jnp.einsum("orc,cn->ron", cotangent, turn, preferred_element_type=F32).astype(BF)
    u = jnp.concatenate([u[:, :h], u[:, h:]], axis=2)
    before = lax.ppermute(jnp.concatenate([x[rows - 3 :], u[rows // 2 - 1 :]]), "blk", up)
    after = lax.ppermute(jnp.concatenate([x[:3], u[:1]]), "blk", down)
    own = jnp.concatenate([x, u])
    weights = []
    for w in (w_first, w_second, w_third):
        w = w.reshape(-1, c)
        weights += [w, across(w)]
    wb1, wb2, wt2, wt1, wt3e, wt3o, tx, tu, th1, dz1, g2 = call(
        inner_kernel, "inner",
        [
            ((2 * c, 3 * stack), BF),
            ((2 * c, 3 * stack), BF),
            ((2 * c, 3 * stack), BF),
            ((c, 3 * stack), BF),
            ((2 * c, stack), BF),
            ((2 * c, 2 * stack), BF),
            ((rows * stack, m), BF),
            ((rows // 2 * stack, m), BF),
            (((rows - 2) * stack, m), BF),
            (((rows - 2) * 2 * c, m), F32),
            (((rows - 1) * 2 * c, m), F32),
        ],
        [], 24, core, own, across(own), *weights,
    )
    before, after, _ = lax.optimization_barrier((before, after, g2))
    around = jnp.concatenate([before, after])

    size = 9 * (c + 2 * h) // 4
    *parts, td1 = call(
        main_kernel, "main",
        [((size, c), BF)] * 4 + [(((rows + 4) * stack, m), BF)],
        [
            ((6 * stack, m), BF),
            ((2 * stack, m), BF),
            ((6 * stack, m), BF),
            ((2 * 2 * c, m), F32),
            (((rows + 2) * 2 * c, m), F32),
            (((rows + 1) * 3 * c, m), BF),
            (((rows + 2) * stack, m), BF),
            ((2, (rows + 4) * h, m), BF),
            ((2, (rows + 4) * h, m), BF),
            ((9 * h, c), BF),
            ((9 * h, c), BF),
            ((9 * c, c), BF),
        ],
        32, core, around, across(around), wb1, wb2, wt2, wt3e, wt3o, tx, tu, th1, dz1, g2,
    )
    mine = total(parts[0], *[swapped(parts[k], k) for k in (3, 1, 2)])
    bit = 4
    while bit < tiles:
        if bit * 2 >= tiles:
            mine, td1 = lax.optimization_barrier((mine, td1))
        mine = total(mine, swapped(mine, bit))
        bit *= 2
    main, rims = call(
        inputs_kernel, "inputs",
        [((rows, h, cols), F32), ((2, h, cols), BF)], [], 16, td1, wt1,
    )
    from_next = lax.ppermute(rims[0], "blk", down)
    from_prev = lax.ppermute(rims[1], "blk", up)
    from_next, from_prev, _ = lax.optimization_barrier((from_next, from_prev, mine))
    from_next, from_prev = from_next.astype(F32), from_prev.astype(F32)
    main = jnp.concatenate([main[:1] + from_prev, main[1:-1], main[-1:] + from_next]).astype(BF)
    grad_inputs = jnp.einsum("rin,cn->irc", main, split, preferred_element_type=F32).astype(BF)

    cells = rows * cols * tiles
    wide, narrow = 1.0 / math.sqrt(cells // 4), 1.0 / math.sqrt(cells)
    third, second, first = call(
        functools.partial(last_kernel, (wide, narrow, narrow)), "last",
        [((9 * c, c), F32), ((9 * h, c), F32), ((9 * h, c), F32)],
        [((9 * c, c), F32), ((18 * h, c), F32), pltpu.SemaphoreType.DMA((4, 3))],
        16, core, mine, *[swapped(mine, k) for k in range(1, 4)], far=True,
    )
    return grad_inputs, first.reshape(3, 3, h, c), second.reshape(3, 3, h, c), third.reshape(3, 3, c, c)


def solution(mesh):
    placed = (
        P("chan", "blk", None),
        P(None, None, "chan", None),
        P(None, None, "chan", None),
        P(None, None, "chan", None),
        P("chan", "blk", None),
        P("blk"),
    )
    return jax.shard_map(
        shards,
        mesh=mesh,
        in_specs=placed,
        out_specs=(
            P("chan", "blk", None),
            P(None, None, "chan", None),
            P(None, None, "chan", None),
            P(None, None, "chan", None),
        ),
        check_vma=False,
    )
```

```python
import functools
import math

import jax
import jax.numpy as jnp
from jax import lax
from jax.experimental import pallas as pl
from jax.experimental.pallas import tpu as pltpu
from jax.sharding import PartitionSpec as P

BF = jnp.bfloat16
F32 = jnp.float32
ROOT = math.sqrt(2.0 / math.pi)
CUBIC = 0.044715


def dot(a, b):
    return jnp.dot(a, b, preferred_element_type=F32)


def dot_t(a, b):
    return lax.dot_general(a, b, (((1,), (1,)), ((), ())), preferred_element_type=F32)


def moved_right(v):
    lane = lax.broadcasted_iota(jnp.int32, v.shape, 1)
    return jnp.where(lane == 0, 0.0, pltpu.roll(v, 1, 1))


def moved_left(v):
    lane = lax.broadcasted_iota(jnp.int32, v.shape, 1)
    width = v.shape[1]
    return jnp.where(lane == width - 1, 0.0, pltpu.roll(v, width - 1, 1))


def gelu_parts(v):
    square = v * v
    t = jnp.tanh(v * (ROOT + (ROOT * CUBIC) * square))
    half = 0.5 * v
    return half + half * t, 0.5 + 0.5 * t + half * (1.0 - t * t) * (ROOT + (3.0 * ROOT * CUBIC) * square)


def either(me, own, other):
    return jnp.where(me == 0, own, other), jnp.where(me == 0, other, own)


def put_weights(me, own1, other1, own2, other2, own3, other3, wb1, wb2, wt2, wt1, wt3e, wt3o):
    c = own1.shape[1]
    h = c // 2
    stack = 4 * c
    for out in (wb1, wb2, wt2, wt1, wt3e, wt3o):
        out[...] = jnp.zeros_like(out)
    for a in range(3):
        for b in range(3):
            tap = a * 3 + b
            at = pl.ds(tap * h, h)
            first = jnp.concatenate(either(me, own1[at, :], other1[at, :]), axis=0)
            second = jnp.concatenate(either(me, own2[at, :], other2[at, :]), axis=0)
            for par in range(2):
                at = pl.ds(a * stack + (b + par) * c, c)
                wb1[pl.ds(par * c, c), at] = first
                wb2[pl.ds(par * c, c), at] = second
            turned = second.T
            first_turned = first.T
            half_turned = jnp.where(me == 0, first_turned[:h], first_turned[h:])
            for par in range(2):
                at = pl.ds((2 - a) * stack + (2 - b + par) * c, c)
                wt2[pl.ds(par * c, c), at] = turned
                wt1[pl.ds(par * h, h), at] = half_turned
            at = pl.ds(tap * c, c)
            third = jnp.concatenate([w.T for w in either(me, own3[at, :], other3[at, :])], axis=1)
            par = 0 if b == 1 else 1
            side = 1 if b == 0 else 0
            if a == 1:
                wt3e[pl.ds(par * c, c), pl.ds(side * 2 * c, 2 * c)] = third
            else:
                back = 0 if a == 2 else 1
                wt3o[pl.ds(par * c, c), pl.ds((back * 2 + side) * 2 * c, 2 * c)] = third


def put_stack(ref, base, row):
    c = row.shape[0] // 2
    even, odd = row[:c], row[c:]
    ref[pl.ds(base, c), :] = moved_right(odd).astype(BF)
    ref[pl.ds(base + c, 2 * c), :] = row.astype(BF)
    ref[pl.ds(base + 3 * c, c), :] = moved_left(even).astype(BF)


def run(tasks):
    waiting = None
    for task in tasks:
        value = task[0]()
        if waiting:
            waiting[0](waiting[1])
        waiting = (task[1], value)
    waiting[0](waiting[1])


def deal(pieces, grads, tile):
    for k, piece in enumerate(pieces):
        at = piece_at(tile, k)
        base = 0
        for grad in grads:
            size = grad.shape[0] // 4
            piece[pl.ds(base, size), :] = grad[pl.ds(pl.multiple_of(at * size, 16), size), :]
            base += size


def put_input(ref, base, at, row):
    h, m = row.shape[0], row.shape[1] // 2
    even, odd = row[:, :m], row[:, m:]
    blocks = (moved_right(odd.astype(F32)).astype(BF), even, odd, moved_left(even.astype(F32)).astype(BF))
    for k, block in enumerate(blocks):
        ref[pl.ds(pl.multiple_of(base + k * 2 * h + at * h, h), h), :] = block


def put_cotangent(ref, base, at, row):
    h, m = row.shape[0], row.shape[1] // 2
    for k in range(2):
        block = row[:, k * m : (k + 1) * m]
        to = base + at * 2 * h + k * h
        ref[pl.ds(pl.multiple_of(to, h), h), :] = block
        ref[pl.ds(pl.multiple_of(to + 4 * h, h), h), :] = moved_left(block.astype(F32)).astype(BF)


def put_outer(tx, tu, at, before, after):
    stack = tx.shape[0] // 6
    for k in range(3):
        put_input(tx, k * stack, at, before[k])
        put_input(tx, (k + 3) * stack, at, after[k])
    put_cotangent(tu, 0, at, before[3])
    put_cotangent(tu, stack, at, after[3])


def outer_kernel(core, before, after, tx, tu):
    put_outer(tx, tu, core[0], before, after)


def inner_kernel(
    core, own, other, w1, other1, w2, other2, w3, other3,
    wb1, wb2, wt2, wt1, wt3e, wt3o, tx, tu, th1, dz1, g2,
):
    me = core[0]
    c = wb1.shape[0] // 2
    stack = 4 * c
    rows = own.shape[0] // 3 * 2
    put_weights(me, w1, other1, w2, other2, w3, other3, wb1, wb2, wt2, wt1, wt3e, wt3o)
    for r in range(rows):
        put_input(tx, r * stack, me, own[r])
        put_input(tx, r * stack, 1 - me, other[r])
    for r in range(rows // 2):
        put_cotangent(tu, r * stack, me, own[rows + r])
        put_cotangent(tu, r * stack, 1 - me, other[rows + r])

    def first_dot(r):
        return dot(wb1[...], tx[pl.ds((r - 1) * stack, 3 * stack), :])

    def first_use(r, z):
        act, slope = gelu_parts(z)
        put_stack(th1, (r - 1) * stack, act)
        dz1[pl.ds((r - 1) * 2 * c, 2 * c), :] = slope

    def third_dot(r):
        if r % 2 == 0:
            return dot(wt3e[...], tu[pl.ds(r // 2 * stack, stack), :])
        return dot(wt3o[...], tu[pl.ds(r // 2 * stack, 2 * stack), :])

    def third_use(r, back):
        g2[pl.ds(r * 2 * c, 2 * c), :] = back

    z1 = [(functools.partial(first_dot, r), functools.partial(first_use, r)) for r in range(1, rows - 1)]
    back = [(functools.partial(third_dot, r), functools.partial(third_use, r)) for r in range(rows - 1)]
    run(z1 + back)


def main_kernel(
    core, _txo, _tuo, before, after, wb1, wb2, wt2, wt3e, wt3o, txi, tui, th1i, dz1i, g2i,
    p0, p1, p2, p3, td1, txo, tuo, th1o, dz1o, dz2, th2, td2, s2, s1, dw1, dw2, dw3,
):
    me = core[0]
    c = wb1.shape[0] // 2
    h = c // 2
    m = td1.shape[1]
    stack = 4 * c
    rows = td1.shape[0] // stack - 4

    def input_at(r):
        if 0 <= r < rows:
            return txi, r * stack
        return txo, (r + 3 if r < 0 else r - rows + 3) * stack

    def first_at(r):
        if 1 <= r < rows - 1:
            return th1i, (r - 1) * stack
        return th1o, (r + 2 if r < 1 else r - rows + 4) * stack

    def cotangent_at(r):
        if 0 <= r < rows // 2:
            return tui, r * stack
        return tuo, 0 if r < 0 else stack

    def window(at, first, count):
        places = [at(r) for r in range(first, first + count)]
        return jnp.concatenate([ref[pl.ds(base, stack), :] for ref, base in places], axis=0)

    def own_channels(ref, index, out, r):
        for par in range(2):
            at = pl.multiple_of(index * stack + (1 + par) * c + me * h, h)
            out[par, pl.ds((rows + 1 - r) * h, h), :] = ref[pl.ds(at, h), :]

    def first_dot(r):
        return dot(wb1[...], window(input_at, r - 1, 3))

    def first_use(r, z):
        act, slope = gelu_parts(z)
        ref, base = first_at(r)
        put_stack(ref, base, act)
        if r in (0, rows - 1):
            dz1o[pl.ds((r > 0) * 2 * c, 2 * c), :] = slope

    def second_dot(r):
        return dot(wb2[...], window(first_at, r - 1, 3))

    def second_use(r, z):
        act, slope = gelu_parts(z)
        k = r + 1
        dz2[pl.ds(k * 2 * c, 2 * c), :] = slope
        if r < rows:
            th2[pl.ds(k * 3 * c, c), :] = moved_right(act[c:]).astype(BF)
            th2[pl.ds(k * 3 * c + c, 2 * c), :] = act.astype(BF)

    def third_dot(r):
        if 0 <= r < rows - 1:
            return None
        if r % 2 == 0:
            return dot(wt3e[...], window(cotangent_at, r // 2, 1))
        return dot(wt3o[...], window(cotangent_at, (r - 1) // 2 if r > 0 else -1, 2))

    def third_use(r, back):
        if back is None:
            back = g2i[pl.ds(r * 2 * c, 2 * c), :]
        k = r + 1
        put_stack(td2, k * stack, back * dz2[pl.ds(k * 2 * c, 2 * c), :])
        if 0 <= r < rows:
            own_channels(td2, k, s2, r)

    def back_dot(r):
        return dot(wt2[...], td2[pl.ds(r * stack, 3 * stack), :])

    def back_use(r, back):
        if 0 < r < rows - 1:
            slope = dz1i[pl.ds((r - 1) * 2 * c, 2 * c), :]
        else:
            slope = dz1o[pl.ds((r > 0) * 2 * c, 2 * c), :]
        put_stack(td1, (r + 2) * stack, back * slope)
        own_channels(td1, r + 2, s1, r)

    def third_grad(a):
        total = jnp.zeros((c, 3 * c), F32)
        for r in range(rows // 2):
            mine = tui[pl.ds(pl.multiple_of(r * stack + me * c, c), c), :]
            total = total + dot_t(mine, th2[pl.ds((2 * r + a) * 3 * c, 3 * c), :])
        return total

    def third_grad_use(a, total):
        for b in range(3):
            dw3[pl.ds((a * 3 + b) * c, c), :] = total[:, b * c : (b + 1) * c].astype(BF)

    def kernel_grad(deltas, at):
        total = jnp.zeros((3 * h, 3 * c), F32)
        for q in range(rows + 2):
            ref, base = at(q - 1)
            for par in range(2):
                mine = deltas[par, pl.ds((rows + 1 - q) * h, 3 * h), :]
                total = total + dot_t(mine, ref[pl.ds(base + par * c, 3 * c), :])
        return total

    def kernel_grad_use(out, total):
        for a in range(3):
            for b in range(3):
                out[pl.ds((a * 3 + b) * h, h), :] = total[a * h : (a + 1) * h, b * c : (b + 1) * c].astype(BF)

    def task(does, uses, r):
        return functools.partial(does, r), functools.partial(uses, r)

    z1 = {r: task(first_dot, first_use, r) for r in range(-2, rows + 2)}
    z2 = {r: task(second_dot, second_use, r) for r in range(-1, rows + 1)}
    g2 = {r: task(third_dot, third_use, r) for r in range(-1, rows + 1)}
    g1 = {r: task(back_dot, back_use, r) for r in range(rows)}
    w3 = {a: task(third_grad, third_grad_use, a) for a in range(3)}
    w2 = (lambda: kernel_grad(s2, first_at), functools.partial(kernel_grad_use, dw2))
    w1 = (lambda: kernel_grad(s1, input_at), functools.partial(kernel_grad_use, dw1))
    tasks = [z1[-2], z1[-1], z1[0], z1[rows - 1], z2[-1], z1[rows], z2[0], z1[rows + 1]]
    tasks += [z2[r] for r in range(1, rows)] + [g2[-1], z2[rows]] + [g2[r] for r in range(rows)]
    tasks += [w3[0], g1[0], g2[rows], w3[1]] + [g1[r] for r in range(1, rows - 1)] + [w3[2], g1[rows - 1], w2, w1]

    put_outer(txo, tuo, 1 - me, before, after)
    for out in (s2, s1):
        for par in range(2):
            out[par, pl.ds(0, 2 * h), :] = jnp.zeros((2 * h, m), BF)
            out[par, pl.ds((rows + 2) * h, 2 * h), :] = jnp.zeros((2 * h, m), BF)
    for k in (0, 1, rows + 2, rows + 3):
        td1[pl.ds(k * stack, stack), :] = jnp.zeros((stack, m), BF)
    run(tasks)
    deal((p0, p1, p2, p3), (dw3, dw2, dw1), core[1])


def inputs_kernel(td1, wt1, main, rims):
    h = wt1.shape[0] // 2
    stack = 8 * h
    rows = main.shape[0]
    for k in range(rows + 2):
        back = dot(wt1[...], td1[pl.ds(k * stack, 3 * stack), :])
        flat = jnp.concatenate([back[:h], back[h:]], axis=1)
        if k == 0:
            rims[0] = flat.astype(BF)
        elif k == rows + 1:
            rims[1] = flat.astype(BF)
        else:
            main[k - 1] = flat


def piece_at(tile, k):
    return lax.bitwise_xor(lax.rem(tile, 4), k)


def sum_kernel(*refs):
    total = refs[0][...].astype(F32)
    for piece in refs[1:-1]:
        total = total + piece[...].astype(F32)
    refs[-1][...] = total.astype(BF)


def last_kernel(scales, core, p0, p3, p2, p1, *outs):
    for k, piece in enumerate((p0, p1, p2, p3)):
        at = piece_at(core[1], k)
        base = 0
        for out, scale in zip(outs, scales):
            size = out.shape[0] // 4
            out[pl.ds(pl.multiple_of(at * size, 16), size), :] = piece[pl.ds(base, size), :].astype(F32) * scale
            base += size


def call(body, name, outs, scratch, limit, *args, aliases=None):
    vmem = pl.BlockSpec(memory_space=pltpu.VMEM)
    scalar = pl.BlockSpec(memory_space=pltpu.SMEM)
    return pl.pallas_call(
        body,
        out_shape=tuple(jax.ShapeDtypeStruct(shape, kind) for shape, kind in outs),
        in_specs=[scalar if a.dtype == jnp.int32 else vmem for a in args],
        out_specs=tuple(vmem for _ in outs),
        scratch_shapes=[pltpu.VMEM(shape, kind) for shape, kind in scratch],
        compiler_params=pltpu.CompilerParams(vmem_limit_bytes=limit * 1024 * 1024),
        cost_estimate=pl.CostEstimate(flops=10**6, bytes_accessed=10**5, transcendentals=0),
        input_output_aliases=aliases or {},
        name=name,
    )(*args)


def shards(inputs, w_first, w_second, w_third, cotangent, mirror):
    h, rows, cols = inputs.shape
    m = cols // 2
    c = 2 * h
    stack = 4 * c
    tiles = lax.axis_size("blk")
    up = [(i, (i + 1) % tiles) for i in range(tiles)]
    down = [(j, i) for i, j in up]
    core = jnp.stack([lax.axis_index("chan"), lax.axis_index("blk")]).astype(jnp.int32)

    def across(piece):
        return lax.ppermute(piece, "chan", [(0, 1), (1, 0)])

    def swapped(piece, k):
        return lax.ppermute(piece, "blk", [(i, i ^ k) for i in range(tiles)])

    def total(*parts):
        return call(sum_kernel, "sum", [(parts[0].shape, BF)], [], 8, *parts)[0]

    to = lax.broadcasted_iota(jnp.int32, (cols, cols), 1)
    place = 2 * (to % m) + to // m
    place = jnp.where(mirror[0] == 1, cols - 1 - place, place)
    split = (lax.broadcasted_iota(jnp.int32, (cols, cols), 0) == place).astype(BF)
    to = lax.broadcasted_iota(jnp.int32, (m, m), 1)
    place = jnp.where(mirror[0] == 1, m - 1 - to, to)
    turn = (lax.broadcasted_iota(jnp.int32, (m, m), 0) == place).astype(BF)

    x = jnp.einsum("irc,cn->rin", inputs, split, preferred_element_type=F32).astype(BF)
    u = jnp.einsum("orc,cn->ron", cotangent, turn, preferred_element_type=F32).astype(BF)
    u = jnp.concatenate([u[:, :h], u[:, h:]], axis=2)
    before = lax.ppermute(jnp.concatenate([x[rows - 3 :], u[rows // 2 - 1 :]]), "blk", up)
    after = lax.ppermute(jnp.concatenate([x[:3], u[:1]]), "blk", down)
    own = jnp.concatenate([x, u])
    weights = []
    for w in (w_first, w_second, w_third):
        w = w.reshape(-1, c)
        weights += [w, across(w)]
    wb1, wb2, wt2, wt1, wt3e, wt3o, tx, tu, th1, dz1, g2 = call(
        inner_kernel, "inner",
        [
            ((2 * c, 3 * stack), BF),
            ((2 * c, 3 * stack), BF),
            ((2 * c, 3 * stack), BF),
            ((c, 3 * stack), BF),
            ((2 * c, stack), BF),
            ((2 * c, 2 * stack), BF),
            ((rows * stack, m), BF),
            ((rows // 2 * stack, m), BF),
            (((rows - 2) * stack, m), BF),
            (((rows - 2) * 2 * c, m), F32),
            (((rows - 1) * 2 * c, m), F32),
        ],
        [], 24, core, own, across(own), *weights,
    )
    before, after, _ = lax.optimization_barrier((before, after, g2))
    outer = [((6 * stack, m), BF), ((2 * stack, m), BF)]
    txo, tuo = call(outer_kernel, "outer", outer, [], 8, core, before, after)

    size = 9 * (c + 2 * h) // 4
    *parts, td1, _, _ = call(
        main_kernel, "main",
        [((size, c), BF)] * 4 + [(((rows + 4) * stack, m), BF)] + outer,
        [
            ((6 * stack, m), BF),
            ((2 * 2 * c, m), F32),
            (((rows + 2) * 2 * c, m), F32),
            (((rows + 1) * 3 * c, m), BF),
            (((rows + 2) * stack, m), BF),
            ((2, (rows + 4) * h, m), BF),
            ((2, (rows + 4) * h, m), BF),
            ((9 * h, c), BF),
            ((9 * h, c), BF),
            ((9 * c, c), BF),
        ],
        32, core, txo, tuo, across(before), across(after), wb1, wb2, wt2, wt3e, wt3o, tx, tu, th1, dz1, g2,
        aliases={1: 5, 2: 6},
    )
    mine = total(parts[0], *[swapped(part, k) for k, part in enumerate(parts[1:], 1)])
    bit = 4
    while bit < tiles:
        if bit * 2 >= tiles:
            mine, td1 = lax.optimization_barrier((mine, td1))
        mine = total(mine, swapped(mine, bit))
        bit *= 2
    main, rims = call(
        inputs_kernel, "inputs",
        [((rows, h, cols), F32), ((2, h, cols), BF)], [], 16, td1, wt1,
    )
    from_next = lax.ppermute(rims[0], "blk", down)
    from_prev = lax.ppermute(rims[1], "blk", up)
    from_next, _ = lax.optimization_barrier((from_next, mine))
    from_prev, _ = lax.optimization_barrier((from_prev, from_next))
    from_next, from_prev = from_next.astype(F32), from_prev.astype(F32)
    main = jnp.concatenate([main[:1] + from_prev, main[1:-1], main[-1:] + from_next]).astype(BF)
    grad_inputs = jnp.einsum("rin,cn->irc", main, split, preferred_element_type=F32).astype(BF)

    cells = rows * cols * tiles
    wide, narrow = 1.0 / math.sqrt(cells // 4), 1.0 / math.sqrt(cells)
    third, second, first = call(
        functools.partial(last_kernel, (wide, narrow, narrow)), "last",
        [((9 * c, c), F32), ((9 * h, c), F32), ((9 * h, c), F32)], [], 16,
        core, mine, *[swapped(mine, k) for k in (3, 2, 1)],
    )
    return grad_inputs, first.reshape(3, 3, h, c), second.reshape(3, 3, h, c), third.reshape(3, 3, c, c)


def solution(mesh):
    placed = (
        P("chan", "blk", None),
        P(None, None, "chan", None),
        P(None, None, "chan", None),
        P(None, None, "chan", None),
        P("chan", "blk", None),
        P("blk"),
    )
    return jax.shard_map(
        shards,
        mesh=mesh,
        in_specs=placed,
        out_specs=(
            P("chan", "blk", None),
            P(None, None, "chan", None),
            P(None, None, "chan", None),
            P(None, None, "chan", None),
        ),
        check_vma=False,
    )
```

```python
import functools
import math

import jax
import jax.numpy as jnp
from jax import lax
from jax.experimental import pallas as pl
from jax.experimental.pallas import tpu as pltpu
from jax.sharding import PartitionSpec as P

BF = jnp.bfloat16
F32 = jnp.float32
ROOT = math.sqrt(2.0 / math.pi)
CUBIC = 0.044715


def dot(a, b):
    return jnp.dot(a, b, preferred_element_type=F32)


def dot_t(a, b):
    return lax.dot_general(a, b, (((1,), (1,)), ((), ())), preferred_element_type=F32)


def moved_right(v):
    lane = lax.broadcasted_iota(jnp.int32, v.shape, 1)
    return jnp.where(lane == 0, 0.0, pltpu.roll(v, 1, 1))


def moved_left(v):
    lane = lax.broadcasted_iota(jnp.int32, v.shape, 1)
    width = v.shape[1]
    return jnp.where(lane == width - 1, 0.0, pltpu.roll(v, width - 1, 1))


def gelu_parts(v):
    square = v * v
    t = jnp.tanh(v * (ROOT + (ROOT * CUBIC) * square))
    half = 0.5 * v
    return half + half * t, 0.5 + 0.5 * t + half * (1.0 - t * t) * (ROOT + (3.0 * ROOT * CUBIC) * square)


def either(me, own, other):
    return jnp.where(me == 0, own, other), jnp.where(me == 0, other, own)


def put_weights(me, own1, other1, own2, other2, own3, other3, wb1, wb2, wt2, wt1, wt3e, wt3o):
    c = own1.shape[1]
    h = c // 2
    stack = 4 * c
    for out in (wb1, wb2, wt2, wt1, wt3e, wt3o):
        out[...] = jnp.zeros_like(out)
    for a in range(3):
        for b in range(3):
            tap = a * 3 + b
            at = pl.ds(tap * h, h)
            first = jnp.concatenate(either(me, own1[at, :], other1[at, :]), axis=0)
            second = jnp.concatenate(either(me, own2[at, :], other2[at, :]), axis=0)
            for par in range(2):
                at = pl.ds(a * stack + (b + par) * c, c)
                wb1[pl.ds(par * c, c), at] = first
                wb2[pl.ds(par * c, c), at] = second
            turned = second.T
            first_turned = first.T
            half_turned = jnp.where(me == 0, first_turned[:h], first_turned[h:])
            for par in range(2):
                at = pl.ds((2 - a) * stack + (2 - b + par) * c, c)
                wt2[pl.ds(par * c, c), at] = turned
                wt1[pl.ds(par * h, h), at] = half_turned
            at = pl.ds(tap * c, c)
            third = jnp.concatenate([w.T for w in either(me, own3[at, :], other3[at, :])], axis=1)
            par = 0 if b == 1 else 1
            side = 1 if b == 0 else 0
            if a == 1:
                wt3e[pl.ds(par * c, c), pl.ds(side * 2 * c, 2 * c)] = third
            else:
                back = 0 if a == 2 else 1
                wt3o[pl.ds(par * c, c), pl.ds((back * 2 + side) * 2 * c, 2 * c)] = third


def put_stack(ref, base, row):
    c = row.shape[0] // 2
    even, odd = row[:c], row[c:]
    ref[pl.ds(base, c), :] = moved_right(odd).astype(BF)
    ref[pl.ds(base + c, 2 * c), :] = row.astype(BF)
    ref[pl.ds(base + 3 * c, c), :] = moved_left(even).astype(BF)


def run(tasks):
    waiting = None
    for task in tasks:
        value = task[0]()
        if waiting:
            waiting[0](waiting[1])
        waiting = (task[1], value)
    waiting[0](waiting[1])


def deal(pieces, grads, tile):
    for k, piece in enumerate(pieces):
        at = piece_at(tile, k)
        base = 0
        for grad in grads:
            size = grad.shape[0] // 4
            piece[pl.ds(base, size), :] = grad[pl.ds(pl.multiple_of(at * size, 16), size), :]
            base += size


def put_input(ref, base, at, row):
    h, m = row.shape[0], row.shape[1] // 2
    even, odd = row[:, :m], row[:, m:]
    blocks = (moved_right(odd.astype(F32)).astype(BF), even, odd, moved_left(even.astype(F32)).astype(BF))
    for k, block in enumerate(blocks):
        ref[pl.ds(pl.multiple_of(base + k * 2 * h + at * h, h), h), :] = block


def put_cotangent(ref, base, at, row):
    h, m = row.shape[0], row.shape[1] // 2
    for k in range(2):
        block = row[:, k * m : (k + 1) * m]
        to = base + at * 2 * h + k * h
        ref[pl.ds(pl.multiple_of(to, h), h), :] = block
        ref[pl.ds(pl.multiple_of(to + 4 * h, h), h), :] = moved_left(block.astype(F32)).astype(BF)


def put_outer(tx, tu, at, before, after):
    stack = tx.shape[0] // 6
    for k in range(3):
        put_input(tx, k * stack, at, before[k])
        put_input(tx, (k + 3) * stack, at, after[k])
    put_cotangent(tu, 0, at, before[3])
    put_cotangent(tu, stack, at, after[3])


def outer_kernel(core, before, after, tx, tu):
    put_outer(tx, tu, core[0], before, after)


def inner_kernel(
    core, own, other, w1, other1, w2, other2, w3, other3,
    wb1, wb2, wt2, wt1, wt3e, wt3o, tx, tu, th1, dz1, g2,
):
    me = core[0]
    c = wb1.shape[0] // 2
    stack = 4 * c
    rows = own.shape[0] // 3 * 2
    put_weights(me, w1, other1, w2, other2, w3, other3, wb1, wb2, wt2, wt1, wt3e, wt3o)
    for r in range(rows):
        put_input(tx, r * stack, me, own[r])
        put_input(tx, r * stack, 1 - me, other[r])
    for r in range(rows // 2):
        put_cotangent(tu, r * stack, me, own[rows + r])
        put_cotangent(tu, r * stack, 1 - me, other[rows + r])

    def first_dot(r):
        return dot(wb1[...], tx[pl.ds((r - 1) * stack, 3 * stack), :])

    def first_use(r, z):
        act, slope = gelu_parts(z)
        put_stack(th1, (r - 1) * stack, act)
        dz1[pl.ds((r - 1) * 2 * c, 2 * c), :] = slope

    def third_dot(r):
        if r % 2 == 0:
            return dot(wt3e[...], tu[pl.ds(r // 2 * stack, stack), :])
        return dot(wt3o[...], tu[pl.ds(r // 2 * stack, 2 * stack), :])

    def third_use(r, back):
        g2[pl.ds(r * 2 * c, 2 * c), :] = back

    z1 = [(functools.partial(first_dot, r), functools.partial(first_use, r)) for r in range(1, rows - 1)]
    back = [(functools.partial(third_dot, r), functools.partial(third_use, r)) for r in range(rows - 1)]
    run(z1 + back)


def main_kernel(
    core, _txo, _tuo, before, after, wb1, wb2, wt2, wt3e, wt3o, txi, tui, th1i, dz1i, g2i,
    p0, p1, p2, p3, td1, txo, tuo, th1o, dz1o, dz2, th2, td2, s2, s1, dw1, dw2, dw3,
):
    me = core[0]
    c = wb1.shape[0] // 2
    h = c // 2
    m = td1.shape[1]
    stack = 4 * c
    rows = td1.shape[0] // stack - 4

    def input_at(r):
        if 0 <= r < rows:
            return txi, r * stack
        return txo, (r + 3 if r < 0 else r - rows + 3) * stack

    def first_at(r):
        if 1 <= r < rows - 1:
            return th1i, (r - 1) * stack
        return th1o, (r + 2 if r < 1 else r - rows + 4) * stack

    def cotangent_at(r):
        if 0 <= r < rows // 2:
            return tui, r * stack
        return tuo, 0 if r < 0 else stack

    def window(at, first, count):
        places = [at(r) for r in range(first, first + count)]
        return jnp.concatenate([ref[pl.ds(base, stack), :] for ref, base in places], axis=0)

    def own_channels(ref, index, out, r):
        for par in range(2):
            at = pl.multiple_of(index * stack + (1 + par) * c + me * h, h)
            out[par, pl.ds((rows + 1 - r) * h, h), :] = ref[pl.ds(at, h), :]

    def first_dot(r):
        return dot(wb1[...], window(input_at, r - 1, 3))

    def first_use(r, z):
        act, slope = gelu_parts(z)
        ref, base = first_at(r)
        put_stack(ref, base, act)
        if r in (0, rows - 1):
            dz1o[pl.ds((r > 0) * 2 * c, 2 * c), :] = slope

    def second_dot(r):
        return dot(wb2[...], window(first_at, r - 1, 3))

    def second_use(r, z):
        act, slope = gelu_parts(z)
        k = r + 1
        dz2[pl.ds(k * 2 * c, 2 * c), :] = slope
        if r < rows:
            th2[pl.ds(k * 3 * c, c), :] = moved_right(act[c:]).astype(BF)
            th2[pl.ds(k * 3 * c + c, 2 * c), :] = act.astype(BF)

    def third_dot(r):
        if 0 <= r < rows - 1:
            return None
        if r % 2 == 0:
            return dot(wt3e[...], window(cotangent_at, r // 2, 1))
        return dot(wt3o[...], window(cotangent_at, (r - 1) // 2 if r > 0 else -1, 2))

    def third_use(r, back):
        if back is None:
            back = g2i[pl.ds(r * 2 * c, 2 * c), :]
        k = r + 1
        put_stack(td2, k * stack, back * dz2[pl.ds(k * 2 * c, 2 * c), :])
        if 0 <= r < rows:
            own_channels(td2, k, s2, r)

    def back_dot(r):
        return dot(wt2[...], td2[pl.ds(r * stack, 3 * stack), :])

    def back_use(r, back):
        if 0 < r < rows - 1:
            slope = dz1i[pl.ds((r - 1) * 2 * c, 2 * c), :]
        else:
            slope = dz1o[pl.ds((r > 0) * 2 * c, 2 * c), :]
        put_stack(td1, (r + 2) * stack, back * slope)
        own_channels(td1, r + 2, s1, r)

    def third_grad(a):
        total = jnp.zeros((c, 3 * c), F32)
        for r in range(rows // 2):
            mine = tui[pl.ds(pl.multiple_of(r * stack + me * c, c), c), :]
            total = total + dot_t(mine, th2[pl.ds((2 * r + a) * 3 * c, 3 * c), :])
        return total

    def third_grad_use(a, total):
        for b in range(3):
            dw3[pl.ds((a * 3 + b) * c, c), :] = total[:, b * c : (b + 1) * c].astype(BF)

    def kernel_grad(deltas, at):
        total = jnp.zeros((3 * h, 3 * c), F32)
        for q in range(rows + 2):
            ref, base = at(q - 1)
            for par in range(2):
                mine = deltas[par, pl.ds((rows + 1 - q) * h, 3 * h), :]
                total = total + dot_t(mine, ref[pl.ds(base + par * c, 3 * c), :])
        return total

    def kernel_grad_use(out, total):
        for a in range(3):
            for b in range(3):
                out[pl.ds((a * 3 + b) * h, h), :] = total[a * h : (a + 1) * h, b * c : (b + 1) * c].astype(BF)

    def task(does, uses, r):
        return functools.partial(does, r), functools.partial(uses, r)

    z1 = {r: task(first_dot, first_use, r) for r in range(-2, rows + 2)}
    z2 = {r: task(second_dot, second_use, r) for r in range(-1, rows + 1)}
    g2 = {r: task(third_dot, third_use, r) for r in range(-1, rows + 1)}
    g1 = {r: task(back_dot, back_use, r) for r in range(rows)}
    w3 = {a: task(third_grad, third_grad_use, a) for a in range(3)}
    w2 = (lambda: kernel_grad(s2, first_at), functools.partial(kernel_grad_use, dw2))
    w1 = (lambda: kernel_grad(s1, input_at), functools.partial(kernel_grad_use, dw1))
    tasks = [z1[-2], z1[-1], z1[0], z1[rows - 1], z2[-1], z1[rows], z2[0], z1[rows + 1]]
    tasks += [z2[r] for r in range(1, rows)] + [g2[-1], z2[rows]] + [g2[r] for r in range(rows)]
    tasks += [w3[0], g1[0], g2[rows], w3[1]] + [g1[r] for r in range(1, rows - 1)] + [w3[2], g1[rows - 1], w2, w1]

    put_outer(txo, tuo, 1 - me, before, after)
    for out in (s2, s1):
        for par in range(2):
            out[par, pl.ds(0, 2 * h), :] = jnp.zeros((2 * h, m), BF)
            out[par, pl.ds((rows + 2) * h, 2 * h), :] = jnp.zeros((2 * h, m), BF)
    for k in (0, 1, rows + 2, rows + 3):
        td1[pl.ds(k * stack, stack), :] = jnp.zeros((stack, m), BF)
    run(tasks)
    deal((p0, p1, p2, p3), (dw3, dw2, dw1), core[1])


def inputs_kernel(td1, wt1, main, rims):
    h = wt1.shape[0] // 2
    stack = 8 * h
    rows = main.shape[0]
    for k in range(rows + 2):
        back = dot(wt1[...], td1[pl.ds(k * stack, 3 * stack), :])
        flat = jnp.concatenate([back[:h], back[h:]], axis=1)
        if k == 0:
            rims[0] = flat.astype(BF)
        elif k == rows + 1:
            rims[1] = flat.astype(BF)
        else:
            main[k - 1] = flat


def piece_at(tile, k):
    return lax.bitwise_xor(lax.rem(tile, 4), k)


def sum_kernel(*refs):
    total = refs[0][...].astype(F32)
    for piece in refs[1:-1]:
        total = total + piece[...].astype(F32)
    refs[-1][...] = total.astype(BF)


def write_kernel(which, scales, core, *rest):
    pieces, rest = rest[: len(which)], rest[len(which) :]
    outs, held, sems = rest[-5:-2], rest[-2], rest[-1]
    copies = []
    for n, (k, piece) in enumerate(zip(which, pieces)):
        size = piece.shape[0]
        at = piece_at(core[1], k)
        base = 0
        for j, (out, scale) in enumerate(zip(outs, scales)):
            part = out.shape[0] // 4
            here = held.at[pl.ds(n * size + base, part)]
            here[...] = piece[pl.ds(base, part), :].astype(F32) * scale
            there = out.at[pl.ds(pl.multiple_of(at * part, 16), part)]
            copies.append(pltpu.make_async_copy(here, there, sems.at[n, j]))
            copies[-1].start()
            base += part
    for copy in copies:
        copy.wait()


def call(body, name, outs, scratch, limit, *args, aliases=None, far=False):
    vmem = pl.BlockSpec(memory_space=pltpu.VMEM)
    hbm = pl.BlockSpec(memory_space=pl.ANY)
    scalar = pl.BlockSpec(memory_space=pltpu.SMEM)
    return pl.pallas_call(
        body,
        out_shape=tuple(jax.ShapeDtypeStruct(shape, kind) for shape, kind in outs),
        in_specs=[scalar if a.dtype == jnp.int32 else hbm if a.dtype == F32 and far else vmem for a in args],
        out_specs=tuple(hbm if far else vmem for _ in outs),
        scratch_shapes=[pltpu.VMEM(*some) if isinstance(some, tuple) else some for some in scratch],
        compiler_params=pltpu.CompilerParams(vmem_limit_bytes=limit * 1024 * 1024),
        cost_estimate=pl.CostEstimate(flops=10**6, bytes_accessed=10**5, transcendentals=0),
        input_output_aliases=aliases or {},
        name=name,
    )(*args)


def shards(inputs, w_first, w_second, w_third, cotangent, mirror):
    h, rows, cols = inputs.shape
    m = cols // 2
    c = 2 * h
    stack = 4 * c
    tiles = lax.axis_size("blk")
    up = [(i, (i + 1) % tiles) for i in range(tiles)]
    down = [(j, i) for i, j in up]
    core = jnp.stack([lax.axis_index("chan"), lax.axis_index("blk")]).astype(jnp.int32)

    def across(piece):
        return lax.ppermute(piece, "chan", [(0, 1), (1, 0)])

    def swapped(piece, k):
        return lax.ppermute(piece, "blk", [(i, i ^ k) for i in range(tiles)])

    def total(*parts):
        return call(sum_kernel, "sum", [(parts[0].shape, BF)], [], 8, *parts)[0]

    to = lax.broadcasted_iota(jnp.int32, (cols, cols), 1)
    place = 2 * (to % m) + to // m
    place = jnp.where(mirror[0] == 1, cols - 1 - place, place)
    split = (lax.broadcasted_iota(jnp.int32, (cols, cols), 0) == place).astype(BF)
    to = lax.broadcasted_iota(jnp.int32, (m, m), 1)
    place = jnp.where(mirror[0] == 1, m - 1 - to, to)
    turn = (lax.broadcasted_iota(jnp.int32, (m, m), 0) == place).astype(BF)

    x = jnp.einsum("irc,cn->rin", inputs, split, preferred_element_type=F32).astype(BF)
    u = jnp.einsum("orc,cn->ron", cotangent, turn, preferred_element_type=F32).astype(BF)
    u = jnp.concatenate([u[:, :h], u[:, h:]], axis=2)
    before = lax.ppermute(jnp.concatenate([x[rows - 3 :], u[rows // 2 - 1 :]]), "blk", up)
    after = lax.ppermute(jnp.concatenate([x[:3], u[:1]]), "blk", down)
    own = jnp.concatenate([x, u])
    weights, _ = lax.optimization_barrier(([w.reshape(-1, c) for w in (w_first, w_second, w_third)], x))
    weights = [part for w in weights for part in (w, across(w))]
    wb1, wb2, wt2, wt1, wt3e, wt3o, tx, tu, th1, dz1, g2 = call(
        inner_kernel, "inner",
        [
            ((2 * c, 3 * stack), BF),
            ((2 * c, 3 * stack), BF),
            ((2 * c, 3 * stack), BF),
            ((c, 3 * stack), BF),
            ((2 * c, stack), BF),
            ((2 * c, 2 * stack), BF),
            ((rows * stack, m), BF),
            ((rows // 2 * stack, m), BF),
            (((rows - 2) * stack, m), BF),
            (((rows - 2) * 2 * c, m), F32),
            (((rows - 1) * 2 * c, m), F32),
        ],
        [], 24, core, own, across(own), *weights,
    )
    before, after, _ = lax.optimization_barrier((before, after, g2))
    outer = [((6 * stack, m), BF), ((2 * stack, m), BF)]
    txo, tuo = call(outer_kernel, "outer", outer, [], 8, core, before, after)

    size = 9 * (c + 2 * h) // 4
    *parts, td1, _, _ = call(
        main_kernel, "main",
        [((size, c), BF)] * 4 + [(((rows + 4) * stack, m), BF)] + outer,
        [
            ((6 * stack, m), BF),
            ((2 * 2 * c, m), F32),
            (((rows + 2) * 2 * c, m), F32),
            (((rows + 1) * 3 * c, m), BF),
            (((rows + 2) * stack, m), BF),
            ((2, (rows + 4) * h, m), BF),
            ((2, (rows + 4) * h, m), BF),
            ((9 * h, c), BF),
            ((9 * h, c), BF),
            ((9 * c, c), BF),
        ],
        32, core, txo, tuo, across(before), across(after), wb1, wb2, wt2, wt3e, wt3o, tx, tu, th1, dz1, g2,
        aliases={1: 5, 2: 6},
    )
    mine = total(parts[0], *[swapped(part, k) for k, part in enumerate(parts[1:], 1)])
    bit = 4
    while bit < tiles:
        if bit * 2 >= tiles:
            mine, td1 = lax.optimization_barrier((mine, td1))
        mine = total(mine, swapped(mine, bit))
        bit *= 2
    main, rims = call(
        inputs_kernel, "inputs",
        [((rows, h, cols), F32), ((2, h, cols), BF)], [], 16, td1, wt1,
    )
    from_next = lax.ppermute(rims[0], "blk", down)
    from_prev = lax.ppermute(rims[1], "blk", up)
    from_next, _ = lax.optimization_barrier((from_next, mine))
    from_prev, _ = lax.optimization_barrier((from_prev, from_next))
    from_next, from_prev = from_next.astype(F32), from_prev.astype(F32)
    main = jnp.concatenate([main[:1] + from_prev, main[1:-1], main[-1:] + from_next]).astype(BF)
    grad_inputs = jnp.einsum("rin,cn->irc", main, split, preferred_element_type=F32).astype(BF)

    cells = rows * cols * tiles
    wide, narrow = 1.0 / math.sqrt(cells // 4), 1.0 / math.sqrt(cells)
    scales = (wide, narrow, narrow)
    results = [((9 * c, c), F32), ((9 * h, c), F32), ((9 * h, c), F32)]
    far, near = swapped(mine, 3), [swapped(mine, 1), swapped(mine, 2)]
    most = call(
        functools.partial(write_kernel, (0, 1, 2), scales), "most", results,
        [((3 * size, c), F32), pltpu.SemaphoreType.DMA((3, 3))], 8, core, mine, *near, far=True,
    )
    third, second, first = call(
        functools.partial(write_kernel, (3,), scales), "last", results,
        [((size, c), F32), pltpu.SemaphoreType.DMA((1, 3))], 8, core, far, *most, far=True, aliases={2: 0, 3: 1, 4: 2},
    )
    return grad_inputs, first.reshape(3, 3, h, c), second.reshape(3, 3, h, c), third.reshape(3, 3, c, c)


def solution(mesh):
    placed = (
        P("chan", "blk", None),
        P(None, None, "chan", None),
        P(None, None, "chan", None),
        P(None, None, "chan", None),
        P("chan", "blk", None),
        P("blk"),
    )
    return jax.shard_map(
        shards,
        mesh=mesh,
        in_specs=placed,
        out_specs=(
            P("chan", "blk", None),
            P(None, None, "chan", None),
            P(None, None, "chan", None),
            P(None, None, "chan", None),
        ),
        check_vma=False,
    )
```

```python
import functools
import math

import jax
import jax.numpy as jnp
from jax import lax
from jax.experimental import pallas as pl
from jax.experimental.pallas import tpu as pltpu
from jax.sharding import PartitionSpec as P

BF = jnp.bfloat16
F32 = jnp.float32
ROOT = math.sqrt(2.0 / math.pi)
CUBIC = 0.044715


def dot(a, b):
    return jnp.dot(a, b, preferred_element_type=F32)


def dot_t(a, b):
    return lax.dot_general(a, b, (((1,), (1,)), ((), ())), preferred_element_type=F32)


def moved_right(v):
    lane = lax.broadcasted_iota(jnp.int32, v.shape, 1)
    return jnp.where(lane == 0, 0.0, pltpu.roll(v, 1, 1))


def moved_left(v):
    lane = lax.broadcasted_iota(jnp.int32, v.shape, 1)
    width = v.shape[1]
    return jnp.where(lane == width - 1, 0.0, pltpu.roll(v, width - 1, 1))


def gelu_parts(v):
    square = v * v
    t = jnp.tanh(v * (ROOT + (ROOT * CUBIC) * square))
    half = 0.5 * v
    return half + half * t, 0.5 + 0.5 * t + half * (1.0 - t * t) * (ROOT + (3.0 * ROOT * CUBIC) * square)


def either(me, own, other):
    return jnp.where(me == 0, own, other), jnp.where(me == 0, other, own)


def put_weights(me, own1, other1, own2, other2, own3, other3, wb1, wb2, wt2, wt1, wt3e, wt3o):
    c = own1.shape[1]
    h = c // 2
    stack = 4 * c
    for out in (wb1, wb2, wt2, wt1, wt3e, wt3o):
        out[...] = jnp.zeros_like(out)
    for a in range(3):
        for b in range(3):
            tap = a * 3 + b
            at = pl.ds(tap * h, h)
            first = jnp.concatenate(either(me, own1[at, :], other1[at, :]), axis=0)
            second = jnp.concatenate(either(me, own2[at, :], other2[at, :]), axis=0)
            for par in range(2):
                at = pl.ds(a * stack + (b + par) * c, c)
                wb1[pl.ds(par * c, c), at] = first
                wb2[pl.ds(par * c, c), at] = second
            turned = second.T
            first_turned = first.T
            half_turned = jnp.where(me == 0, first_turned[:h], first_turned[h:])
            for par in range(2):
                at = pl.ds((2 - a) * stack + (2 - b + par) * c, c)
                wt2[pl.ds(par * c, c), at] = turned
                wt1[pl.ds(par * h, h), at] = half_turned
            at = pl.ds(tap * c, c)
            third = jnp.concatenate([w.T for w in either(me, own3[at, :], other3[at, :])], axis=1)
            par = 0 if b == 1 else 1
            side = 1 if b == 0 else 0
            if a == 1:
                wt3e[pl.ds(par * c, c), pl.ds(side * 2 * c, 2 * c)] = third
            else:
                back = 0 if a == 2 else 1
                wt3o[pl.ds(par * c, c), pl.ds((back * 2 + side) * 2 * c, 2 * c)] = third


def put_stack(ref, base, row):
    c = row.shape[0] // 2
    even, odd = row[:c], row[c:]
    ref[pl.ds(base, c), :] = moved_right(odd).astype(BF)
    ref[pl.ds(base + c, 2 * c), :] = row.astype(BF)
    ref[pl.ds(base + 3 * c, c), :] = moved_left(even).astype(BF)


def run(tasks):
    waiting = None
    for task in tasks:
        value = task[0]()
        if waiting:
            waiting[0](waiting[1])
        waiting = (task[1], value)
    waiting[0](waiting[1])


def deal(pieces, grads, tile):
    for k, piece in enumerate(pieces):
        at = piece_at(tile, k)
        base = 0
        for grad in grads:
            size = grad.shape[0] // 4
            piece[pl.ds(base, size), :] = grad[pl.ds(pl.multiple_of(at * size, 16), size), :]
            base += size


def put_input(ref, base, at, row):
    h, m = row.shape[0], row.shape[1] // 2
    even, odd = row[:, :m], row[:, m:]
    blocks = (moved_right(odd.astype(F32)).astype(BF), even, odd, moved_left(even.astype(F32)).astype(BF))
    for k, block in enumerate(blocks):
        ref[pl.ds(pl.multiple_of(base + k * 2 * h + at * h, h), h), :] = block


def put_cotangent(ref, base, at, row):
    h, m = row.shape[0], row.shape[1] // 2
    for k in range(2):
        block = row[:, k * m : (k + 1) * m]
        to = base + at * 2 * h + k * h
        ref[pl.ds(pl.multiple_of(to, h), h), :] = block
        ref[pl.ds(pl.multiple_of(to + 4 * h, h), h), :] = moved_left(block.astype(F32)).astype(BF)


def put_outer(tx, tu, at, around):
    stack = tx.shape[0] // 3
    for k in range(3):
        put_input(tx, k * stack, at, around[k])
    put_cotangent(tu, 0, at, around[3])


def outer_kernel(core, around, tx, tu):
    put_outer(tx, tu, core[0], around)


def taps(r, first, last):
    mine = [a for a in range(3) if first <= r + a - 1 < last]
    return mine, [a for a in range(3) if a not in mine]


def inner_kernel(
    core, own, other, w1, other1, w2, other2, w3, other3,
    wb1, wb2, wt2, wt1, wt3e, wt3o, tx, tu, th1, dz1, g2, part1, part2,
):
    me = core[0]
    c = wb1.shape[0] // 2
    stack = 4 * c
    rows = own.shape[0] // 3 * 2

    def part_dot(weight, ref, first, last, r):
        mine = taps(r, first, last)[0]
        some = ref[pl.ds((r + mine[0] - 1 - first) * stack, len(mine) * stack), :]
        return dot(weight[:, pl.ds(mine[0] * stack, len(mine) * stack)], some)

    def part_use(out, k, value):
        out[pl.ds(k * 2 * c, 2 * c), :] = value

    put_weights(me, w1, other1, w2, other2, w3, other3, wb1, wb2, wt2, wt1, wt3e, wt3o)
    for r in range(rows):
        put_input(tx, r * stack, me, own[r])
        put_input(tx, r * stack, 1 - me, other[r])
    for r in range(rows // 2):
        put_cotangent(tu, r * stack, me, own[rows + r])
        put_cotangent(tu, r * stack, 1 - me, other[rows + r])

    def first_dot(r):
        return dot(wb1[...], tx[pl.ds((r - 1) * stack, 3 * stack), :])

    def first_use(r, z):
        act, slope = gelu_parts(z)
        put_stack(th1, (r - 1) * stack, act)
        dz1[pl.ds((r - 1) * 2 * c, 2 * c), :] = slope

    def third_dot(r):
        if r % 2 == 0:
            return dot(wt3e[...], tu[pl.ds(r // 2 * stack, stack), :])
        return dot(wt3o[...], tu[pl.ds(r // 2 * stack, 2 * stack), :])

    def third_use(r, back):
        g2[pl.ds(r * 2 * c, 2 * c), :] = back

    z1 = [(functools.partial(first_dot, r), functools.partial(first_use, r)) for r in range(1, rows - 1)]
    back = [(functools.partial(third_dot, r), functools.partial(third_use, r)) for r in range(rows - 1)]
    outer = (-1, 0, rows - 1, rows)
    first = [(functools.partial(part_dot, wb1, tx, 0, rows, r), functools.partial(part_use, part1, k)) for k, r in enumerate(outer)]
    second = [(functools.partial(part_dot, wb2, th1, 1, rows - 1, r), functools.partial(part_use, part2, r)) for r in range(rows)]
    run(z1 + back + first + second)


def main_kernel(
    core, _txb, _tub, _txa, _tua, before, after, wb1, wb2, wt2, wt3e, wt3o, txi, tui, th1i, dz1i, g2i, part1, part2,
    p0, p1, p2, p3, td1, txb, tub, txa, tua, th1o, dz1o, dz2, th2, td2, s2, s1, dw1, dw2, dw3,
):
    me = core[0]
    c = wb1.shape[0] // 2
    h = c // 2
    m = td1.shape[1]
    stack = 4 * c
    rows = td1.shape[0] // stack - 4

    def input_at(r):
        if 0 <= r < rows:
            return txi, r * stack
        return (txb, (r + 3) * stack) if r < 0 else (txa, (r - rows) * stack)

    def first_at(r):
        if 1 <= r < rows - 1:
            return th1i, (r - 1) * stack
        return th1o, (r + 2 if r < 1 else r - rows + 4) * stack

    def cotangent_at(r):
        if 0 <= r < rows // 2:
            return tui, r * stack
        return tub if r < 0 else tua, 0

    def window(at, first, count):
        places = [at(r) for r in range(first, first + count)]
        return jnp.concatenate([ref[pl.ds(base, stack), :] for ref, base in places], axis=0)

    def own_channels(ref, index, out, r):
        for par in range(2):
            at = pl.multiple_of(index * stack + (1 + par) * c + me * h, h)
            out[par, pl.ds((rows + 1 - r) * h, h), :] = ref[pl.ds(at, h), :]

    def rest_dot(weight, at, first, last, part, k, r):
        others = taps(r, first, last)[1]
        some = window(at, r + others[0] - 1, len(others))
        value = dot(weight[:, pl.ds(others[0] * stack, len(others) * stack)], some)
        return value if len(others) == 3 else value + part[pl.ds(k * 2 * c, 2 * c), :]

    def first_dot(r):
        return rest_dot(wb1, input_at, 0, rows, part1, r + 1 if r < 1 else r - rows + 3, r)

    def first_use(r, z):
        act, slope = gelu_parts(z)
        ref, base = first_at(r)
        put_stack(ref, base, act)
        if r in (0, rows - 1):
            dz1o[pl.ds((r > 0) * 2 * c, 2 * c), :] = slope

    def second_dot(r):
        return rest_dot(wb2, first_at, 1, rows - 1, part2, r, r)

    def second_use(r, z):
        act, slope = gelu_parts(z)
        k = r + 1
        dz2[pl.ds(k * 2 * c, 2 * c), :] = slope
        if r < rows:
            th2[pl.ds(k * 3 * c, c), :] = moved_right(act[c:]).astype(BF)
            th2[pl.ds(k * 3 * c + c, 2 * c), :] = act.astype(BF)

    def third_dot(r):
        if 0 <= r < rows - 1:
            return None
        if r % 2 == 0:
            return dot(wt3e[...], window(cotangent_at, r // 2, 1))
        return dot(wt3o[...], window(cotangent_at, (r - 1) // 2 if r > 0 else -1, 2))

    def third_use(r, back):
        if back is None:
            back = g2i[pl.ds(r * 2 * c, 2 * c), :]
        k = r + 1
        put_stack(td2, k * stack, back * dz2[pl.ds(k * 2 * c, 2 * c), :])
        if 0 <= r < rows:
            own_channels(td2, k, s2, r)

    def back_dot(r):
        return dot(wt2[...], td2[pl.ds(r * stack, 3 * stack), :])

    def back_use(r, back):
        if 0 < r < rows - 1:
            slope = dz1i[pl.ds((r - 1) * 2 * c, 2 * c), :]
        else:
            slope = dz1o[pl.ds((r > 0) * 2 * c, 2 * c), :]
        put_stack(td1, (r + 2) * stack, back * slope)
        own_channels(td1, r + 2, s1, r)

    def third_grad(a):
        total = jnp.zeros((c, 3 * c), F32)
        for r in range(rows // 2):
            mine = tui[pl.ds(pl.multiple_of(r * stack + me * c, c), c), :]
            total = total + dot_t(mine, th2[pl.ds((2 * r + a) * 3 * c, 3 * c), :])
        return total

    def third_grad_use(a, total):
        for b in range(3):
            dw3[pl.ds((a * 3 + b) * c, c), :] = total[:, b * c : (b + 1) * c].astype(BF)

    def kernel_grad(deltas, at):
        total = jnp.zeros((3 * h, 3 * c), F32)
        for q in range(rows + 2):
            ref, base = at(q - 1)
            for par in range(2):
                mine = deltas[par, pl.ds((rows + 1 - q) * h, 3 * h), :]
                total = total + dot_t(mine, ref[pl.ds(base + par * c, 3 * c), :])
        return total

    def kernel_grad_use(out, total):
        for a in range(3):
            for b in range(3):
                out[pl.ds((a * 3 + b) * h, h), :] = total[a * h : (a + 1) * h, b * c : (b + 1) * c].astype(BF)

    def task(does, uses, r):
        return functools.partial(does, r), functools.partial(uses, r)

    z1 = {r: task(first_dot, first_use, r) for r in range(-2, rows + 2)}
    z2 = {r: task(second_dot, second_use, r) for r in range(-1, rows + 1)}
    g2 = {r: task(third_dot, third_use, r) for r in range(-1, rows + 1)}
    g1 = {r: task(back_dot, back_use, r) for r in range(rows)}
    w3 = {a: task(third_grad, third_grad_use, a) for a in range(3)}
    w2 = (lambda: kernel_grad(s2, first_at), functools.partial(kernel_grad_use, dw2))
    w1 = (lambda: kernel_grad(s1, input_at), functools.partial(kernel_grad_use, dw1))
    tasks = [z1[-2], z1[-1], z1[0], z1[rows - 1], z2[-1], z1[rows], z2[0], z1[rows + 1]]
    tasks += [z2[r] for r in range(1, rows)] + [g2[-1], z2[rows]] + [g2[r] for r in range(rows)]
    tasks += [w3[0], g1[0], g2[rows], w3[1]] + [g1[r] for r in range(1, rows - 1)] + [w3[2], g1[rows - 1], w2, w1]

    put_outer(txb, tub, 1 - me, before)
    put_outer(txa, tua, 1 - me, after)
    for out in (s2, s1):
        for par in range(2):
            out[par, pl.ds(0, 2 * h), :] = jnp.zeros((2 * h, m), BF)
            out[par, pl.ds((rows + 2) * h, 2 * h), :] = jnp.zeros((2 * h, m), BF)
    for k in (0, 1, rows + 2, rows + 3):
        td1[pl.ds(k * stack, stack), :] = jnp.zeros((stack, m), BF)
    run(tasks)
    deal((p0, p1, p2, p3), (dw3, dw2, dw1), core[1])


def inputs_kernel(td1, wt1, main, rims):
    h = wt1.shape[0] // 2
    stack = 8 * h
    rows = main.shape[0]
    for k in range(rows + 2):
        back = dot(wt1[...], td1[pl.ds(k * stack, 3 * stack), :])
        flat = jnp.concatenate([back[:h], back[h:]], axis=1)
        if k == 0:
            rims[0] = flat.astype(BF)
        elif k == rows + 1:
            rims[1] = flat.astype(BF)
        else:
            main[k - 1] = flat


def piece_at(tile, k):
    return lax.bitwise_xor(lax.rem(tile, 4), k)


def sum_kernel(*refs):
    total = refs[0][...].astype(F32)
    for piece in refs[1:-1]:
        total = total + piece[...].astype(F32)
    refs[-1][...] = total.astype(BF)


def write_kernel(which, scales, core, *rest):
    pieces, rest = rest[: len(which)], rest[len(which) :]
    outs, held, sems = rest[-5:-2], rest[-2], rest[-1]
    copies = []
    for n, (k, piece) in enumerate(zip(which, pieces)):
        size = piece.shape[0]
        at = piece_at(core[1], k)
        base = 0
        for j, (out, scale) in enumerate(zip(outs, scales)):
            part = out.shape[0] // 4
            here = held.at[pl.ds(n * size + base, part)]
            here[...] = piece[pl.ds(base, part), :].astype(F32) * scale
            there = out.at[pl.ds(pl.multiple_of(at * part, 16), part)]
            copies.append(pltpu.make_async_copy(here, there, sems.at[n, j]))
            copies[-1].start()
            base += part
    for copy in copies:
        copy.wait()


def call(body, name, outs, scratch, limit, *args, aliases=None, far=False):
    vmem = pl.BlockSpec(memory_space=pltpu.VMEM)
    hbm = pl.BlockSpec(memory_space=pl.ANY)
    scalar = pl.BlockSpec(memory_space=pltpu.SMEM)
    return pl.pallas_call(
        body,
        out_shape=tuple(jax.ShapeDtypeStruct(shape, kind) for shape, kind in outs),
        in_specs=[scalar if a.dtype == jnp.int32 else hbm if a.dtype == F32 and far else vmem for a in args],
        out_specs=tuple(hbm if far else vmem for _ in outs),
        scratch_shapes=[pltpu.VMEM(*some) if isinstance(some, tuple) else some for some in scratch],
        compiler_params=pltpu.CompilerParams(vmem_limit_bytes=limit * 1024 * 1024),
        cost_estimate=pl.CostEstimate(flops=10**6, bytes_accessed=10**5, transcendentals=0),
        input_output_aliases=aliases or {},
        name=name,
    )(*args)


def shards(inputs, w_first, w_second, w_third, cotangent, mirror):
    h, rows, cols = inputs.shape
    m = cols // 2
    c = 2 * h
    stack = 4 * c
    tiles = lax.axis_size("blk")
    up = [(i, (i + 1) % tiles) for i in range(tiles)]
    down = [(j, i) for i, j in up]
    core = jnp.stack([lax.axis_index("chan"), lax.axis_index("blk")]).astype(jnp.int32)

    def across(piece):
        return lax.ppermute(piece, "chan", [(0, 1), (1, 0)])

    def swapped(piece, k):
        return lax.ppermute(piece, "blk", [(i, i ^ k) for i in range(tiles)])

    def total(*parts):
        return call(sum_kernel, "sum", [(parts[0].shape, BF)], [], 8, *parts)[0]

    to = lax.broadcasted_iota(jnp.int32, (cols, cols), 1)
    place = 2 * (to % m) + to // m
    place = jnp.where(mirror[0] == 1, cols - 1 - place, place)
    split = (lax.broadcasted_iota(jnp.int32, (cols, cols), 0) == place).astype(BF)
    to = lax.broadcasted_iota(jnp.int32, (m, m), 1)
    place = jnp.where(mirror[0] == 1, m - 1 - to, to)
    turn = (lax.broadcasted_iota(jnp.int32, (m, m), 0) == place).astype(BF)

    x = jnp.einsum("irc,cn->rin", inputs, split, preferred_element_type=F32).astype(BF)
    u = jnp.einsum("orc,cn->ron", cotangent, turn, preferred_element_type=F32).astype(BF)
    u = jnp.concatenate([u[:, :h], u[:, h:]], axis=2)
    before = lax.ppermute(jnp.concatenate([x[rows - 3 :], u[rows // 2 - 1 :]]), "blk", up)
    after = lax.ppermute(jnp.concatenate([x[:3], u[:1]]), "blk", down)
    own = jnp.concatenate([x, u])
    weights, _ = lax.optimization_barrier(([w.reshape(-1, c) for w in (w_first, w_second, w_third)], x))
    weights = [part for w in weights for part in (w, across(w))]
    wb1, wb2, wt2, wt1, wt3e, wt3o, tx, tu, th1, dz1, g2, part1, part2 = call(
        inner_kernel, "inner",
        [
            ((2 * c, 3 * stack), BF),
            ((2 * c, 3 * stack), BF),
            ((2 * c, 3 * stack), BF),
            ((c, 3 * stack), BF),
            ((2 * c, stack), BF),
            ((2 * c, 2 * stack), BF),
            ((rows * stack, m), BF),
            ((rows // 2 * stack, m), BF),
            (((rows - 2) * stack, m), BF),
            (((rows - 2) * 2 * c, m), F32),
            (((rows - 1) * 2 * c, m), F32),
            ((4 * 2 * c, m), F32),
            ((rows * 2 * c, m), F32),
        ],
        [], 24, core, own, across(own), *weights,
    )
    outer = [((3 * stack, m), BF), ((stack, m), BF)]
    before, _ = lax.optimization_barrier((before, g2))
    other_before = across(before)
    txb, tub = call(outer_kernel, "outer", outer, [], 8, core, before)
    after, _ = lax.optimization_barrier((after, txb))
    txa, tua = call(outer_kernel, "outer", outer, [], 8, core, after)

    size = 9 * (c + 2 * h) // 4
    *parts, td1, _, _, _, _ = call(
        main_kernel, "main",
        [((size, c), BF)] * 4 + [(((rows + 4) * stack, m), BF)] + 2 * outer,
        [
            ((6 * stack, m), BF),
            ((2 * 2 * c, m), F32),
            (((rows + 2) * 2 * c, m), F32),
            (((rows + 1) * 3 * c, m), BF),
            (((rows + 2) * stack, m), BF),
            ((2, (rows + 4) * h, m), BF),
            ((2, (rows + 4) * h, m), BF),
            ((9 * h, c), BF),
            ((9 * h, c), BF),
            ((9 * c, c), BF),
        ],
        32, core, txb, tub, txa, tua, other_before, across(after), wb1, wb2, wt2, wt3e, wt3o, tx, tu, th1, dz1, g2, part1, part2,
        aliases={1: 5, 2: 6, 3: 7, 4: 8},
    )
    mine = total(parts[0], *[swapped(part, k) for k, part in enumerate(parts[1:], 1)])
    bit = 4
    while bit < tiles:
        if bit * 2 >= tiles:
            mine, td1 = lax.optimization_barrier((mine, td1))
        mine = total(mine, swapped(mine, bit))
        bit *= 2
    main, rims = call(
        inputs_kernel, "inputs",
        [((rows, h, cols), F32), ((2, h, cols), BF)], [], 16, td1, wt1,
    )
    from_next = lax.ppermute(rims[0], "blk", down)
    from_prev = lax.ppermute(rims[1], "blk", up)
    from_next, _ = lax.optimization_barrier((from_next, mine))
    from_prev, _ = lax.optimization_barrier((from_prev, from_next))
    from_next, from_prev = from_next.astype(F32), from_prev.astype(F32)
    main = jnp.concatenate([main[:1] + from_prev, main[1:-1], main[-1:] + from_next]).astype(BF)
    grad_inputs = jnp.einsum("rin,cn->irc", main, split, preferred_element_type=F32).astype(BF)

    cells = rows * cols * tiles
    wide, narrow = 1.0 / math.sqrt(cells // 4), 1.0 / math.sqrt(cells)
    scales = (wide, narrow, narrow)
    results = [((9 * c, c), F32), ((9 * h, c), F32), ((9 * h, c), F32)]
    far, near = swapped(mine, 3), [swapped(mine, 1), swapped(mine, 2)]
    most = call(
        functools.partial(write_kernel, (0, 1, 2), scales), "most", results,
        [((3 * size, c), F32), pltpu.SemaphoreType.DMA((3, 3))], 8, core, mine, *near, far=True,
    )
    third, second, first = call(
        functools.partial(write_kernel, (3,), scales), "last", results,
        [((size, c), F32), pltpu.SemaphoreType.DMA((1, 3))], 8, core, far, *most, far=True, aliases={2: 0, 3: 1, 4: 2},
    )
    return grad_inputs, first.reshape(3, 3, h, c), second.reshape(3, 3, h, c), third.reshape(3, 3, c, c)


def solution(mesh):
    placed = (
        P("chan", "blk", None),
        P(None, None, "chan", None),
        P(None, None, "chan", None),
        P(None, None, "chan", None),
        P("chan", "blk", None),
        P("blk"),
    )
    return jax.shard_map(
        shards,
        mesh=mesh,
        in_specs=placed,
        out_specs=(
            P("chan", "blk", None),
            P(None, None, "chan", None),
            P(None, None, "chan", None),
            P(None, None, "chan", None),
        ),
        check_vma=False,
    )
```

```python
import functools
import math

import jax
import jax.numpy as jnp
from jax import lax
from jax.experimental import pallas as pl
from jax.experimental.pallas import tpu as pltpu
from jax.sharding import PartitionSpec as P

BF = jnp.bfloat16
F32 = jnp.float32
ROOT = math.sqrt(2.0 / math.pi)
CUBIC = 0.044715


def dot(a, b):
    return jnp.dot(a, b, preferred_element_type=F32)


def dot_t(a, b):
    return lax.dot_general(a, b, (((1,), (1,)), ((), ())), preferred_element_type=F32)


def moved_right(v):
    lane = lax.broadcasted_iota(jnp.int32, v.shape, 1)
    return jnp.where(lane == 0, 0.0, pltpu.roll(v, 1, 1))


def moved_left(v):
    lane = lax.broadcasted_iota(jnp.int32, v.shape, 1)
    width = v.shape[1]
    return jnp.where(lane == width - 1, 0.0, pltpu.roll(v, width - 1, 1))


def gelu_parts(v):
    square = v * v
    t = jnp.tanh(v * (ROOT + (ROOT * CUBIC) * square))
    half = 0.5 * v
    return half + half * t, 0.5 + 0.5 * t + half * (1.0 - t * t) * (ROOT + (3.0 * ROOT * CUBIC) * square)


def either(me, own, other):
    return jnp.where(me == 0, own, other), jnp.where(me == 0, other, own)


def put_weights(me, own1, other1, own2, other2, own3, other3, wb1, wb2, wt2, wt1, wt3e, wt3o):
    c = own1.shape[1]
    h = c // 2
    stack = 4 * c
    for out in (wb1, wb2, wt2, wt1, wt3e, wt3o):
        out[...] = jnp.zeros_like(out)
    for a in range(3):
        for b in range(3):
            tap = a * 3 + b
            at = pl.ds(tap * h, h)
            first = jnp.concatenate(either(me, own1[at, :], other1[at, :]), axis=0)
            second = jnp.concatenate(either(me, own2[at, :], other2[at, :]), axis=0)
            for par in range(2):
                at = pl.ds(a * stack + (b + par) * c, c)
                wb1[pl.ds(par * c, c), at] = first
                wb2[pl.ds(par * c, c), at] = second
            turned = second.T
            first_turned = first.T
            half_turned = jnp.where(me == 0, first_turned[:h], first_turned[h:])
            for par in range(2):
                at = pl.ds((2 - a) * stack + (2 - b + par) * c, c)
                wt2[pl.ds(par * c, c), at] = turned
                wt1[pl.ds(par * h, h), at] = half_turned
            at = pl.ds(tap * c, c)
            third = jnp.concatenate([w.T for w in either(me, own3[at, :], other3[at, :])], axis=1)
            par = 0 if b == 1 else 1
            side = 1 if b == 0 else 0
            if a == 1:
                wt3e[pl.ds(par * c, c), pl.ds(side * 2 * c, 2 * c)] = third
            else:
                back = 0 if a == 2 else 1
                wt3o[pl.ds(par * c, c), pl.ds((back * 2 + side) * 2 * c, 2 * c)] = third


def put_stack(ref, base, row):
    c = row.shape[0] // 2
    even, odd = row[:c], row[c:]
    ref[pl.ds(base, c), :] = moved_right(odd).astype(BF)
    ref[pl.ds(base + c, 2 * c), :] = row.astype(BF)
    ref[pl.ds(base + 3 * c, c), :] = moved_left(even).astype(BF)


def run(tasks):
    waiting = None
    for task in tasks:
        value = task[0]()
        if waiting:
            waiting[0](waiting[1])
        waiting = (task[1], value)
    waiting[0](waiting[1])


def deal(pieces, grads, tile):
    for k, piece in enumerate(pieces):
        at = piece_at(tile, k)
        base = 0
        for grad in grads:
            size = grad.shape[0] // 4
            piece[pl.ds(base, size), :] = grad[pl.ds(pl.multiple_of(at * size, 16), size), :]
            base += size


def put_input(ref, base, at, row):
    h, m = row.shape[0], row.shape[1] // 2
    even, odd = row[:, :m], row[:, m:]
    blocks = (moved_right(odd.astype(F32)).astype(BF), even, odd, moved_left(even.astype(F32)).astype(BF))
    for k, block in enumerate(blocks):
        ref[pl.ds(pl.multiple_of(base + k * 2 * h + at * h, h), h), :] = block


def put_cotangent(ref, base, at, row):
    h, m = row.shape[0], row.shape[1] // 2
    for k in range(2):
        block = row[:, k * m : (k + 1) * m]
        to = base + at * 2 * h + k * h
        ref[pl.ds(pl.multiple_of(to, h), h), :] = block
        ref[pl.ds(pl.multiple_of(to + 4 * h, h), h), :] = moved_left(block.astype(F32)).astype(BF)


def put_outer(tx, tu, at, around):
    stack = tx.shape[0] // 3
    for k in range(3):
        put_input(tx, k * stack, at, around[k])
    put_cotangent(tu, 0, at, around[3])


def outer_kernel(core, around, tx, tu):
    put_outer(tx, tu, core[0], around)


def taps(r, first, last):
    mine = [a for a in range(3) if first <= r + a - 1 < last]
    return mine, [a for a in range(3) if a not in mine]


def inner_kernel(
    core, own, other, w1, other1, w2, other2, w3, other3,
    wb1, wb2, wt2, wt1, wt3e, wt3o, tx, tu, th1, dz1, g2, part1, part2,
):
    me = core[0]
    c = wb1.shape[0] // 2
    stack = 4 * c
    rows = own.shape[0] // 3 * 2

    def part_dot(weight, ref, first, last, r):
        mine = taps(r, first, last)[0]
        some = ref[pl.ds((r + mine[0] - 1 - first) * stack, len(mine) * stack), :]
        return dot(weight[:, pl.ds(mine[0] * stack, len(mine) * stack)], some)

    def part_use(out, k, value):
        out[pl.ds(k * 2 * c, 2 * c), :] = value

    put_weights(me, w1, other1, w2, other2, w3, other3, wb1, wb2, wt2, wt1, wt3e, wt3o)
    for r in range(rows):
        put_input(tx, r * stack, me, own[r])
        put_input(tx, r * stack, 1 - me, other[r])
    for r in range(rows // 2):
        put_cotangent(tu, r * stack, me, own[rows + r])
        put_cotangent(tu, r * stack, 1 - me, other[rows + r])

    def first_dot(r):
        return dot(wb1[...], tx[pl.ds((r - 1) * stack, 3 * stack), :])

    def first_use(r, z):
        act, slope = gelu_parts(z)
        put_stack(th1, (r - 1) * stack, act)
        dz1[pl.ds((r - 1) * 2 * c, 2 * c), :] = slope

    def third_dot(r):
        if r % 2 == 0:
            return dot(wt3e[...], tu[pl.ds(r // 2 * stack, stack), :])
        return dot(wt3o[...], tu[pl.ds(r // 2 * stack, 2 * stack), :])

    def third_use(r, back):
        g2[pl.ds(r * 2 * c, 2 * c), :] = back

    z1 = [(functools.partial(first_dot, r), functools.partial(first_use, r)) for r in range(1, rows - 1)]
    back = [(functools.partial(third_dot, r), functools.partial(third_use, r)) for r in range(rows - 1)]
    outer = (-1, 0, rows - 1, rows)
    first = [(functools.partial(part_dot, wb1, tx, 0, rows, r), functools.partial(part_use, part1, k)) for k, r in enumerate(outer)]
    second = [(functools.partial(part_dot, wb2, th1, 1, rows - 1, r), functools.partial(part_use, part2, r)) for r in range(rows)]
    run(z1 + back + first + second)


def main_kernel(
    core, _txb, _tub, _txa, _tua, before, after, wb1, wb2, wt2, wt3e, wt3o, txi, tui, th1i, dz1i, g2i, part1, part2,
    p0, p1, p2, p3, td1, txb, tub, txa, tua, th1o, dz1o, dz2, th2, td2, s2, s1, dw1, dw2, dw3,
):
    me = core[0]
    c = wb1.shape[0] // 2
    h = c // 2
    m = td1.shape[1]
    stack = 4 * c
    rows = td1.shape[0] // stack - 4

    def input_at(r):
        if 0 <= r < rows:
            return txi, r * stack
        return (txb, (r + 3) * stack) if r < 0 else (txa, (r - rows) * stack)

    def first_at(r):
        if 1 <= r < rows - 1:
            return th1i, (r - 1) * stack
        return th1o, (r + 2 if r < 1 else r - rows + 4) * stack

    def cotangent_at(r):
        if 0 <= r < rows // 2:
            return tui, r * stack
        return tub if r < 0 else tua, 0

    def window(at, first, count):
        places = [at(r) for r in range(first, first + count)]
        return jnp.concatenate([ref[pl.ds(base, stack), :] for ref, base in places], axis=0)

    def own_channels(ref, index, out, r):
        for par in range(2):
            at = pl.multiple_of(index * stack + (1 + par) * c + me * h, h)
            out[par, pl.ds((rows + 1 - r) * h, h), :] = ref[pl.ds(at, h), :]

    def rest_dot(weight, at, first, last, part, k, r):
        others = taps(r, first, last)[1]
        some = window(at, r + others[0] - 1, len(others))
        value = dot(weight[:, pl.ds(others[0] * stack, len(others) * stack)], some)
        return value if len(others) == 3 else value + part[pl.ds(k * 2 * c, 2 * c), :]

    def first_dot(r):
        return rest_dot(wb1, input_at, 0, rows, part1, r + 1 if r < 1 else r - rows + 3, r)

    def first_use(r, z):
        act, slope = gelu_parts(z)
        ref, base = first_at(r)
        put_stack(ref, base, act)
        if r in (0, rows - 1):
            dz1o[pl.ds((r > 0) * 2 * c, 2 * c), :] = slope

    def second_dot(r):
        return rest_dot(wb2, first_at, 1, rows - 1, part2, r, r)

    def second_use(r, z):
        act, slope = gelu_parts(z)
        k = r + 1
        dz2[pl.ds(k * 2 * c, 2 * c), :] = slope
        if r < rows:
            th2[pl.ds(k * 3 * c, c), :] = moved_right(act[c:]).astype(BF)
            th2[pl.ds(k * 3 * c + c, 2 * c), :] = act.astype(BF)

    def third_dot(r):
        if 0 <= r < rows - 1:
            return None
        if r % 2 == 0:
            return dot(wt3e[...], window(cotangent_at, r // 2, 1))
        return dot(wt3o[...], window(cotangent_at, (r - 1) // 2 if r > 0 else -1, 2))

    def third_use(r, back):
        if back is None:
            back = g2i[pl.ds(r * 2 * c, 2 * c), :]
        k = r + 1
        put_stack(td2, k * stack, back * dz2[pl.ds(k * 2 * c, 2 * c), :])
        if 0 <= r < rows:
            own_channels(td2, k, s2, r)

    def back_dot(r):
        return dot(wt2[...], td2[pl.ds(r * stack, 3 * stack), :])

    def back_use(r, back):
        if 0 < r < rows - 1:
            slope = dz1i[pl.ds((r - 1) * 2 * c, 2 * c), :]
        else:
            slope = dz1o[pl.ds((r > 0) * 2 * c, 2 * c), :]
        put_stack(td1, (r + 2) * stack, back * slope)
        own_channels(td1, r + 2, s1, r)

    def third_grad(a):
        left, right = [], []
        for r in range(rows // 2):
            left.append(tui[pl.ds(pl.multiple_of(r * stack + me * c, c), c), :])
            right.append(th2[pl.ds((2 * r + a) * 3 * c, 3 * c), :])
        return dot_t(jnp.concatenate(left, axis=1), jnp.concatenate(right, axis=1))

    def third_grad_use(a, total):
        for b in range(3):
            dw3[pl.ds((a * 3 + b) * c, c), :] = total[:, b * c : (b + 1) * c].astype(BF)

    def kernel_grad(deltas, at):
        left, right = [], []
        for q in range(rows + 2):
            ref, base = at(q - 1)
            for par in range(2):
                left.append(deltas[par, pl.ds((rows + 1 - q) * h, 3 * h), :])
                right.append(ref[pl.ds(base + par * c, 3 * c), :])
        return dot_t(jnp.concatenate(left, axis=1), jnp.concatenate(right, axis=1))

    def kernel_grad_use(out, total):
        for a in range(3):
            for b in range(3):
                out[pl.ds((a * 3 + b) * h, h), :] = total[a * h : (a + 1) * h, b * c : (b + 1) * c].astype(BF)

    def task(does, uses, r):
        return functools.partial(does, r), functools.partial(uses, r)

    z1 = {r: task(first_dot, first_use, r) for r in range(-2, rows + 2)}
    z2 = {r: task(second_dot, second_use, r) for r in range(-1, rows + 1)}
    g2 = {r: task(third_dot, third_use, r) for r in range(-1, rows + 1)}
    g1 = {r: task(back_dot, back_use, r) for r in range(rows)}
    w3 = {a: task(third_grad, third_grad_use, a) for a in range(3)}
    w2 = (lambda: kernel_grad(s2, first_at), functools.partial(kernel_grad_use, dw2))
    w1 = (lambda: kernel_grad(s1, input_at), functools.partial(kernel_grad_use, dw1))
    tasks = [z1[-2], z1[-1], z1[0], z1[rows - 1], z2[-1], z1[rows], z2[0], z1[rows + 1]]
    tasks += [z2[r] for r in range(1, rows)] + [g2[-1], z2[rows]] + [g2[r] for r in range(rows)]
    tasks += [w3[0], g1[0], g2[rows], w3[1]] + [g1[r] for r in range(1, rows - 1)] + [w3[2], g1[rows - 1], w2, w1]

    put_outer(txb, tub, 1 - me, before)
    put_outer(txa, tua, 1 - me, after)
    for out in (s2, s1):
        for par in range(2):
            out[par, pl.ds(0, 2 * h), :] = jnp.zeros((2 * h, m), BF)
            out[par, pl.ds((rows + 2) * h, 2 * h), :] = jnp.zeros((2 * h, m), BF)
    for k in (0, 1, rows + 2, rows + 3):
        td1[pl.ds(k * stack, stack), :] = jnp.zeros((stack, m), BF)
    run(tasks)
    deal((p0, p1, p2, p3), (dw3, dw2, dw1), core[1])


def inputs_kernel(td1, wt1, main, rims):
    h = wt1.shape[0] // 2
    stack = 8 * h
    rows = main.shape[0]
    for k in range(rows + 2):
        back = dot(wt1[...], td1[pl.ds(k * stack, 3 * stack), :])
        flat = jnp.concatenate([back[:h], back[h:]], axis=1)
        if k == 0:
            rims[0] = flat.astype(BF)
        elif k == rows + 1:
            rims[1] = flat.astype(BF)
        else:
            main[k - 1] = flat


def piece_at(tile, k):
    return lax.bitwise_xor(lax.rem(tile, 4), k)


def sum_kernel(*refs):
    total = refs[0][...].astype(F32)
    for piece in refs[1:-1]:
        total = total + piece[...].astype(F32)
    refs[-1][...] = total.astype(BF)


def write_kernel(which, scales, core, *rest):
    pieces, rest = rest[: len(which)], rest[len(which) :]
    outs, held, sems = rest[-5:-2], rest[-2], rest[-1]
    copies = []
    for n, (k, piece) in enumerate(zip(which, pieces)):
        size = piece.shape[0]
        at = piece_at(core[1], k)
        base = 0
        for j, (out, scale) in enumerate(zip(outs, scales)):
            part = out.shape[0] // 4
            here = held.at[pl.ds(n * size + base, part)]
            here[...] = piece[pl.ds(base, part), :].astype(F32) * scale
            there = out.at[pl.ds(pl.multiple_of(at * part, 16), part)]
            copies.append(pltpu.make_async_copy(here, there, sems.at[n, j]))
            copies[-1].start()
            base += part
    for copy in copies:
        copy.wait()


def call(body, name, outs, scratch, limit, *args, aliases=None, far=False):
    vmem = pl.BlockSpec(memory_space=pltpu.VMEM)
    hbm = pl.BlockSpec(memory_space=pl.ANY)
    scalar = pl.BlockSpec(memory_space=pltpu.SMEM)
    return pl.pallas_call(
        body,
        out_shape=tuple(jax.ShapeDtypeStruct(shape, kind) for shape, kind in outs),
        in_specs=[scalar if a.dtype == jnp.int32 else hbm if a.dtype == F32 and far else vmem for a in args],
        out_specs=tuple(hbm if far else vmem for _ in outs),
        scratch_shapes=[pltpu.VMEM(*some) if isinstance(some, tuple) else some for some in scratch],
        compiler_params=pltpu.CompilerParams(vmem_limit_bytes=limit * 1024 * 1024),
        cost_estimate=pl.CostEstimate(flops=10**6, bytes_accessed=10**5, transcendentals=0),
        input_output_aliases=aliases or {},
        name=name,
    )(*args)


def shards(inputs, w_first, w_second, w_third, cotangent, mirror):
    h, rows, cols = inputs.shape
    m = cols // 2
    c = 2 * h
    stack = 4 * c
    tiles = lax.axis_size("blk")
    up = [(i, (i + 1) % tiles) for i in range(tiles)]
    down = [(j, i) for i, j in up]
    core = jnp.stack([lax.axis_index("chan"), lax.axis_index("blk")]).astype(jnp.int32)

    def across(piece):
        return lax.ppermute(piece, "chan", [(0, 1), (1, 0)])

    def swapped(piece, k):
        return lax.ppermute(piece, "blk", [(i, i ^ k) for i in range(tiles)])

    def total(*parts):
        return call(sum_kernel, "sum", [(parts[0].shape, BF)], [], 8, *parts)[0]

    to = lax.broadcasted_iota(jnp.int32, (cols, cols), 1)
    place = 2 * (to % m) + to // m
    place = jnp.where(mirror[0] == 1, cols - 1 - place, place)
    split = (lax.broadcasted_iota(jnp.int32, (cols, cols), 0) == place).astype(BF)
    to = lax.broadcasted_iota(jnp.int32, (m, m), 1)
    place = jnp.where(mirror[0] == 1, m - 1 - to, to)
    turn = (lax.broadcasted_iota(jnp.int32, (m, m), 0) == place).astype(BF)

    x = jnp.einsum("irc,cn->rin", inputs, split, preferred_element_type=F32).astype(BF)
    u = jnp.einsum("orc,cn->ron", cotangent, turn, preferred_element_type=F32).astype(BF)
    u = jnp.concatenate([u[:, :h], u[:, h:]], axis=2)
    before = lax.ppermute(jnp.concatenate([x[rows - 3 :], u[rows // 2 - 1 :]]), "blk", up)
    after = lax.ppermute(jnp.concatenate([x[:3], u[:1]]), "blk", down)
    own = jnp.concatenate([x, u])
    weights, _ = lax.optimization_barrier(([w.reshape(-1, c) for w in (w_first, w_second, w_third)], x))
    weights = [part for w in weights for part in (w, across(w))]
    wb1, wb2, wt2, wt1, wt3e, wt3o, tx, tu, th1, dz1, g2, part1, part2 = call(
        inner_kernel, "inner",
        [
            ((2 * c, 3 * stack), BF),
            ((2 * c, 3 * stack), BF),
            ((2 * c, 3 * stack), BF),
            ((c, 3 * stack), BF),
            ((2 * c, stack), BF),
            ((2 * c, 2 * stack), BF),
            ((rows * stack, m), BF),
            ((rows // 2 * stack, m), BF),
            (((rows - 2) * stack, m), BF),
            (((rows - 2) * 2 * c, m), F32),
            (((rows - 1) * 2 * c, m), F32),
            ((4 * 2 * c, m), F32),
            ((rows * 2 * c, m), F32),
        ],
        [], 24, core, own, across(own), *weights,
    )
    outer = [((3 * stack, m), BF), ((stack, m), BF)]
    before, _ = lax.optimization_barrier((before, g2))
    other_before = across(before)
    txb, tub = call(outer_kernel, "outer", outer, [], 8, core, before)
    after, _ = lax.optimization_barrier((after, txb))
    txa, tua = call(outer_kernel, "outer", outer, [], 8, core, after)

    size = 9 * (c + 2 * h) // 4
    *parts, td1, _, _, _, _ = call(
        main_kernel, "main",
        [((size, c), BF)] * 4 + [(((rows + 4) * stack, m), BF)] + 2 * outer,
        [
            ((6 * stack, m), BF),
            ((2 * 2 * c, m), F32),
            (((rows + 2) * 2 * c, m), F32),
            (((rows + 1) * 3 * c, m), BF),
            (((rows + 2) * stack, m), BF),
            ((2, (rows + 4) * h, m), BF),
            ((2, (rows + 4) * h, m), BF),
            ((9 * h, c), BF),
            ((9 * h, c), BF),
            ((9 * c, c), BF),
        ],
        32, core, txb, tub, txa, tua, other_before, across(after), wb1, wb2, wt2, wt3e, wt3o, tx, tu, th1, dz1, g2, part1, part2,
        aliases={1: 5, 2: 6, 3: 7, 4: 8},
    )
    mine = total(parts[0], *[swapped(part, k) for k, part in enumerate(parts[1:], 1)])
    bit = 4
    while bit < tiles:
        if bit * 2 >= tiles:
            mine, td1 = lax.optimization_barrier((mine, td1))
        mine = total(mine, swapped(mine, bit))
        bit *= 2
    main, rims = call(
        inputs_kernel, "inputs",
        [((rows, h, cols), F32), ((2, h, cols), BF)], [], 16, td1, wt1,
    )
    from_next = lax.ppermute(rims[0], "blk", down)
    from_prev = lax.ppermute(rims[1], "blk", up)
    from_next, _ = lax.optimization_barrier((from_next, mine))
    from_prev, _ = lax.optimization_barrier((from_prev, from_next))
    from_next, from_prev = from_next.astype(F32), from_prev.astype(F32)
    main = jnp.concatenate([main[:1] + from_prev, main[1:-1], main[-1:] + from_next]).astype(BF)
    grad_inputs = jnp.einsum("rin,cn->irc", main, split, preferred_element_type=F32).astype(BF)

    cells = rows * cols * tiles
    wide, narrow = 1.0 / math.sqrt(cells // 4), 1.0 / math.sqrt(cells)
    scales = (wide, narrow, narrow)
    results = [((9 * c, c), F32), ((9 * h, c), F32), ((9 * h, c), F32)]
    far, near = swapped(mine, 3), [swapped(mine, 1), swapped(mine, 2)]
    most = call(
        functools.partial(write_kernel, (0, 1, 2), scales), "most", results,
        [((3 * size, c), F32), pltpu.SemaphoreType.DMA((3, 3))], 8, core, mine, *near, far=True,
    )
    third, second, first = call(
        functools.partial(write_kernel, (3,), scales), "last", results,
        [((size, c), F32), pltpu.SemaphoreType.DMA((1, 3))], 8, core, far, *most, far=True, aliases={2: 0, 3: 1, 4: 2},
    )
    return grad_inputs, first.reshape(3, 3, h, c), second.reshape(3, 3, h, c), third.reshape(3, 3, c, c)


def solution(mesh):
    placed = (
        P("chan", "blk", None),
        P(None, None, "chan", None),
        P(None, None, "chan", None),
        P(None, None, "chan", None),
        P("chan", "blk", None),
        P("blk"),
    )
    return jax.shard_map(
        shards,
        mesh=mesh,
        in_specs=placed,
        out_specs=(
            P("chan", "blk", None),
            P(None, None, "chan", None),
            P(None, None, "chan", None),
            P(None, None, "chan", None),
        ),
        check_vma=False,
    )
```

```python
import functools
import math

import jax
import jax.numpy as jnp
from jax import lax
from jax.experimental import pallas as pl
from jax.experimental.pallas import tpu as pltpu
from jax.sharding import PartitionSpec as P

BF = jnp.bfloat16
F32 = jnp.float32
ROOT = math.sqrt(2.0 / math.pi)
CUBIC = 0.044715


def dot(a, b):
    return jnp.dot(a, b, preferred_element_type=F32)


def dot_t(a, b):
    return lax.dot_general(a, b, (((1,), (1,)), ((), ())), preferred_element_type=F32)


def moved_right(v):
    lane = lax.broadcasted_iota(jnp.int32, v.shape, 1)
    return jnp.where(lane == 0, 0.0, pltpu.roll(v, 1, 1))


def moved_left(v):
    lane = lax.broadcasted_iota(jnp.int32, v.shape, 1)
    width = v.shape[1]
    return jnp.where(lane == width - 1, 0.0, pltpu.roll(v, width - 1, 1))


def gelu_parts(v):
    square = v * v
    t = jnp.tanh(v * (ROOT + (ROOT * CUBIC) * square))
    half = 0.5 * v
    return half + half * t, 0.5 + 0.5 * t + half * (1.0 - t * t) * (ROOT + (3.0 * ROOT * CUBIC) * square)


def either(me, own, other):
    return jnp.where(me == 0, own, other), jnp.where(me == 0, other, own)


def put_weights(me, own1, other1, own2, other2, own3, other3, wb1, wb2, wt2, wt1, wt3e, wt3o):
    c = own1.shape[1]
    h = c // 2
    stack = 4 * c
    for out in (wb1, wb2, wt2, wt1, wt3e, wt3o):
        out[...] = jnp.zeros_like(out)
    for a in range(3):
        for b in range(3):
            tap = a * 3 + b
            at = pl.ds(tap * h, h)
            first = jnp.concatenate(either(me, own1[at, :], other1[at, :]), axis=0)
            second = jnp.concatenate(either(me, own2[at, :], other2[at, :]), axis=0)
            for par in range(2):
                at = pl.ds(a * stack + (b + par) * c, c)
                wb1[pl.ds(par * c, c), at] = first
                wb2[pl.ds(par * c, c), at] = second
            turned = second.T
            first_turned = first.T
            half_turned = jnp.where(me == 0, first_turned[:h], first_turned[h:])
            for par in range(2):
                at = pl.ds((2 - a) * stack + (2 - b + par) * c, c)
                wt2[pl.ds(par * c, c), at] = turned
                wt1[pl.ds(par * h, h), at] = half_turned
            at = pl.ds(tap * c, c)
            third = jnp.concatenate([w.T for w in either(me, own3[at, :], other3[at, :])], axis=1)
            par = 0 if b == 1 else 1
            side = 1 if b == 0 else 0
            if a == 1:
                wt3e[pl.ds(par * c, c), pl.ds(side * 2 * c, 2 * c)] = third
            else:
                back = 0 if a == 2 else 1
                wt3o[pl.ds(par * c, c), pl.ds((back * 2 + side) * 2 * c, 2 * c)] = third


def put_stack(ref, base, row):
    c = row.shape[0] // 2
    even, odd = row[:c], row[c:]
    ref[pl.ds(base, c), :] = moved_right(odd).astype(BF)
    ref[pl.ds(base + c, 2 * c), :] = row.astype(BF)
    ref[pl.ds(base + 3 * c, c), :] = moved_left(even).astype(BF)


def run(tasks):
    waiting = None
    for task in tasks:
        value = task[0]()
        if waiting:
            waiting[0](waiting[1])
        waiting = (task[1], value)
    waiting[0](waiting[1])


def deal(pieces, grads, tile):
    for k, piece in enumerate(pieces):
        at = piece_at(tile, k)
        base = 0
        for grad in grads:
            size = grad.shape[0] // 4
            piece[pl.ds(base, size), :] = grad[pl.ds(pl.multiple_of(at * size, 16), size), :]
            base += size


def put_input(ref, base, at, row):
    h, m = row.shape[0], row.shape[1] // 2
    even, odd = row[:, :m], row[:, m:]
    blocks = (moved_right(odd.astype(F32)).astype(BF), even, odd, moved_left(even.astype(F32)).astype(BF))
    for k, block in enumerate(blocks):
        ref[pl.ds(pl.multiple_of(base + k * 2 * h + at * h, h), h), :] = block


def put_cotangent(ref, base, at, row):
    h, m = row.shape[0], row.shape[1] // 2
    for k in range(2):
        block = row[:, k * m : (k + 1) * m]
        to = base + at * 2 * h + k * h
        ref[pl.ds(pl.multiple_of(to, h), h), :] = block
        ref[pl.ds(pl.multiple_of(to + 4 * h, h), h), :] = moved_left(block.astype(F32)).astype(BF)


def put_outer(tx, tu, at, around):
    stack = tx.shape[0] // 3
    for k in range(3):
        put_input(tx, k * stack, at, around[k])
    put_cotangent(tu, 0, at, around[3])


def outer_kernel(core, around, tx, tu):
    put_outer(tx, tu, core[0], around)


def taps(r, first, last):
    mine = [a for a in range(3) if first <= r + a - 1 < last]
    return mine, [a for a in range(3) if a not in mine]


def inner_kernel(
    core, own, other, w1, other1, w2, other2, w3, other3,
    wb1, wb2, wt2, wt1, wt3e, wt3o, tx, tu, th1, dz1, g2, part1, part2,
):
    me = core[0]
    c = wb1.shape[0] // 2
    stack = 4 * c
    rows = own.shape[0] // 3 * 2

    def part_dot(weight, ref, first, last, r):
        mine = taps(r, first, last)[0]
        some = ref[pl.ds((r + mine[0] - 1 - first) * stack, len(mine) * stack), :]
        return dot(weight[:, pl.ds(mine[0] * stack, len(mine) * stack)], some)

    def part_use(out, k, value):
        out[pl.ds(k * 2 * c, 2 * c), :] = value

    put_weights(me, w1, other1, w2, other2, w3, other3, wb1, wb2, wt2, wt1, wt3e, wt3o)
    for r in range(rows):
        put_input(tx, r * stack, me, own[r])
        put_input(tx, r * stack, 1 - me, other[r])
    for r in range(rows // 2):
        put_cotangent(tu, r * stack, me, own[rows + r])
        put_cotangent(tu, r * stack, 1 - me, other[rows + r])

    def first_dot(r):
        return dot(wb1[...], tx[pl.ds((r - 1) * stack, 3 * stack), :])

    def first_use(r, z):
        act, slope = gelu_parts(z)
        put_stack(th1, (r - 1) * stack, act)
        dz1[pl.ds((r - 1) * 2 * c, 2 * c), :] = slope

    def third_dot(r):
        if r % 2 == 0:
            return dot(wt3e[...], tu[pl.ds(r // 2 * stack, stack), :])
        return dot(wt3o[...], tu[pl.ds(r // 2 * stack, 2 * stack), :])

    def third_use(r, back):
        g2[pl.ds(r * 2 * c, 2 * c), :] = back

    z1 = [(functools.partial(first_dot, r), functools.partial(first_use, r)) for r in range(1, rows - 1)]
    back = [(functools.partial(third_dot, r), functools.partial(third_use, r)) for r in range(rows - 1)]
    outer = (-1, 0, rows - 1, rows)
    first = [(functools.partial(part_dot, wb1, tx, 0, rows, r), functools.partial(part_use, part1, k)) for k, r in enumerate(outer)]
    second = [(functools.partial(part_dot, wb2, th1, 1, rows - 1, r), functools.partial(part_use, part2, r)) for r in range(rows)]
    run(z1 + back + first + second)


def main_kernel(
    core, _txb, _tub, _txa, _tua, before, after, wb1, wb2, wt2, wt3e, wt3o, txi, tui, th1i, dz1i, g2i, part1, part2,
    p0, p1, p2, p3, td1, txb, tub, txa, tua, th1o, dz1o, dz2, th2, td2, s2, s1, dw1, dw2, dw3,
):
    me = core[0]
    c = wb1.shape[0] // 2
    h = c // 2
    m = td1.shape[1]
    stack = 4 * c
    rows = td1.shape[0] // stack - 4

    def input_at(r):
        if 0 <= r < rows:
            return txi, r * stack
        return (txb, (r + 3) * stack) if r < 0 else (txa, (r - rows) * stack)

    def first_at(r):
        if 1 <= r < rows - 1:
            return th1i, (r - 1) * stack
        return th1o, (r + 2 if r < 1 else r - rows + 4) * stack

    def cotangent_at(r):
        if 0 <= r < rows // 2:
            return tui, r * stack
        return tub if r < 0 else tua, 0

    def window(at, first, count):
        places = [at(r) for r in range(first, first + count)]
        return jnp.concatenate([ref[pl.ds(base, stack), :] for ref, base in places], axis=0)

    def own_channels(ref, index, out, r):
        for par in range(2):
            at = pl.multiple_of(index * stack + (1 + par) * c + me * h, h)
            out[par, pl.ds((rows + 1 - r) * h, h), :] = ref[pl.ds(at, h), :]

    def rest_dot(weight, at, first, last, part, k, r):
        others = taps(r, first, last)[1]
        some = window(at, r + others[0] - 1, len(others))
        value = dot(weight[:, pl.ds(others[0] * stack, len(others) * stack)], some)
        return value if len(others) == 3 else value + part[pl.ds(k * 2 * c, 2 * c), :]

    def first_dot(r):
        return rest_dot(wb1, input_at, 0, rows, part1, r + 1 if r < 1 else r - rows + 3, r)

    def first_use(r, z):
        act, slope = gelu_parts(z)
        ref, base = first_at(r)
        put_stack(ref, base, act)
        if r in (0, rows - 1):
            dz1o[pl.ds((r > 0) * 2 * c, 2 * c), :] = slope

    def second_dot(r):
        return rest_dot(wb2, first_at, 1, rows - 1, part2, r, r)

    def second_use(r, z):
        act, slope = gelu_parts(z)
        k = r + 1
        dz2[pl.ds(k * 2 * c, 2 * c), :] = slope
        if r < rows:
            th2[pl.ds(k * 3 * c, c), :] = moved_right(act[c:]).astype(BF)
            th2[pl.ds(k * 3 * c + c, 2 * c), :] = act.astype(BF)

    def third_dot(r):
        if 0 <= r < rows - 1:
            return None
        if r % 2 == 0:
            return dot(wt3e[...], window(cotangent_at, r // 2, 1))
        return dot(wt3o[...], window(cotangent_at, (r - 1) // 2 if r > 0 else -1, 2))

    def third_use(r, back):
        if back is None:
            back = g2i[pl.ds(r * 2 * c, 2 * c), :]
        k = r + 1
        put_stack(td2, k * stack, back * dz2[pl.ds(k * 2 * c, 2 * c), :])
        if 0 <= r < rows:
            own_channels(td2, k, s2, r)

    def back_dot(r):
        return dot(wt2[...], td2[pl.ds(r * stack, 3 * stack), :])

    def back_use(r, back):
        if 0 < r < rows - 1:
            slope = dz1i[pl.ds((r - 1) * 2 * c, 2 * c), :]
        else:
            slope = dz1o[pl.ds((r > 0) * 2 * c, 2 * c), :]
        put_stack(td1, (r + 2) * stack, back * slope)
        own_channels(td1, r + 2, s1, r)

    def third_grad(a):
        left, right = [], []
        for r in range(rows // 2):
            left.append(tui[pl.ds(pl.multiple_of(r * stack + me * c, c), c), :])
            right.append(th2[pl.ds((2 * r + a) * 3 * c, 3 * c), :])
        return dot_t(jnp.concatenate(left, axis=1), jnp.concatenate(right, axis=1))

    def third_grad_use(a, total):
        for b in range(3):
            dw3[pl.ds((a * 3 + b) * c, c), :] = total[:, b * c : (b + 1) * c].astype(BF)

    def kernel_grad(deltas, at):
        left, right = [], []
        for q in range(rows + 2):
            ref, base = at(q - 1)
            for par in range(2):
                left.append(deltas[par, pl.ds((rows + 1 - q) * h, 3 * h), :])
                right.append(ref[pl.ds(base + par * c, 3 * c), :])
        return dot_t(jnp.concatenate(left, axis=1), jnp.concatenate(right, axis=1))

    def kernel_grad_use(out, total):
        for a in range(3):
            for b in range(3):
                out[pl.ds((a * 3 + b) * h, h), :] = total[a * h : (a + 1) * h, b * c : (b + 1) * c].astype(BF)

    def task(does, uses, r):
        return functools.partial(does, r), functools.partial(uses, r)

    z1 = {r: task(first_dot, first_use, r) for r in range(-2, rows + 2)}
    z2 = {r: task(second_dot, second_use, r) for r in range(-1, rows + 1)}
    g2 = {r: task(third_dot, third_use, r) for r in range(-1, rows + 1)}
    g1 = {r: task(back_dot, back_use, r) for r in range(rows)}
    w3 = {a: task(third_grad, third_grad_use, a) for a in range(3)}
    w2 = (lambda: kernel_grad(s2, first_at), functools.partial(kernel_grad_use, dw2))
    w1 = (lambda: kernel_grad(s1, input_at), functools.partial(kernel_grad_use, dw1))
    tasks = [z1[-2], z1[-1], z1[0], z1[rows - 1], z2[-1], z1[rows], z2[0], z1[rows + 1]]
    tasks += [z2[r] for r in range(1, rows)] + [g2[-1], z2[rows]] + [g2[r] for r in range(rows)]
    tasks += [w3[0], g1[0], g2[rows], w3[1]] + [g1[r] for r in range(1, rows - 1)] + [w3[2], g1[rows - 1], w2, w1]

    put_outer(txb, tub, 1 - me, before)
    put_outer(txa, tua, 1 - me, after)
    for out in (s2, s1):
        for par in range(2):
            out[par, pl.ds(0, 2 * h), :] = jnp.zeros((2 * h, m), BF)
            out[par, pl.ds((rows + 2) * h, 2 * h), :] = jnp.zeros((2 * h, m), BF)
    for k in (0, 1, rows + 2, rows + 3):
        td1[pl.ds(k * stack, stack), :] = jnp.zeros((stack, m), BF)
    run(tasks)
    deal((p0, p1, p2, p3), (dw3, dw2, dw1), core[1])


def inputs_kernel(td1, wt1, main, rims):
    h = wt1.shape[0] // 2
    stack = 8 * h
    rows = main.shape[0]
    for k in range(rows + 2):
        back = dot(wt1[...], td1[pl.ds(k * stack, 3 * stack), :])
        flat = jnp.concatenate([back[:h], back[h:]], axis=1)
        if k == 0:
            rims[0] = flat.astype(BF)
        elif k == rows + 1:
            rims[1] = flat.astype(BF)
        else:
            main[k - 1] = flat


def piece_at(tile, k):
    return lax.bitwise_xor(lax.rem(tile, 4), k)


def sum_kernel(*refs):
    total = refs[0][...].astype(F32)
    for piece in refs[1:-1]:
        total = total + piece[...].astype(F32)
    refs[-1][...] = total.astype(BF)


def write_kernel(which, scales, core, *rest):
    pieces, rest = rest[: len(which)], rest[len(which) :]
    outs, held, sems = rest[-5:-2], rest[-2], rest[-1]
    copies = []
    for n, (k, piece) in enumerate(zip(which, pieces)):
        size = piece.shape[0]
        at = piece_at(core[1], k)
        base = 0
        for j, (out, scale) in enumerate(zip(outs, scales)):
            part = out.shape[0] // 4
            here = held.at[pl.ds(n * size + base, part)]
            here[...] = piece[pl.ds(base, part), :].astype(F32) * scale
            there = out.at[pl.ds(pl.multiple_of(at * part, 16), part)]
            copies.append(pltpu.make_async_copy(here, there, sems.at[n, j]))
            copies[-1].start()
            base += part
    for copy in copies:
        copy.wait()


def call(body, name, outs, scratch, limit, *args, aliases=None, far=False):
    vmem = pl.BlockSpec(memory_space=pltpu.VMEM)
    hbm = pl.BlockSpec(memory_space=pl.ANY)
    scalar = pl.BlockSpec(memory_space=pltpu.SMEM)
    return pl.pallas_call(
        body,
        out_shape=tuple(jax.ShapeDtypeStruct(shape, kind) for shape, kind in outs),
        in_specs=[scalar if a.dtype == jnp.int32 else hbm if a.dtype == F32 and far else vmem for a in args],
        out_specs=tuple(hbm if far else vmem for _ in outs),
        scratch_shapes=[pltpu.VMEM(*some) if isinstance(some, tuple) else some for some in scratch],
        compiler_params=pltpu.CompilerParams(vmem_limit_bytes=limit * 1024 * 1024),
        cost_estimate=pl.CostEstimate(flops=10**6, bytes_accessed=10**5, transcendentals=0),
        input_output_aliases=aliases or {},
        name=name,
    )(*args)


def shards(inputs, w_first, w_second, w_third, cotangent, mirror):
    h, rows, cols = inputs.shape
    m = cols // 2
    c = 2 * h
    stack = 4 * c
    tiles = lax.axis_size("blk")
    up = [(i, (i + 1) % tiles) for i in range(tiles)]
    down = [(j, i) for i, j in up]
    core = jnp.stack([lax.axis_index("chan"), lax.axis_index("blk")]).astype(jnp.int32)

    def across(piece):
        return lax.ppermute(piece, "chan", [(0, 1), (1, 0)])

    def swapped(piece, k):
        return lax.ppermute(piece, "blk", [(i, i ^ k) for i in range(tiles)])

    def total(*parts):
        return call(sum_kernel, "sum", [(parts[0].shape, BF)], [], 8, *parts)[0]

    to = lax.broadcasted_iota(jnp.int32, (cols, cols), 1)
    place = 2 * (to % m) + to // m
    place = jnp.where(mirror[0] == 1, cols - 1 - place, place)
    split = (lax.broadcasted_iota(jnp.int32, (cols, cols), 0) == place).astype(BF)
    to = lax.broadcasted_iota(jnp.int32, (m, m), 1)
    place = jnp.where(mirror[0] == 1, m - 1 - to, to)
    turn = (lax.broadcasted_iota(jnp.int32, (m, m), 0) == place).astype(BF)

    x = jnp.einsum("irc,cn->rin", inputs, split, preferred_element_type=F32).astype(BF)
    u = jnp.einsum("orc,cn->ron", cotangent, turn, preferred_element_type=F32).astype(BF)
    u = jnp.concatenate([u[:, :h], u[:, h:]], axis=2)
    before = lax.ppermute(jnp.concatenate([x[rows - 3 :], u[rows // 2 - 1 :]]), "blk", up)
    after = lax.ppermute(jnp.concatenate([x[:3], u[:1]]), "blk", down)
    own = jnp.concatenate([x, u])
    weights, _ = lax.optimization_barrier(([w.reshape(-1, c) for w in (w_first, w_second, w_third)], x))
    weights = [part for w in weights for part in (w, across(w))]
    wb1, wb2, wt2, wt1, wt3e, wt3o, tx, tu, th1, dz1, g2, part1, part2 = call(
        inner_kernel, "inner",
        [
            ((2 * c, 3 * stack), BF),
            ((2 * c, 3 * stack), BF),
            ((2 * c, 3 * stack), BF),
            ((c, 3 * stack), BF),
            ((2 * c, stack), BF),
            ((2 * c, 2 * stack), BF),
            ((rows * stack, m), BF),
            ((rows // 2 * stack, m), BF),
            (((rows - 2) * stack, m), BF),
            (((rows - 2) * 2 * c, m), F32),
            (((rows - 1) * 2 * c, m), F32),
            ((4 * 2 * c, m), F32),
            ((rows * 2 * c, m), F32),
        ],
        [], 24, core, own, across(own), *weights,
    )
    outer = [((3 * stack, m), BF), ((stack, m), BF)]
    before, _ = lax.optimization_barrier((before, g2))
    other_before = across(before)
    txb, tub = call(outer_kernel, "outer", outer, [], 8, core, before)
    after, _ = lax.optimization_barrier((after, txb))
    txa, tua = call(outer_kernel, "outer", outer, [], 8, core, after)

    size = 9 * (c + 2 * h) // 4
    *parts, td1, _, _, _, _ = call(
        main_kernel, "main",
        [((size, c), BF)] * 4 + [(((rows + 4) * stack, m), BF)] + 2 * outer,
        [
            ((6 * stack, m), BF),
            ((2 * 2 * c, m), F32),
            (((rows + 2) * 2 * c, m), F32),
            (((rows + 1) * 3 * c, m), BF),
            (((rows + 2) * stack, m), BF),
            ((2, (rows + 4) * h, m), BF),
            ((2, (rows + 4) * h, m), BF),
            ((9 * h, c), BF),
            ((9 * h, c), BF),
            ((9 * c, c), BF),
        ],
        32, core, txb, tub, txa, tua, other_before, across(after), wb1, wb2, wt2, wt3e, wt3o, tx, tu, th1, dz1, g2, part1, part2,
        aliases={1: 5, 2: 6, 3: 7, 4: 8},
    )
    mine = total(parts[0], *[swapped(part, k) for k, part in enumerate(parts[1:], 1)])
    mine, td1 = lax.optimization_barrier((mine, td1))
    main, rims = call(
        inputs_kernel, "inputs",
        [((rows, h, cols), F32), ((2, h, cols), BF)], [], 16, td1, wt1,
    )
    bit = 4
    while bit < tiles:
        if bit * 2 >= tiles:
            mine, rims = lax.optimization_barrier((mine, rims))
        mine = total(mine, swapped(mine, bit))
        bit *= 2
    from_next = lax.ppermute(rims[0], "blk", down)
    from_prev = lax.ppermute(rims[1], "blk", up)
    from_next, _ = lax.optimization_barrier((from_next, mine))
    from_prev, _ = lax.optimization_barrier((from_prev, from_next))
    from_next, from_prev = from_next.astype(F32), from_prev.astype(F32)
    main = jnp.concatenate([main[:1] + from_prev, main[1:-1], main[-1:] + from_next]).astype(BF)
    grad_inputs = jnp.einsum("rin,cn->irc", main, split, preferred_element_type=F32).astype(BF)

    cells = rows * cols * tiles
    wide, narrow = 1.0 / math.sqrt(cells // 4), 1.0 / math.sqrt(cells)
    scales = (wide, narrow, narrow)
    results = [((9 * c, c), F32), ((9 * h, c), F32), ((9 * h, c), F32)]
    far, near = swapped(mine, 3), [swapped(mine, 1), swapped(mine, 2)]
    most = call(
        functools.partial(write_kernel, (0, 1, 2), scales), "most", results,
        [((3 * size, c), F32), pltpu.SemaphoreType.DMA((3, 3))], 8, core, mine, *near, far=True,
    )
    third, second, first = call(
        functools.partial(write_kernel, (3,), scales), "last", results,
        [((size, c), F32), pltpu.SemaphoreType.DMA((1, 3))], 8, core, far, *most, far=True, aliases={2: 0, 3: 1, 4: 2},
    )
    return grad_inputs, first.reshape(3, 3, h, c), second.reshape(3, 3, h, c), third.reshape(3, 3, c, c)


def solution(mesh):
    placed = (
        P("chan", "blk", None),
        P(None, None, "chan", None),
        P(None, None, "chan", None),
        P(None, None, "chan", None),
        P("chan", "blk", None),
        P("blk"),
    )
    return jax.shard_map(
        shards,
        mesh=mesh,
        in_specs=placed,
        out_specs=(
            P("chan", "blk", None),
            P(None, None, "chan", None),
            P(None, None, "chan", None),
            P(None, None, "chan", None),
        ),
        check_vma=False,
    )
```

```python
import functools
import math

import jax
import jax.numpy as jnp
from jax import lax
from jax.experimental import pallas as pl
from jax.experimental.pallas import tpu as pltpu
from jax.sharding import PartitionSpec as P

BF = jnp.bfloat16
F32 = jnp.float32
ROOT = math.sqrt(2.0 / math.pi)
CUBIC = 0.044715


def dot(a, b):
    return jnp.dot(a, b, preferred_element_type=F32)


def dot_t(a, b):
    return lax.dot_general(a, b, (((1,), (1,)), ((), ())), preferred_element_type=F32)


def moved_right(v):
    lane = lax.broadcasted_iota(jnp.int32, v.shape, 1)
    return jnp.where(lane == 0, 0.0, pltpu.roll(v, 1, 1))


def moved_left(v):
    lane = lax.broadcasted_iota(jnp.int32, v.shape, 1)
    width = v.shape[1]
    return jnp.where(lane == width - 1, 0.0, pltpu.roll(v, width - 1, 1))


def gelu_parts(v):
    square = v * v
    t = jnp.tanh(v * (ROOT + (ROOT * CUBIC) * square))
    half = 0.5 * v
    return half + half * t, 0.5 + 0.5 * t + half * (1.0 - t * t) * (ROOT + (3.0 * ROOT * CUBIC) * square)


def either(me, own, other):
    return jnp.where(me == 0, own, other), jnp.where(me == 0, other, own)


def put_weights(me, own1, other1, own2, other2, own3, other3, wb1, wb2, wt2, wt1, wt3e, wt3o):
    c = own1.shape[1]
    h = c // 2
    stack = 4 * c
    for out in (wb1, wb2, wt2, wt1, wt3e, wt3o):
        out[...] = jnp.zeros_like(out)
    for a in range(3):
        for b in range(3):
            tap = a * 3 + b
            at = pl.ds(tap * h, h)
            first = jnp.concatenate(either(me, own1[at, :], other1[at, :]), axis=0)
            second = jnp.concatenate(either(me, own2[at, :], other2[at, :]), axis=0)
            for par in range(2):
                at = pl.ds(a * stack + (b + par) * c, c)
                wb1[pl.ds(par * c, c), at] = first
                wb2[pl.ds(par * c, c), at] = second
            turned = second.T
            first_turned = first.T
            half_turned = jnp.where(me == 0, first_turned[:h], first_turned[h:])
            for par in range(2):
                at = pl.ds((2 - a) * stack + (2 - b + par) * c, c)
                wt2[pl.ds(par * c, c), at] = turned
                wt1[pl.ds(par * h, h), at] = half_turned
            at = pl.ds(tap * c, c)
            third = jnp.concatenate([w.T for w in either(me, own3[at, :], other3[at, :])], axis=1)
            par = 0 if b == 1 else 1
            side = 1 if b == 0 else 0
            if a == 1:
                wt3e[pl.ds(par * c, c), pl.ds(side * 2 * c, 2 * c)] = third
            else:
                back = 0 if a == 2 else 1
                wt3o[pl.ds(par * c, c), pl.ds((back * 2 + side) * 2 * c, 2 * c)] = third


def put_stack(ref, base, row):
    c = row.shape[0] // 2
    even, odd = row[:c], row[c:]
    ref[pl.ds(base, c), :] = moved_right(odd).astype(BF)
    ref[pl.ds(base + c, 2 * c), :] = row.astype(BF)
    ref[pl.ds(base + 3 * c, c), :] = moved_left(even).astype(BF)


def run(tasks):
    waiting = None
    for task in tasks:
        value = task[0]()
        if waiting:
            waiting[0](waiting[1])
        waiting = (task[1], value)
    waiting[0](waiting[1])


def deal(pieces, grads, tile):
    for k, piece in enumerate(pieces):
        at = piece_at(tile, k)
        base = 0
        for grad in grads:
            size = grad.shape[0] // 4
            piece[pl.ds(base, size), :] = grad[pl.ds(pl.multiple_of(at * size, 16), size), :]
            base += size


def put_input(ref, base, at, row):
    h, m = row.shape[0], row.shape[1] // 2
    even, odd = row[:, :m], row[:, m:]
    blocks = (moved_right(odd.astype(F32)).astype(BF), even, odd, moved_left(even.astype(F32)).astype(BF))
    for k, block in enumerate(blocks):
        ref[pl.ds(pl.multiple_of(base + k * 2 * h + at * h, h), h), :] = block


def put_cotangent(ref, base, at, row):
    h, m = row.shape[0], row.shape[1] // 2
    for k in range(2):
        block = row[:, k * m : (k + 1) * m]
        to = base + at * 2 * h + k * h
        ref[pl.ds(pl.multiple_of(to, h), h), :] = block
        ref[pl.ds(pl.multiple_of(to + 4 * h, h), h), :] = moved_left(block.astype(F32)).astype(BF)


def put_outer(tx, tu, at, around):
    stack = tx.shape[0] // 3
    for k in range(3):
        put_input(tx, k * stack, at, around[k])
    put_cotangent(tu, 0, at, around[3])


def outer_kernel(core, around, tx, tu):
    put_outer(tx, tu, core[0], around)


def taps(r, first, last):
    mine = [a for a in range(3) if first <= r + a - 1 < last]
    return mine, [a for a in range(3) if a not in mine]


def inner_kernel(
    core, own, other, w1, other1, w2, other2, w3, other3,
    wb1, wb2, wt2, wt1, wt3e, wt3o, tx, tu, th1, dz1, g2, part1, part2,
):
    me = core[0]
    c = wb1.shape[0] // 2
    stack = 4 * c
    rows = own.shape[0] // 3 * 2

    def part_dot(weight, ref, first, last, r):
        mine = taps(r, first, last)[0]
        some = ref[pl.ds((r + mine[0] - 1 - first) * stack, len(mine) * stack), :]
        return dot(weight[:, pl.ds(mine[0] * stack, len(mine) * stack)], some)

    def part_use(out, k, value):
        out[pl.ds(k * 2 * c, 2 * c), :] = value

    put_weights(me, w1, other1, w2, other2, w3, other3, wb1, wb2, wt2, wt1, wt3e, wt3o)
    for r in range(rows):
        put_input(tx, r * stack, me, own[r])
        put_input(tx, r * stack, 1 - me, other[r])
    for r in range(rows // 2):
        put_cotangent(tu, r * stack, me, own[rows + r])
        put_cotangent(tu, r * stack, 1 - me, other[rows + r])

    def first_dot(r):
        return dot(wb1[...], tx[pl.ds((r - 1) * stack, 3 * stack), :])

    def first_use(r, z):
        act, slope = gelu_parts(z)
        put_stack(th1, (r - 1) * stack, act)
        dz1[pl.ds((r - 1) * 2 * c, 2 * c), :] = slope

    def third_dot(r):
        if r % 2 == 0:
            return dot(wt3e[...], tu[pl.ds(r // 2 * stack, stack), :])
        return dot(wt3o[...], tu[pl.ds(r // 2 * stack, 2 * stack), :])

    def third_use(r, back):
        g2[pl.ds(r * 2 * c, 2 * c), :] = back

    z1 = [(functools.partial(first_dot, r), functools.partial(first_use, r)) for r in range(1, rows - 1)]
    back = [(functools.partial(third_dot, r), functools.partial(third_use, r)) for r in range(rows - 1)]
    outer = (-1, 0, rows - 1, rows)
    first = [(functools.partial(part_dot, wb1, tx, 0, rows, r), functools.partial(part_use, part1, k)) for k, r in enumerate(outer)]
    second = [(functools.partial(part_dot, wb2, th1, 1, rows - 1, r), functools.partial(part_use, part2, r)) for r in range(rows)]
    run(z1 + back + first + second)


def main_kernel(
    core, _txb, _tub, _txa, _tua, before, after, wb1, wb2, wt2, wt3e, wt3o, txi, tui, th1i, dz1i, g2i, part1, part2,
    p0, p1, p2, p3, td1, txb, tub, txa, tua, th1o, dz1o, dz2, th2, td2, s2, s1, dw1, dw2, dw3,
):
    me = core[0]
    c = wb1.shape[0] // 2
    h = c // 2
    m = td1.shape[1]
    stack = 4 * c
    rows = td1.shape[0] // stack - 4

    def input_at(r):
        if 0 <= r < rows:
            return txi, r * stack
        return (txb, (r + 3) * stack) if r < 0 else (txa, (r - rows) * stack)

    def first_at(r):
        if 1 <= r < rows - 1:
            return th1i, (r - 1) * stack
        return th1o, (r + 2 if r < 1 else r - rows + 4) * stack

    def cotangent_at(r):
        if 0 <= r < rows // 2:
            return tui, r * stack
        return tub if r < 0 else tua, 0

    def window(at, first, count):
        places = [at(r) for r in range(first, first + count)]
        return jnp.concatenate([ref[pl.ds(base, stack), :] for ref, base in places], axis=0)

    def own_channels(ref, index, out, r):
        for par in range(2):
            at = pl.multiple_of(index * stack + (1 + par) * c + me * h, h)
            out[par, pl.ds((rows + 1 - r) * h, h), :] = ref[pl.ds(at, h), :]

    def rest_dot(weight, at, first, last, part, k, r):
        others = taps(r, first, last)[1]
        some = window(at, r + others[0] - 1, len(others))
        value = dot(weight[:, pl.ds(others[0] * stack, len(others) * stack)], some)
        return value if len(others) == 3 else value + part[pl.ds(k * 2 * c, 2 * c), :]

    def first_dot(r):
        return rest_dot(wb1, input_at, 0, rows, part1, r + 1 if r < 1 else r - rows + 3, r)

    def first_use(r, z):
        act, slope = gelu_parts(z)
        ref, base = first_at(r)
        put_stack(ref, base, act)
        if r in (0, rows - 1):
            dz1o[pl.ds((r > 0) * 2 * c, 2 * c), :] = slope

    def second_dot(r):
        return rest_dot(wb2, first_at, 1, rows - 1, part2, r, r)

    def second_use(r, z):
        act, slope = gelu_parts(z)
        k = r + 1
        dz2[pl.ds(k * 2 * c, 2 * c), :] = slope
        if r < rows:
            th2[pl.ds(k * 3 * c, c), :] = moved_right(act[c:]).astype(BF)
            th2[pl.ds(k * 3 * c + c, 2 * c), :] = act.astype(BF)

    def third_dot(r):
        if 0 <= r < rows - 1:
            return None
        if r % 2 == 0:
            return dot(wt3e[...], window(cotangent_at, r // 2, 1))
        return dot(wt3o[...], window(cotangent_at, (r - 1) // 2 if r > 0 else -1, 2))

    def third_use(r, back):
        if back is None:
            back = g2i[pl.ds(r * 2 * c, 2 * c), :]
        k = r + 1
        put_stack(td2, k * stack, back * dz2[pl.ds(k * 2 * c, 2 * c), :])
        if 0 <= r < rows:
            own_channels(td2, k, s2, r)

    def back_dot(r):
        return dot(wt2[...], td2[pl.ds(r * stack, 3 * stack), :])

    def back_use(r, back):
        if 0 < r < rows - 1:
            slope = dz1i[pl.ds((r - 1) * 2 * c, 2 * c), :]
        else:
            slope = dz1o[pl.ds((r > 0) * 2 * c, 2 * c), :]
        put_stack(td1, (r + 2) * stack, back * slope)
        own_channels(td1, r + 2, s1, r)

    def third_grad(a):
        left, right = [], []
        for r in range(rows // 2):
            left.append(tui[pl.ds(pl.multiple_of(r * stack + me * c, c), c), :])
            right.append(th2[pl.ds((2 * r + a) * 3 * c, 3 * c), :])
        return dot_t(jnp.concatenate(left, axis=1), jnp.concatenate(right, axis=1))

    def third_grad_use(a, total):
        for b in range(3):
            dw3[pl.ds((a * 3 + b) * c, c), :] = total[:, b * c : (b + 1) * c].astype(BF)

    def kernel_grad(deltas, at):
        left, right = [], []
        for q in range(rows + 2):
            ref, base = at(q - 1)
            for par in range(2):
                left.append(deltas[par, pl.ds((rows + 1 - q) * h, 3 * h), :])
                right.append(ref[pl.ds(base + par * c, 3 * c), :])
        return dot_t(jnp.concatenate(left, axis=1), jnp.concatenate(right, axis=1))

    def kernel_grad_use(out, total):
        for a in range(3):
            for b in range(3):
                out[pl.ds((a * 3 + b) * h, h), :] = total[a * h : (a + 1) * h, b * c : (b + 1) * c].astype(BF)

    def task(does, uses, r):
        return functools.partial(does, r), functools.partial(uses, r)

    z1 = {r: task(first_dot, first_use, r) for r in range(-2, rows + 2)}
    z2 = {r: task(second_dot, second_use, r) for r in range(-1, rows + 1)}
    g2 = {r: task(third_dot, third_use, r) for r in range(-1, rows + 1)}
    g1 = {r: task(back_dot, back_use, r) for r in range(rows)}
    w3 = {a: task(third_grad, third_grad_use, a) for a in range(3)}
    w2 = (lambda: kernel_grad(s2, first_at), functools.partial(kernel_grad_use, dw2))
    w1 = (lambda: kernel_grad(s1, input_at), functools.partial(kernel_grad_use, dw1))
    tasks = [z1[-2], z1[-1], z1[0], z1[rows - 1], z2[-1], z1[rows], z2[0], z1[rows + 1]]
    tasks += [z2[r] for r in range(1, rows)] + [g2[-1], z2[rows]] + [g2[r] for r in range(rows)]
    tasks += [w3[0], g1[0], g2[rows], w3[1]] + [g1[r] for r in range(1, rows - 1)] + [w3[2], g1[rows - 1], w2, w1]

    put_outer(txb, tub, 1 - me, before)
    put_outer(txa, tua, 1 - me, after)
    for out in (s2, s1):
        for par in range(2):
            out[par, pl.ds(0, 2 * h), :] = jnp.zeros((2 * h, m), BF)
            out[par, pl.ds((rows + 2) * h, 2 * h), :] = jnp.zeros((2 * h, m), BF)
    for k in (0, 1, rows + 2, rows + 3):
        td1[pl.ds(k * stack, stack), :] = jnp.zeros((stack, m), BF)
    run(tasks)
    deal((p0, p1, p2, p3), (dw3, dw2, dw1), core[1])


def inputs_kernel(td1, wt1, main, rims):
    h = wt1.shape[0] // 2
    stack = 8 * h
    rows = main.shape[0]
    for k in range(rows + 2):
        back = dot(wt1[...], td1[pl.ds(k * stack, 3 * stack), :])
        flat = jnp.concatenate([back[:h], back[h:]], axis=1)
        if k == 0:
            rims[0] = flat.astype(BF)
        elif k == rows + 1:
            rims[1] = flat.astype(BF)
        else:
            main[k - 1] = flat


def piece_at(tile, k):
    return lax.bitwise_xor(lax.rem(tile, 4), k)


def sum_kernel(*refs):
    total = refs[0][...].astype(F32)
    for piece in refs[1:-1]:
        total = total + piece[...].astype(F32)
    refs[-1][...] = total.astype(BF)


def write_kernel(which, scales, core, *rest):
    pieces, rest = rest[: len(which)], rest[len(which) :]
    outs, held, sems = rest[-5:-2], rest[-2], rest[-1]
    copies = []
    for n, (k, piece) in enumerate(zip(which, pieces)):
        size = piece.shape[0]
        at = piece_at(core[1], k)
        base = 0
        for j, (out, scale) in enumerate(zip(outs, scales)):
            part = out.shape[0] // 4
            here = held.at[pl.ds(n * size + base, part)]
            here[...] = piece[pl.ds(base, part), :].astype(F32) * scale
            there = out.at[pl.ds(pl.multiple_of(at * part, 16), part)]
            copies.append(pltpu.make_async_copy(here, there, sems.at[n, j]))
            copies[-1].start()
            base += part
    for copy in copies:
        copy.wait()


def call(body, name, outs, scratch, limit, *args, aliases=None, far=False):
    vmem = pl.BlockSpec(memory_space=pltpu.VMEM)
    hbm = pl.BlockSpec(memory_space=pl.ANY)
    scalar = pl.BlockSpec(memory_space=pltpu.SMEM)
    return pl.pallas_call(
        body,
        out_shape=tuple(jax.ShapeDtypeStruct(shape, kind) for shape, kind in outs),
        in_specs=[scalar if a.dtype == jnp.int32 else hbm if a.dtype == F32 and far else vmem for a in args],
        out_specs=tuple(hbm if far else vmem for _ in outs),
        scratch_shapes=[pltpu.VMEM(*some) if isinstance(some, tuple) else some for some in scratch],
        compiler_params=pltpu.CompilerParams(vmem_limit_bytes=limit * 1024 * 1024),
        cost_estimate=pl.CostEstimate(flops=10**6, bytes_accessed=10**5, transcendentals=0),
        input_output_aliases=aliases or {},
        name=name,
    )(*args)


def shards(inputs, w_first, w_second, w_third, cotangent, mirror):
    h, rows, cols = inputs.shape
    m = cols // 2
    c = 2 * h
    stack = 4 * c
    tiles = lax.axis_size("blk")
    up = [(i, (i + 1) % tiles) for i in range(tiles)]
    down = [(j, i) for i, j in up]
    core = jnp.stack([lax.axis_index("chan"), lax.axis_index("blk")]).astype(jnp.int32)

    def across(piece):
        return lax.ppermute(piece, "chan", [(0, 1), (1, 0)])

    def swapped(piece, k):
        return lax.ppermute(piece, "blk", [(i, i ^ k) for i in range(tiles)])

    def total(*parts):
        return call(sum_kernel, "sum", [(parts[0].shape, BF)], [], 8, *parts)[0]

    to = lax.broadcasted_iota(jnp.int32, (cols, cols), 1)
    place = 2 * (to % m) + to // m
    place = jnp.where(mirror[0] == 1, cols - 1 - place, place)
    split = (lax.broadcasted_iota(jnp.int32, (cols, cols), 0) == place).astype(BF)
    to = lax.broadcasted_iota(jnp.int32, (m, m), 1)
    place = jnp.where(mirror[0] == 1, m - 1 - to, to)
    turn = (lax.broadcasted_iota(jnp.int32, (m, m), 0) == place).astype(BF)

    x = jnp.einsum("irc,cn->rin", inputs, split, preferred_element_type=F32).astype(BF)
    u = jnp.einsum("orc,cn->ron", cotangent, turn, preferred_element_type=F32).astype(BF)
    u = jnp.concatenate([u[:, :h], u[:, h:]], axis=2)
    before = lax.ppermute(jnp.concatenate([x[rows - 3 :], u[rows // 2 - 1 :]]), "blk", up)
    after = lax.ppermute(jnp.concatenate([x[:3], u[:1]]), "blk", down)
    own = jnp.concatenate([x, u])
    weights, _ = lax.optimization_barrier(([w.reshape(-1, c) for w in (w_first, w_second, w_third)], x))
    weights = [part for w in weights for part in (w, across(w))]
    wb1, wb2, wt2, wt1, wt3e, wt3o, tx, tu, th1, dz1, g2, part1, part2 = call(
        inner_kernel, "inner",
        [
            ((2 * c, 3 * stack), BF),
            ((2 * c, 3 * stack), BF),
            ((2 * c, 3 * stack), BF),
            ((c, 3 * stack), BF),
            ((2 * c, stack), BF),
            ((2 * c, 2 * stack), BF),
            ((rows * stack, m), BF),
            ((rows // 2 * stack, m), BF),
            (((rows - 2) * stack, m), BF),
            (((rows - 2) * 2 * c, m), F32),
            (((rows - 1) * 2 * c, m), F32),
            ((4 * 2 * c, m), F32),
            ((rows * 2 * c, m), F32),
        ],
        [], 24, core, own, across(own), *weights,
    )
    outer = [((3 * stack, m), BF), ((stack, m), BF)]
    before, _ = lax.optimization_barrier((before, g2))
    other_before = across(before)
    txb, tub = call(outer_kernel, "outer", outer, [], 8, core, before)
    after, _ = lax.optimization_barrier((after, txb))
    txa, tua = call(outer_kernel, "outer", outer, [], 8, core, after)

    size = 9 * (c + 2 * h) // 4
    *parts, td1, _, _, _, _ = call(
        main_kernel, "main",
        [((size, c), BF)] * 4 + [(((rows + 4) * stack, m), BF)] + 2 * outer,
        [
            ((6 * stack, m), BF),
            ((2 * 2 * c, m), F32),
            (((rows + 2) * 2 * c, m), F32),
            (((rows + 1) * 3 * c, m), BF),
            (((rows + 2) * stack, m), BF),
            ((2, (rows + 4) * h, m), BF),
            ((2, (rows + 4) * h, m), BF),
            ((9 * h, c), BF),
            ((9 * h, c), BF),
            ((9 * c, c), BF),
        ],
        32, core, txb, tub, txa, tua, other_before, across(after), wb1, wb2, wt2, wt3e, wt3o, tx, tu, th1, dz1, g2, part1, part2,
        aliases={1: 5, 2: 6, 3: 7, 4: 8},
    )
    mine = total(parts[0], *[swapped(part, k) for k, part in enumerate(parts[1:], 1)])
    bit = 4
    while bit < tiles:
        if bit * 2 >= tiles:
            mine, td1 = lax.optimization_barrier((mine, td1))
        mine = total(mine, swapped(mine, bit))
        bit *= 2
    main, rims = call(
        inputs_kernel, "inputs",
        [((rows, h, cols), F32), ((2, h, cols), BF)], [], 16, td1, wt1,
    )
    from_next = lax.ppermute(rims[0], "blk", down)
    from_prev = lax.ppermute(rims[1], "blk", up)
    from_next, _ = lax.optimization_barrier((from_next, mine))
    from_prev, _ = lax.optimization_barrier((from_prev, from_next))
    from_next, from_prev = from_next.astype(F32), from_prev.astype(F32)
    main = jnp.concatenate([main[:1] + from_prev, main[1:-1], main[-1:] + from_next]).astype(BF)
    grad_inputs = jnp.einsum("rin,cn->irc", main, split, preferred_element_type=F32).astype(BF)

    cells = rows * cols * tiles
    wide, narrow = 1.0 / math.sqrt(cells // 4), 1.0 / math.sqrt(cells)
    scales = (wide, narrow, narrow)
    results = [((9 * c, c), F32), ((9 * h, c), F32), ((9 * h, c), F32)]
    far, near = swapped(mine, 1), [swapped(mine, 2), swapped(mine, 3)]
    most = call(
        functools.partial(write_kernel, (0, 2, 3), scales), "most", results,
        [((3 * size, c), F32), pltpu.SemaphoreType.DMA((3, 3))], 8, core, mine, *near, far=True,
    )
    third, second, first = call(
        functools.partial(write_kernel, (1,), scales), "last", results,
        [((size, c), F32), pltpu.SemaphoreType.DMA((1, 3))], 8, core, far, *most, far=True, aliases={2: 0, 3: 1, 4: 2},
    )
    return grad_inputs, first.reshape(3, 3, h, c), second.reshape(3, 3, h, c), third.reshape(3, 3, c, c)


def solution(mesh):
    placed = (
        P("chan", "blk", None),
        P(None, None, "chan", None),
        P(None, None, "chan", None),
        P(None, None, "chan", None),
        P("chan", "blk", None),
        P("blk"),
    )
    return jax.shard_map(
        shards,
        mesh=mesh,
        in_specs=placed,
        out_specs=(
            P("chan", "blk", None),
            P(None, None, "chan", None),
            P(None, None, "chan", None),
            P(None, None, "chan", None),
        ),
        check_vma=False,
    )
```
